128 devices in a mesh: seq: 32 (over y, x, core), head: 4 (over z).
Axes of the slice: x: 4, y: 4, z: 4, core: 2. Of those that a mesh axis runs over, the one named last changes fastest.
Arguments:
- queries: bfloat16 [4096, 128, 576], P('seq', 'head'), may hold values from -51 to 51
- cache: bfloat16 [4096, 576], P(('seq', 'head')), may hold values from -6 to 6
- lists: int32 [64, 15], P('seq'), may hold values from -1 to 62, as said below
- w_uv: bfloat16 [128, 512, 128], P('head'), may hold values from -0.25 to 0.25
- grad_out: bfloat16 [4096, 128, 128], P('seq', 'head'), may hold values from -6 to 6
Outputs:
- head_out: bfloat16 [4096, 128, 128], P('seq', 'head')
- grad_queries: bfloat16 [4096, 128, 576], P('seq', 'head')
- grad_cache: float32 [4096, 576], P(('seq', 'head'))
- grad_uv: bfloat16 [128, 512, 128], P('head')
The draws below stay inside these ranges and needn't reach their ends.
Inputs may be any that keep to these rules, and one draw needn't show every extreme that they name: `lists`: -1 marks an empty entry. Any other entry of row g names a block of a lower sequence shard than block g's, or a block of the same shard before g, at most once in the row. The rows of one sequence shard together name at most 1 distinct blocks of any one shard's 128 // 64 blocks, and exactly 1 in some draw pair.
All inputs are finite; a program needn't handle non-finite values.
Results may differ from the reference program's by a relative error of at most 0.015.
Values may be sent and summed in bfloat16 or wider, within the bound.
A program may use at most 192 MiB of HBM per device.

```python
import jax
import jax.numpy as jnp
from jax import lax

H = 128
D_LAT = 512
V_HEAD = 128
BLK = 64
KEEP = 15
TOK_DEV = 128
TOKENS = 4096
KV = 576
NB = 64
CAP = 1


def draw_queries(key, part):
    key = jax.random.fold_in(key, 11)
    first_key = jax.random.fold_in(key, 0)
    values = jnp.clip(jax.random.normal(first_key, (TOKENS, H, KV), jnp.float32), -4.0, 4.0)
    return values.astype(jnp.bfloat16)


def draw_lists(key, part):
    key = jax.random.fold_in(key, 23)
    subset_key, order_key = jax.random.split(key)
    per_dev = TOK_DEV // BLK
    shards = TOKENS // TOK_DEV
    nblocks = TOKENS // BLK
    shard_ids = jnp.arange(shards)
    local_ids = jnp.arange(per_dev)
    forced = (shard_ids[:, None, None] == shards - 1) & (shard_ids[None, :, None] == shards - 1) & (local_ids[None, None, :] == per_dev - 2)
    subset_scores = jax.random.randint(subset_key, (shards, shards, per_dev), 0, 2 ** 20) * per_dev + local_ids + forced.astype(jnp.int32) * 2 ** 24
    ranks = jnp.argsort(jnp.argsort(subset_scores, axis=-1), axis=-1)
    chosen = ranks < CAP
    block_ids = jnp.arange(nblocks)
    shard_of = block_ids // per_dev
    local_of = block_ids % per_dev
    picked = chosen[shard_of[:, None], shard_of[None, :], local_of[None, :]]
    earlier = (shard_of[None, :] < shard_of[:, None]) | (shard_of[None, :] == shard_of[:, None]) & (block_ids[None, :] < block_ids[:, None])
    eligible = picked & earlier
    favoured = (block_ids[:, None] == nblocks - 1) & (block_ids[None, :] == nblocks - 2) & eligible
    scores = jax.random.randint(order_key, (nblocks, nblocks), 0, 2 ** 16) * nblocks + block_ids[None, :] + eligible.astype(jnp.int32) * 2 ** 28 + favoured.astype(jnp.int32) * 2 ** 27
    top_scores, top_index = lax.top_k(scores, KEEP)
    return jnp.where(top_scores >= 2 ** 28, top_index, -1).astype(jnp.int32)


def shard_levels(own_key, shape, pieces, smallest, top_value):
    loudness, own = 1.0, jax.random.fold_in(own_key, 6)
    for dim, parts in pieces:
        steps = jnp.exp(jax.random.uniform(jax.random.fold_in(own, dim), (parts,), jnp.float32, smallest / len(pieces), top_value / len(pieces)))
        loudness = loudness * jnp.repeat(steps, shape[dim] // parts).reshape([-1 if axis == dim else 1 for axis in range(len(shape))])
    return loudness


def scatter_about(stream_key, dims, spread, most, cuts=(), kind=jnp.bfloat16):
    level = shard_levels(stream_key, dims, cuts, -0.22, 0.18) if cuts else 1.0
    values = jax.random.normal(stream_key, dims, jnp.float32) * spread * level
    return jnp.minimum(jnp.maximum(values, -most), most).astype(kind)


def setup_inputs(seed: int = 0) -> dict:
    splits = jax.random.split(jax.random.key(seed), 6)
    queries = draw_queries(jax.random.fold_in(splits[5], 71), 0)
    cache = scatter_about(splits[1], (TOKENS, KV), 1.0, 6.0, ((0, 128),))
    lists = draw_lists(jax.random.fold_in(splits[5], 71), 0)
    w_uv = scatter_about(splits[3], (H, D_LAT, V_HEAD), D_LAT ** -0.5, 0.25, ((0, 4),))
    grad_out = scatter_about(splits[4], (TOKENS, H, V_HEAD), 1.0, 6.0, ((0, 32), (1, 4)))
    return {"queries": queries, "cache": cache, "lists": lists, "w_uv": w_uv, "grad_out": grad_out}


score_scale = 192.0 ** -0.5


def key_mask(entries):
    row_pos = jnp.arange(BLK)[:, None]
    col_pos = jnp.arange((KEEP + 1) * BLK)[None, :]
    slot_pos = col_pos // BLK
    present = jnp.concatenate([jnp.array([True]), entries >= 0])
    return jnp.where(slot_pos == 0, col_pos <= row_pos, present[slot_pos])


def block_pass(query_rows, key_rows, valid, grad_rows, weight):
    query_f = query_rows.astype(jnp.float32)
    key_f = key_rows.astype(jnp.float32)
    value_f = key_f[:, :D_LAT]
    weight_f = weight.astype(jnp.float32)
    scores = jnp.einsum("rhk,ck->hrc", query_f, key_f) * score_scale
    scores = jnp.where(valid[None], scores, -jnp.inf)
    top_score = jnp.max(scores, axis=-1, keepdims=True)
    expo = jnp.exp(scores - top_score)
    probs = (expo / jnp.sum(expo, axis=-1, keepdims=True)).astype(jnp.bfloat16)
    probs_f = probs.astype(jnp.float32)
    latent_out = jnp.einsum("hrc,cd->rhd", probs_f, value_f).astype(jnp.bfloat16)
    latent_f = latent_out.astype(jnp.float32)
    output = jnp.einsum("rhd,hde->rhe", latent_f, weight_f).astype(jnp.bfloat16)
    grad_f = grad_rows.astype(jnp.float32)
    grad_latent = jnp.einsum("rhe,hde->rhd", grad_f, weight_f).astype(jnp.bfloat16)
    grad_latent_f = grad_latent.astype(jnp.float32)
    weight_term = jnp.einsum("rhd,rhe->hde", latent_f, grad_f)
    grad_probs = jnp.einsum("rhd,cd->hrc", grad_latent_f, value_f)
    centre = jnp.sum(probs_f * grad_probs, axis=-1, keepdims=True)
    grad_scores = (score_scale * probs_f * (grad_probs - centre)).astype(jnp.bfloat16)
    grad_scores_f = grad_scores.astype(jnp.float32)
    grad_query = jnp.einsum("hrc,ck->rhk", grad_scores_f, key_f).astype(jnp.bfloat16)
    grad_keys = jnp.einsum("hrc,rhk->ck", grad_scores_f, query_f)
    grad_values = jnp.einsum("hrc,rhd->cd", probs_f, grad_latent_f)
    grad_keys = grad_keys.at[:, :D_LAT].add(grad_values)
    return output, grad_query, grad_keys, weight_term


def reference(queries, cache, lists, w_uv, grad_out):
    blocks = cache.reshape(NB, BLK, KV)

    def step(carry, block_index):
        grad_blocks, grad_weight = carry
        entries = lists[block_index]
        safe_entries = jnp.maximum(entries, 0).astype(jnp.int32)
        key_rows = jnp.concatenate([blocks[block_index][None], blocks[safe_entries]], 0).reshape(-1, KV)
        query_rows = lax.dynamic_slice_in_dim(queries, block_index * BLK, BLK, 0)
        grad_rows = lax.dynamic_slice_in_dim(grad_out, block_index * BLK, BLK, 0)
        output, grad_query, grad_keys, weight_term = block_pass(query_rows, key_rows, key_mask(entries), grad_rows, w_uv)
        grad_keys = grad_keys.reshape(KEEP + 1, BLK, KV)
        grad_blocks = grad_blocks.at[block_index].add(grad_keys[0]).at[safe_entries].add(grad_keys[1:])
        return (grad_blocks, grad_weight + weight_term), (output, grad_query)

    init = (jnp.zeros((NB, BLK, KV), jnp.float32), jnp.zeros((H, D_LAT, V_HEAD), jnp.float32))
    (grad_blocks, grad_weight), (outputs, grad_queries) = lax.scan(step, init, jnp.arange(NB, dtype=jnp.int32))
    return (outputs.reshape(TOKENS, H, V_HEAD), grad_queries.reshape(TOKENS, H, KV), grad_blocks.reshape(TOKENS, KV), grad_weight.astype(jnp.bfloat16))
```

```python
import functools, jax, jax.numpy as jnp, numpy as np
from jax import lax
from jax.experimental import pallas as pl
from jax.experimental.pallas import tpu as pltpu
from jax.sharding import PartitionSpec as P

BLK=64; KEEP=15; SLOTS=16; KEYS=1024; DL=512; KV=576; KP=640; NH=32; VH=128; TD=128
ROWS=2048; TILE=256; NT=8
SC=192.0**-0.5
L2E=1.4426950408889634
NEG=-1e30
F32=jnp.float32; BF=jnp.bfloat16
NTD=(((1,),(1,)),((),()))
TND=(((0,),(0,)),((),()))

def halves(a,b):
    return (jnp.concatenate([a[:, :64], b[:, :64]],1), jnp.concatenate([a[:, 64:], b[:, 64:]],1))

def build_keys(g, lists_ref, full_ref, k_ref, kt_ref, own):
    colid = lax.broadcasted_iota(jnp.int32,(BLK,KP-DL),1)
    for j in range(SLOTS):
        if j==0:
            row = own+g; bias=jnp.float32(0.0)
        else:
            e = lists_ref[g, j-1]
            row = jnp.maximum(e,0)
            bias = jnp.where(e>=0, 0.0, NEG).astype(F32)
        blk = full_ref[row]
        k_ref[g, j*BLK:(j+1)*BLK, :DL] = blk[:, :DL]
        rot = jnp.concatenate([blk[:, DL:].astype(F32), jnp.zeros((BLK,64),F32)],1)
        rot = jnp.where(colid==64, bias, rot).astype(BF)
        k_ref[g, j*BLK:(j+1)*BLK, DL:] = rot
    for c in range(8):
        kt_ref[g, :, c*128:(c+1)*128] = jnp.swapaxes(k_ref[g, c*128:(c+1)*128, :], 0, 1)

def prep_q(qt_ref, qg_ref):
    def body(hp, _):
        a=qt_ref[2*hp]; b=qt_ref[2*hp+1]
        x,y=halves(a,b)
        col=pl.ds(pl.multiple_of(hp*128,128),128)
        qg_ref[0,:KV,col]=x
        qg_ref[1,:KV,col]=y
        return 0
    lax.fori_loop(0,16,body,0)
    r=lax.broadcasted_iota(jnp.int32,(64,ROWS),0)
    one=jnp.where(r==0,1.0,0.0).astype(BF)
    qg_ref[0,KV:,:]=one
    qg_ref[1,KV:,:]=one

def make_mask(mask_ref):
    r=lax.broadcasted_iota(jnp.int32,(BLK,TILE),0)
    c=lax.broadcasted_iota(jnp.int32,(BLK,TILE),1)
    mask_ref[...]=jnp.where(r<=(c%BLK),0.0,NEG).astype(F32)

def forward(qg,k,kt,w,gout,mask,pt,do,cen,ot,uv,ho):
    def tile(i,_):
        col=pl.ds(pl.multiple_of(i*TILE,TILE),TILE)
        for p in range(2):
            h=i*4+2*p
            d0=lax.dot_general(w[h],gout[h],NTD,preferred_element_type=F32).astype(BF)
            d1=lax.dot_general(w[h+1],gout[h+1],NTD,preferred_element_type=F32).astype(BF)
            x,y=halves(d0,d1)
            c2=pl.ds(pl.multiple_of(i*TILE+p*128,128),128)
            do[0,:,c2]=x
            do[1,:,c2]=y
        for g in range(2):
            s=jnp.dot(k[g],qg[g,:,col],preferred_element_type=F32)
            s=jnp.concatenate([s[:BLK]+mask[...],s[BLK:]],0)
            m=jnp.max(s,axis=0,keepdims=True)
            e=jnp.exp2((s-m)*(SC*L2E))
            l=jnp.sum(e,axis=0,keepdims=True)
            pb=e.astype(BF)
            pt[g,:,col]=pb
            inv=1.0/l
            o=jnp.dot(kt[g,:DL,:],pb,preferred_element_type=F32)*inv
            ot[g]=o.astype(BF)
            dn=(do[g,:,col].astype(F32)*inv).astype(BF)
            do[g,:,col]=dn
            cen[g,:,col]=jnp.broadcast_to(jnp.sum(o*dn.astype(F32),axis=0,keepdims=True),(8,TILE))
        for p in range(2):
            hh=halves(ot[0,:,p*128:(p+1)*128],ot[1,:,p*128:(p+1)*128])
            for q in range(2):
                h=i*4+2*p+q
                uv[h]=jnp.dot(hh[q],gout[h],preferred_element_type=F32).astype(BF)
                ho[h]=lax.dot_general(hh[q],w[h],TND,preferred_element_type=F32).astype(BF)
        return 0
    lax.fori_loop(0,NT,tile,0)

def back_ds(g,k,pt,do,cen,ds):
    def tile(i,_):
        col=pl.ds(pl.multiple_of(i*TILE,TILE),TILE)
        dp=jnp.dot(k[g,:,:DL],do[g,:,col],preferred_element_type=F32)
        x=pt[g,:,col].astype(F32)*(dp-cen[g,0:1,col])
        ds[g,:,col]=x.astype(BF)
        return 0
    lax.fori_loop(0,NT,tile,0)

def back_kv(g,qg,do,pt,ds,gk):
    def chunk(c,_):
        rows=pl.ds(pl.multiple_of(c*TILE,TILE),TILE)
        a=lax.dot_general(qg[g,:KV,:],ds[g,rows,:],NTD,preferred_element_type=F32)*SC
        b=lax.dot_general(do[g],pt[g,rows,:],NTD,preferred_element_type=F32)
        t=jnp.concatenate([a[:DL]+b,a[DL:],jnp.zeros((KP-KV,TILE),F32)],0)
        gk[g,rows,:]=jnp.swapaxes(t,0,1).astype(gk.dtype)
        return 0
    lax.fori_loop(0,KEYS//TILE,chunk,0)

def back_q(kt,ds,dq):
    def tile(i,_):
        col=pl.ds(pl.multiple_of(i*TILE,TILE),TILE)
        r=[ (jnp.dot(kt[g,:KV,:],ds[g,:,col],preferred_element_type=F32)*SC).astype(BF) for g in range(2)]
        for p in range(2):
            x,y=halves(r[0][:,p*128:(p+1)*128],r[1][:,p*128:(p+1)*128])
            dq[i*4+2*p]=x
            dq[i*4+2*p+1]=y
        return 0
    lax.fori_loop(0,NT,tile,0)

def kern(parts, own, lists, qt, full, w, gout, ho, dq, gk, uv, qg,k,kt,mask,pt,do,cen,ot,ds):
    own=own[0]
    if 'p' in parts:
        make_mask(mask); prep_q(qt,qg)
        for g in range(2): build_keys(g,lists,full,k,kt,own)
    if 'f' in parts: forward(qg,k,kt,w,gout,mask,pt,do,cen,ot,uv,ho)
    if 's' in parts:
        for g in range(2): back_ds(g,k,pt,do,cen,ds)
    if 'k' in parts:
        for g in range(2): back_kv(g,qg,do,pt,ds,gk)
    if 'q' in parts: back_q(kt,ds,dq)

def call(own,lists,qt,full,w,gout,parts='pfskq'):
    V=pl.BlockSpec(memory_space=pltpu.VMEM)
    S=pl.BlockSpec(memory_space=pltpu.SMEM)
    return pl.pallas_call(functools.partial(kern,parts),
      out_shape=(jax.ShapeDtypeStruct((NH,TD,VH),BF),jax.ShapeDtypeStruct((NH,KV,TD),BF),
                 jax.ShapeDtypeStruct((2,KEYS,KP),BF),jax.ShapeDtypeStruct((NH,DL,VH),BF)),
      in_specs=[S,S,V,V,V,V], out_specs=(V,V,V,V),
      scratch_shapes=[pltpu.VMEM((2,KP,ROWS),BF),pltpu.VMEM((2,KEYS,KP),BF),pltpu.VMEM((2,KP,KEYS),BF),
        pltpu.VMEM((BLK,TILE),F32),pltpu.VMEM((2,KEYS,ROWS),BF),pltpu.VMEM((2,DL,ROWS),BF),
        pltpu.VMEM((2,8,ROWS),F32),pltpu.VMEM((2,DL,TILE),BF),pltpu.VMEM((2,KEYS,ROWS),BF)],
      compiler_params=pltpu.CompilerParams(vmem_limit_bytes=62*2**20), name="latent_attn")(own,lists,qt,full,w,gout)
MESH = pl.DeviceIdType.MESH
NCH = 4
CROWS = NH * DL // NCH
CH = CROWS // 2
QA = CH // 4
QB = QA // 4


def place():
    s = lax.axis_index("seq")
    z = lax.axis_index("head")
    return s, z, s % 2, (s // 2) % 4, s // 8


def seq_at(y, x, c):
    return (y * 4 + x) * 2 + c


def rcopy(src, dst, ssem, rsem, s, z):
    return pltpu.make_async_remote_copy(
        src_ref=src, dst_ref=dst, send_sem=ssem, recv_sem=rsem, device_id=(s, z), device_id_type=MESH
    )


def greet(seq_steps, head_steps):
    s, z, _, _, _ = place()
    barrier = pltpu.get_barrier_semaphore()
    for d in seq_steps:
        pl.semaphore_signal(barrier, inc=1, device_id=((s + d) % 32, z), device_id_type=MESH)
    for d in head_steps:
        pl.semaphore_signal(barrier, inc=1, device_id=(s, (z + d) % 4), device_id_type=MESH)
    pl.semaphore_wait(barrier, len(seq_steps) + len(head_steps))


def gather_body(cache_ref, full, lsem, zs, zr, s1, r1, s2, r2, s3, r3, s4, r4, s5, r5):
    s, z, c, x, y = place()
    barrier = pltpu.get_barrier_semaphore()
    peers = [(s, (z + d) % 4) for d in (1, 2, 3)]
    for d in (1, 3):
        peers.append((seq_at(y, (x + d) % 4, c), z))
        peers.append((seq_at((y + d) % 4, x, c), z))
    peers.append((seq_at(y, x, 1 - c), z))
    for p in peers:
        pl.semaphore_signal(barrier, inc=1, device_id=p, device_id_type=MESH)
    pl.semaphore_wait(barrier, len(peers))

    def nbr_a(d):
        return seq_at((y + d * c) % 4, (x + d * (1 - c)) % 4, c)

    def nbr_b(d):
        return seq_at((y + d * (1 - c)) % 4, (x + d * c) % 4, c)

    def at(a, b):
        return full.at[(y + a * c + b * (1 - c)) % 4, (x + a * (1 - c) + b * c) % 4, c]

    def shard(a, b):
        return at(a, b)

    rows = pl.ds(pl.multiple_of(z * 32, 32), 32)
    own = at(0, 0)
    local = pltpu.make_async_copy(cache_ref, own.at[rows], lsem)
    local.start()
    pend = []
    zc = []
    for d in (1, 2, 3):
        q = rcopy(cache_ref, own.at[rows], zs.at[d - 1], zr.at[d - 1], s, (z + d) % 4)
        q.start()
        zc.append(q)
    local.wait()
    for q in zc:
        q.wait_recv()
    pend += zc

    def start(src, ssem, rsem, dev):
        q = rcopy(src, src, ssem, rsem, dev, z)
        q.start()
        pend.append(q)

    def got(dst, rsem):
        rcopy(dst, dst, s5.at[0], rsem, s, (z + 1) % 4).wait_recv()

    lo, hi = pl.ds(0, 64), pl.ds(64, 64)
    twin = seq_at(y, x, 1 - c)

    def to_twin(a, b):
        k = (a % 4) * 4 + b % 4
        start(shard(a, b), s5.at[k], r5.at[k], twin)

    def b_sends(a):
        k = a % 4
        start(shard(a, 0), s3.at[k, 0], r3.at[k, 0], nbr_b(1))
        start(shard(a, 0), s3.at[k, 1], r3.at[k, 1], nbr_b(-1))

    start(own, s1.at[0], r1.at[0], nbr_a(1))
    start(own, s1.at[1], r1.at[1], nbr_a(-1))
    b_sends(0)
    to_twin(0, 0)
    got(shard(-1, 0), r1.at[0])
    start(shard(-1, 0).at[lo], s2.at[0], r2.at[0], nbr_a(1))
    got(shard(1, 0), r1.at[1])
    start(shard(1, 0).at[hi], s2.at[1], r2.at[1], nbr_a(-1))
    b_sends(-1)
    b_sends(1)
    to_twin(-1, 0)
    to_twin(1, 0)

    def b_relay(a):
        k = a % 4
        got(shard(a, -1), r3.at[k, 0])
        start(shard(a, -1).at[lo], s4.at[k, 0], r4.at[k, 0], nbr_b(1))
        got(shard(a, 1), r3.at[k, 1])
        start(shard(a, 1).at[hi], s4.at[k, 1], r4.at[k, 1], nbr_b(-1))
        to_twin(a, -1)
        to_twin(a, 1)

    b_relay(0)
    got(shard(2, 0).at[lo], r2.at[0])
    got(shard(2, 0).at[hi], r2.at[1])
    b_sends(2)
    to_twin(2, 0)
    for a in (-1, 1, 2):
        b_relay(a)
    for a in (0, -1, 1, 2):
        k = a % 4
        got(shard(a, 2).at[lo], r4.at[k, 0])
        got(shard(a, 2).at[hi], r4.at[k, 1])
        to_twin(a, 2)
    for a in range(4):
        for b in range(4):
            dst = full.at[(y + a * (1 - c) + b * c) % 4, (x + a * c + b * (1 - c)) % 4, 1 - c]
            got(dst, r5.at[a * 4 + b])
    for q in pend:
        q.wait_send()


def gather(cache):
    sems = [pltpu.SemaphoreType.DMA]
    for shape in ((3,), (3,), (2,), (2,), (2,), (2,), (4, 2), (4, 2), (4, 2), (4, 2), (16,), (16,)):
        sems.append(pltpu.SemaphoreType.DMA(shape))
    return pl.pallas_call(
        gather_body,
        out_shape=jax.ShapeDtypeStruct((4, 4, 2, TD, KV), BF),
        in_specs=[pl.BlockSpec(memory_space=pltpu.VMEM)],
        out_specs=pl.BlockSpec(memory_space=pltpu.VMEM),
        scratch_shapes=sems,
        compiler_params=pltpu.CompilerParams(
            collective_id=0, has_side_effects=True, vmem_limit_bytes=60 * 2**20
        ),
        name="gather_cache",
    )(cache)


def uv_stages(u, o, rc, ra1, ra2, rb, rb1, rb2, ss, rs):
    s, z, c, x, y = place()
    twin = seq_at(y, x, 1 - c)
    pa = x * (1 - c) + y * c
    pb = y * (1 - c) + x * c

    def nbr_a(d):
        return seq_at((y + d * c) % 4, (x + d * (1 - c)) % 4, c)

    def nbr_b(d):
        return seq_at((y + d * (1 - c)) % 4, (x + d * c) % 4, c)

    def ds(start, size):
        return pl.ds(pl.multiple_of(start, size), size)

    def add(dst, dst_ix, terms):
        t = terms[0][...].astype(F32)
        for r in terms[1:]:
            t = t + r[...].astype(F32)
        dst[dst_ix] = t.astype(BF)

    def pair(k, st, a, b, nbr):
        return [
            rcopy(a[0], a[1], ss.at[k, st, 0], rs.at[k, st, 0], nbr(1), z),
            rcopy(b[0], b[1], ss.at[k, st, 1], rs.at[k, st, 1], nbr(-1), z),
        ]

    base = c * CH

    def out(k, start, size):
        return o.at[k, pl.ds(pl.multiple_of(start, size), size)]

    def c0(k):
        return [rcopy(u.at[k, ds((1 - c) * CH, CH)], rc.at[k], ss.at[k, 0, 0], rs.at[k, 0, 0], twin, z)]

    def c1(k):
        q = ((pa + 2) % 4) * QA
        return pair(k, 1, (rc.at[k, ds(q, QA // 2)], ra1.at[k, 0]),
                    (rc.at[k, ds(q + QA // 2, QA // 2)], ra1.at[k, 1]), nbr_a)

    def c2(k):
        return pair(k, 2, (rc.at[k, ds((pa + 1) % 4 * QA, QA)], ra2.at[k, 0]),
                    (rc.at[k, ds((pa + 3) % 4 * QA, QA)], ra2.at[k, 1]), nbr_a)

    def c3(k):
        q = ((pb + 2) % 4) * QB
        return pair(k, 3, (rb.at[k, ds(q, QB // 2)], rb1.at[k, 0]),
                    (rb.at[k, ds(q + QB // 2, QB // 2)], rb1.at[k, 1]), nbr_b)

    def c4(k):
        return pair(k, 4, (rb.at[k, ds((pb + 1) % 4 * QB, QB)], rb2.at[k, 0]),
                    (rb.at[k, ds((pb + 3) % 4 * QB, QB)], rb2.at[k, 1]), nbr_b)

    def c5(k):
        m = out(k, base + pa * QA + pb * QB, QB)
        return pair(k, 5, (m, m), (m, m), nbr_b)

    def c6(k):
        lo = out(k, base + pa * QA + (pb + 3) % 4 * QB, QB // 2)
        hi = out(k, base + pa * QA + (pb + 1) % 4 * QB + QB // 2, QB // 2)
        return pair(k, 6, (lo, lo), (hi, hi), nbr_b)

    def c7(k):
        m = out(k, base + pa * QA, QA)
        return pair(k, 7, (m, m), (m, m), nbr_a)

    def c8(k):
        lo = out(k, base + (pa + 3) % 4 * QA, QA // 2)
        hi = out(k, base + (pa + 1) % 4 * QA + QA // 2, QA // 2)
        return pair(k, 8, (lo, lo), (hi, hi), nbr_a)

    def c9(k):
        m = out(k, base, CH)
        return [rcopy(m, m, ss.at[k, 9, 0], rs.at[k, 9, 0], twin, z)]

    def got5(k):
        return [out(k, base + pa * QA + (pb + 3) % 4 * QB, QB), out(k, base + pa * QA + (pb + 1) % 4 * QB, QB)]

    def got6(k):
        q = base + pa * QA + (pb + 2) % 4 * QB
        return [out(k, q, QB // 2), out(k, q + QB // 2, QB // 2)]

    def got7(k):
        return [out(k, base + (pa + 3) % 4 * QA, QA), out(k, base + (pa + 1) % 4 * QA, QA)]

    def got8(k):
        q = base + (pa + 2) % 4 * QA
        return [out(k, q, QA // 2), out(k, q + QA // 2, QA // 2)]

    def got9(k):
        return [out(k, (1 - c) * CH, CH)]

    makers = [c0, c1, c2, c3, c4, c5, c6, c7, c8, c9]

    def arrived(k, st):
        if st in (0, 1, 2, 3, 4):
            for q in makers[st](k):
                q.wait_recv()
        else:
            for i, dst in enumerate({5: got5, 6: got6, 7: got7, 8: got8, 9: got9}[st](k)):
                rcopy(dst, dst, ss.at[k, st, i], rs.at[k, st, i], twin, z).wait_recv()
        for q in makers[st](k):
            q.wait_send()

    def stage(k, st):
        if st > 0:
            arrived(k, st - 1)
        if st == 1:
            add(rc, (k,), [u.at[k, ds(base, CH)], rc.at[k]])
        elif st == 2:
            a = ds((pa + 1) % 4 * QA, QA // 2)
            b = ds((pa + 3) % 4 * QA + QA // 2, QA // 2)
            add(rc, (k, a), [rc.at[k, a], ra1.at[k, 0]])
            add(rc, (k, b), [rc.at[k, b], ra1.at[k, 1]])
        elif st == 3:
            add(rb, (k,), [rc.at[k, ds(pa * QA, QA)], ra2.at[k, 0], ra2.at[k, 1]])
        elif st == 4:
            a = ds((pb + 1) % 4 * QB, QB // 2)
            b = ds((pb + 3) % 4 * QB + QB // 2, QB // 2)
            add(rb, (k, a), [rb.at[k, a], rb1.at[k, 0]])
            add(rb, (k, b), [rb.at[k, b], rb1.at[k, 1]])
        elif st == 5:
            add(o, (k, ds(base + pa * QA + pb * QB, QB)),
                [rb.at[k, ds(pb * QB, QB)], rb2.at[k, 0], rb2.at[k, 1]])
        if st < 10:
            for q in makers[st](k):
                q.start()

    return stage


UV_SCRATCH = [
    pltpu.VMEM((NCH, CH, 128), BF),
    pltpu.VMEM((NCH, 2, QA // 2, 128), BF),
    pltpu.VMEM((NCH, 2, QA, 128), BF),
    pltpu.VMEM((NCH, QA, 128), BF),
    pltpu.VMEM((NCH, 2, QB // 2, 128), BF),
    pltpu.VMEM((NCH, 2, QB, 128), BF),
    pltpu.SemaphoreType.DMA((NCH, 10, 2)),
    pltpu.SemaphoreType.DMA((NCH, 10, 2)),
]


def cache_stages(inv, flag, gk, gc, zr1, zr2, rz, send, recv, part, zss, zrs, xss, xrs, fss, frs):
    s, z, c, x, y = place()
    z1, z2, z3 = (z + 1) % 4, (z + 2) % 4, (z + 3) % 4

    def first(g):
        return [
            rcopy(gk.at[g, 0:8, z2], zr1.at[g, 0], zss.at[g, 0, 0], zrs.at[g, 0, 0], s, z1),
            rcopy(gk.at[g, 8:16, z2], zr1.at[g, 1], zss.at[g, 0, 1], zrs.at[g, 0, 1], s, z3),
        ]

    def second(g):
        return [
            rcopy(gk.at[g, :, z1], zr2.at[g, 0], zss.at[g, 1, 0], zrs.at[g, 1, 0], s, z1),
            rcopy(gk.at[g, :, z3], zr2.at[g, 1], zss.at[g, 1, 1], zrs.at[g, 1, 1], s, z3),
        ]

    def head_send(g):
        for q in first(g):
            q.start()

    def head_relay(g):
        for q in first(g):
            q.wait()
        gk[g, 0:8, z1] = (gk[g, 0:8, z1].astype(F32) + zr1[g, 0].astype(F32)).astype(BF)
        gk[g, 8:16, z3] = (gk[g, 8:16, z3].astype(F32) + zr1[g, 1].astype(F32)).astype(BF)
        for q in second(g):
            q.start()

    def head_sum(g):
        for q in second(g):
            q.wait()
        rz[g, 0:16] = (gk[g, :, z].astype(F32) + zr2[g, 0].astype(F32) + zr2[g, 1].astype(F32)).astype(BF)
        rz[g, 16] = jnp.zeros((16, KP), BF)

    col = lax.broadcasted_iota(jnp.int32, (16, KP), 1)

    def spread():
        for d in range(32):
            t = (s + d) % 32
            v = rz[0, inv[0, t]].astype(F32) + rz[1, inv[1, t]].astype(F32)
            v = jnp.where(col == KV, flag[t], v)
            send[d] = v.astype(BF)
            if d:
                rcopy(send.at[d], recv.at[d], xss.at[d], xrs.at[d], t, z).start()

    def collect():
        a = jnp.zeros((16, KP), F32)
        b = jnp.zeros((16, KP), F32)
        for d in range(32):
            if d:
                q = rcopy(send.at[d], recv.at[d], xss.at[d], xrs.at[d], (s + d) % 32, z)
                q.wait()
                v = recv[d].astype(F32)
            else:
                v = send[0].astype(F32)
            f = v[:, KV : KV + 1]
            second_part = v * f
            b = b + second_part
            a = a + (v - second_part)
        part[0, 0] = a + rz[0, 0].astype(F32)
        part[0, 1] = b + rz[1, 0].astype(F32)
        for d in (1, 2, 3):
            rcopy(part.at[0], part.at[d], fss.at[d - 1], frs.at[d - 1], s, (z + d) % 4).start()

    def finish():
        for d in (1, 2, 3):
            rcopy(part.at[0], part.at[d], fss.at[d - 1], frs.at[d - 1], s, (z + d) % 4).wait()
        q = 2 * (z % 2)
        gc[0:16] = part[(z - q + 4) % 4, z // 2][:, :KV]
        gc[16:32] = part[(z - q + 3) % 4, z // 2][:, :KV]

    return head_send, head_relay, head_sum, spread, collect, finish


CACHE_SCRATCH = [
    pltpu.VMEM((2, 2, 8, 16, KP), BF),
    pltpu.VMEM((2, 2, 16, 16, KP), BF),
    pltpu.VMEM((2, 17, 16, KP), BF),
    pltpu.VMEM((32, 16, KP), BF),
    pltpu.VMEM((32, 16, KP), BF),
    pltpu.VMEM((4, 2, 16, KP), F32),
    pltpu.SemaphoreType.DMA((2, 2, 2)),
    pltpu.SemaphoreType.DMA((2, 2, 2)),
    pltpu.SemaphoreType.DMA((32,)),
    pltpu.SemaphoreType.DMA((32,)),
    pltpu.SemaphoreType.DMA((3,)),
    pltpu.SemaphoreType.DMA((3,)),
]


def reduce_body(inv, flag, u, gk_in, o, gc, gk, *scr):
    uv_scr, cache_scr = scr[: len(UV_SCRATCH)], scr[len(UV_SCRATCH) :]
    greet(range(1, 32), (1, 2, 3))
    stage = uv_stages(u, o, *uv_scr)
    head_send, head_relay, head_sum, spread, collect, finish = cache_stages(inv, flag, gk, gc, *cache_scr)
    gk[...] = gk_in[...]
    for g in range(2):
        head_send(g)
    steps = {3: [lambda: head_relay(0)], 4: [lambda: head_relay(1)], 6: [lambda: head_sum(0)],
             7: [lambda: head_sum(1), spread], 9: [collect], 10: [finish]}
    for slot in range(NCH + 10):
        for st in range(11):
            k = slot - st
            if 0 <= k < NCH:
                stage(k, st)
        for f in steps.get(slot, []):
            f()


def reduce(inv, flag, u, gk):
    v = pl.BlockSpec(memory_space=pltpu.VMEM)
    m = pl.BlockSpec(memory_space=pltpu.SMEM)
    return pl.pallas_call(
        reduce_body,
        out_shape=(jax.ShapeDtypeStruct((NCH, CROWS, 128), BF), jax.ShapeDtypeStruct((32, KV), F32)),
        in_specs=[m, m, v, v],
        out_specs=(v, v),
        scratch_shapes=[pltpu.VMEM((2, 16, 4, 16, KP), BF)] + UV_SCRATCH + CACHE_SCRATCH,
        compiler_params=pltpu.CompilerParams(
            collective_id=1, has_side_effects=True, vmem_limit_bytes=60 * 2**20
        ),
        name="reduce_grads",
    )(inv, flag, u, gk)


def on_device(queries, cache, lists, w_uv, grad_out):
    first_block = lax.axis_index("seq") * 2
    full = gather(cache).reshape(64, BLK, KV)
    ho, dq, gk, uv = call(first_block.reshape(1), lists, queries.transpose(1, 2, 0), full, w_uv, grad_out.transpose(1, 0, 2))
    shard = jnp.where(lists >= 0, lists // 2, -1)
    hit = shard[:, None, :] == jnp.arange(32)[None, :, None]
    inv = jnp.min(jnp.where(hit, jnp.arange(1, 16), 16), axis=-1).astype(jnp.int32)
    flag = jnp.max(jnp.where(hit, (lists % 2)[:, None, :], 0), axis=(0, 2)).astype(F32)
    o, gc = reduce(inv, flag, uv.reshape(NCH, CROWS, 128), gk.reshape(2, 16, 4, 16, KP))
    return ho.transpose(1, 0, 2), dq.transpose(2, 0, 1), gc, o.reshape(NH, DL, VH)


def solution(mesh):
    return jax.shard_map(
        on_device,
        mesh=mesh,
        in_specs=(
            P("seq", "head", None),
            P(("seq", "head"), None),
            P("seq", None),
            P("head", None, None),
            P("seq", "head", None),
        ),
        out_specs=(
            P("seq", "head", None),
            P("seq", "head", None),
            P(("seq", "head"), None),
            P("head", None, None),
        ),
        check_vma=False,
    )
```

```python
import functools, jax, jax.numpy as jnp, numpy as np
from jax import lax
from jax.experimental import pallas as pl
from jax.experimental.pallas import tpu as pltpu
from jax.sharding import PartitionSpec as P

BLK=64; KEEP=15; SLOTS=16; KEYS=1024; DL=512; KV=576; KP=640; NH=32; VH=128; TD=128
ROWS=2048; TILE=256; NT=8
SC=192.0**-0.5
L2E=1.4426950408889634
NEG=-1e30
F32=jnp.float32; BF=jnp.bfloat16
NTD=(((1,),(1,)),((),()))
TND=(((0,),(0,)),((),()))

def halves(a,b):
    return (jnp.concatenate([a[:, :64], b[:, :64]],1), jnp.concatenate([a[:, 64:], b[:, 64:]],1))

def make_mask(mask_ref):
    r=lax.broadcasted_iota(jnp.int32,(BLK,TILE),0)
    c=lax.broadcasted_iota(jnp.int32,(BLK,TILE),1)
    mask_ref[...]=jnp.where(r<=(c%BLK),0.0,NEG).astype(F32)

MESH = pl.DeviceIdType.MESH
NCH = 4
CROWS = NH * DL // NCH
CH = CROWS // 2
QA = CH // 4
QB = QA // 4


def place():
    s = lax.axis_index("seq")
    z = lax.axis_index("head")
    return s, z, s % 2, (s // 2) % 4, s // 8


def seq_at(y, x, c):
    return (y * 4 + x) * 2 + c


def rcopy(src, dst, ssem, rsem, s, z):
    return pltpu.make_async_remote_copy(
        src_ref=src, dst_ref=dst, send_sem=ssem, recv_sem=rsem, device_id=(s, z), device_id_type=MESH
    )


def greet(seq_steps, head_steps):
    s, z, _, _, _ = place()
    barrier = pltpu.get_barrier_semaphore()
    for d in seq_steps:
        pl.semaphore_signal(barrier, inc=1, device_id=((s + d) % 32, z), device_id_type=MESH)
    for d in head_steps:
        pl.semaphore_signal(barrier, inc=1, device_id=(s, (z + d) % 4), device_id_type=MESH)
    pl.semaphore_wait(barrier, len(seq_steps) + len(head_steps))


def uv_stages(u, o, rc, ra1, ra2, rb, rb1, rb2, ss, rs):
    s, z, c, x, y = place()
    twin = seq_at(y, x, 1 - c)
    pa = x * (1 - c) + y * c
    pb = y * (1 - c) + x * c

    def nbr_a(d):
        return seq_at((y + d * c) % 4, (x + d * (1 - c)) % 4, c)

    def nbr_b(d):
        return seq_at((y + d * (1 - c)) % 4, (x + d * c) % 4, c)

    def ds(start, size):
        return pl.ds(pl.multiple_of(start, size), size)

    def add(dst, dst_ix, terms):
        t = terms[0][...].astype(F32)
        for r in terms[1:]:
            t = t + r[...].astype(F32)
        dst[dst_ix] = t.astype(BF)

    def pair(k, st, a, b, nbr):
        return [
            rcopy(a[0], a[1], ss.at[k, st, 0], rs.at[k, st, 0], nbr(1), z),
            rcopy(b[0], b[1], ss.at[k, st, 1], rs.at[k, st, 1], nbr(-1), z),
        ]

    base = c * CH

    def out(k, start, size):
        return o.at[k, pl.ds(pl.multiple_of(start, size), size)]

    def c0(k):
        return [rcopy(u.at[k, ds((1 - c) * CH, CH)], rc.at[k], ss.at[k, 0, 0], rs.at[k, 0, 0], twin, z)]

    def c1(k):
        q = ((pa + 2) % 4) * QA
        return pair(k, 1, (rc.at[k, ds(q, QA // 2)], ra1.at[k, 0]),
                    (rc.at[k, ds(q + QA // 2, QA // 2)], ra1.at[k, 1]), nbr_a)

    def c2(k):
        return pair(k, 2, (rc.at[k, ds((pa + 1) % 4 * QA, QA)], ra2.at[k, 0]),
                    (rc.at[k, ds((pa + 3) % 4 * QA, QA)], ra2.at[k, 1]), nbr_a)

    def c3(k):
        q = ((pb + 2) % 4) * QB
        return pair(k, 3, (rb.at[k, ds(q, QB // 2)], rb1.at[k, 0]),
                    (rb.at[k, ds(q + QB // 2, QB // 2)], rb1.at[k, 1]), nbr_b)

    def c4(k):
        return pair(k, 4, (rb.at[k, ds((pb + 1) % 4 * QB, QB)], rb2.at[k, 0]),
                    (rb.at[k, ds((pb + 3) % 4 * QB, QB)], rb2.at[k, 1]), nbr_b)

    def c5(k):
        m = out(k, base + pa * QA + pb * QB, QB)
        return pair(k, 5, (m, m), (m, m), nbr_b)

    def c6(k):
        lo = out(k, base + pa * QA + (pb + 3) % 4 * QB, QB // 2)
        hi = out(k, base + pa * QA + (pb + 1) % 4 * QB + QB // 2, QB // 2)
        return pair(k, 6, (lo, lo), (hi, hi), nbr_b)

    def c7(k):
        m = out(k, base + pa * QA, QA)
        return pair(k, 7, (m, m), (m, m), nbr_a)

    def c8(k):
        lo = out(k, base + (pa + 3) % 4 * QA, QA // 2)
        hi = out(k, base + (pa + 1) % 4 * QA + QA // 2, QA // 2)
        return pair(k, 8, (lo, lo), (hi, hi), nbr_a)

    def c9(k):
        m = out(k, base, CH)
        return [rcopy(m, m, ss.at[k, 9, 0], rs.at[k, 9, 0], twin, z)]

    def got5(k):
        return [out(k, base + pa * QA + (pb + 3) % 4 * QB, QB), out(k, base + pa * QA + (pb + 1) % 4 * QB, QB)]

    def got6(k):
        q = base + pa * QA + (pb + 2) % 4 * QB
        return [out(k, q, QB // 2), out(k, q + QB // 2, QB // 2)]

    def got7(k):
        return [out(k, base + (pa + 3) % 4 * QA, QA), out(k, base + (pa + 1) % 4 * QA, QA)]

    def got8(k):
        q = base + (pa + 2) % 4 * QA
        return [out(k, q, QA // 2), out(k, q + QA // 2, QA // 2)]

    def got9(k):
        return [out(k, (1 - c) * CH, CH)]

    makers = [c0, c1, c2, c3, c4, c5, c6, c7, c8, c9]

    def arrived(k, st):
        if st in (0, 1, 2, 3, 4):
            for q in makers[st](k):
                q.wait_recv()
        else:
            for i, dst in enumerate({5: got5, 6: got6, 7: got7, 8: got8, 9: got9}[st](k)):
                rcopy(dst, dst, ss.at[k, st, i], rs.at[k, st, i], twin, z).wait_recv()
        for q in makers[st](k):
            q.wait_send()

    def stage(k, st):
        if st > 0:
            arrived(k, st - 1)
        if st == 1:
            add(rc, (k,), [u.at[k, ds(base, CH)], rc.at[k]])
        elif st == 2:
            a = ds((pa + 1) % 4 * QA, QA // 2)
            b = ds((pa + 3) % 4 * QA + QA // 2, QA // 2)
            add(rc, (k, a), [rc.at[k, a], ra1.at[k, 0]])
            add(rc, (k, b), [rc.at[k, b], ra1.at[k, 1]])
        elif st == 3:
            add(rb, (k,), [rc.at[k, ds(pa * QA, QA)], ra2.at[k, 0], ra2.at[k, 1]])
        elif st == 4:
            a = ds((pb + 1) % 4 * QB, QB // 2)
            b = ds((pb + 3) % 4 * QB + QB // 2, QB // 2)
            add(rb, (k, a), [rb.at[k, a], rb1.at[k, 0]])
            add(rb, (k, b), [rb.at[k, b], rb1.at[k, 1]])
        elif st == 5:
            add(o, (k, ds(base + pa * QA + pb * QB, QB)),
                [rb.at[k, ds(pb * QB, QB)], rb2.at[k, 0], rb2.at[k, 1]])
        if st < 10:
            for q in makers[st](k):
                q.start()

    return stage


UV_SCRATCH = [
    pltpu.VMEM((NCH, CH, 128), BF),
    pltpu.VMEM((NCH, 2, QA // 2, 128), BF),
    pltpu.VMEM((NCH, 2, QA, 128), BF),
    pltpu.VMEM((NCH, QA, 128), BF),
    pltpu.VMEM((NCH, 2, QB // 2, 128), BF),
    pltpu.VMEM((NCH, 2, QB, 128), BF),
    pltpu.SemaphoreType.DMA((NCH, 10, 2)),
    pltpu.SemaphoreType.DMA((NCH, 10, 2)),
]


class Gather:
    def __init__(self, cache_ref, full, lsem, zs, zr, s1, r1, s2, r2, s3, r3, s4, r4, s5, r5):
        self.__dict__.update(locals())
        self.pend = []

    def at(self, a, b, part=None):
        _, _, c, x, y = place()
        t = seq_at((y + a * c + b * (1 - c)) % 4, (x + a * (1 - c) + b * c) % 4, c)
        return self.block(t, part)

    def block(self, t, part):
        if part is None:
            return self.full.at[pl.ds(2 * t, 2)]
        return self.full.at[2 * t + part]

    def nbr_a(self, d):
        _, _, c, x, y = place()
        return seq_at((y + d * c) % 4, (x + d * (1 - c)) % 4, c)

    def nbr_b(self, d):
        _, _, c, x, y = place()
        return seq_at((y + d * (1 - c)) % 4, (x + d * c) % 4, c)

    def start(self, src, ssem, rsem, dev):
        q = rcopy(src, src, ssem, rsem, dev, place()[1])
        q.start()
        self.pend.append(q)

    def got(self, dst, rsem):
        s, z, _, _, _ = place()
        rcopy(dst, dst, self.s5.at[0], rsem, s, (z + 1) % 4).wait_recv()

    def to_twin(self, a, b):
        _, _, c, x, y = place()
        k = (a % 4) * 4 + b % 4
        self.start(self.at(a, b), self.s5.at[k], self.r5.at[k], seq_at(y, x, 1 - c))

    def b_sends(self, a):
        k = a % 4
        self.start(self.at(a, 0), self.s3.at[k, 0], self.r3.at[k, 0], self.nbr_b(1))
        self.start(self.at(a, 0), self.s3.at[k, 1], self.r3.at[k, 1], self.nbr_b(-1))

    def b_relay(self, a):
        k = a % 4
        self.got(self.at(a, -1), self.r3.at[k, 0])
        self.start(self.at(a, -1, 0), self.s4.at[k, 0], self.r4.at[k, 0], self.nbr_b(1))
        self.got(self.at(a, 1), self.r3.at[k, 1])
        self.start(self.at(a, 1, 1), self.s4.at[k, 1], self.r4.at[k, 1], self.nbr_b(-1))
        self.to_twin(a, -1)
        self.to_twin(a, 1)

    def step0(self):
        s, z, _, _, _ = place()
        mine = self.full.at[2 * s + z // 2, pl.ds(pl.multiple_of((z % 2) * 32, 32), 32)]
        self.local = pltpu.make_async_copy(self.cache_ref, mine, self.lsem)
        self.local.start()
        self.zc = [
            rcopy(self.cache_ref, mine, self.zs.at[d - 1], self.zr.at[d - 1], s, (z + d) % 4) for d in (1, 2, 3)
        ]
        for q in self.zc:
            q.start()
        self.pend += self.zc

    def step1(self):
        self.local.wait()
        for q in self.zc:
            q.wait_recv()
        self.start(self.at(0, 0), self.s1.at[0], self.r1.at[0], self.nbr_a(1))
        self.start(self.at(0, 0), self.s1.at[1], self.r1.at[1], self.nbr_a(-1))
        self.b_sends(0)
        self.to_twin(0, 0)

    def step2(self):
        self.got(self.at(-1, 0), self.r1.at[0])
        self.start(self.at(-1, 0, 0), self.s2.at[0], self.r2.at[0], self.nbr_a(1))
        self.got(self.at(1, 0), self.r1.at[1])
        self.start(self.at(1, 0, 1), self.s2.at[1], self.r2.at[1], self.nbr_a(-1))
        self.b_sends(-1)
        self.b_sends(1)
        self.to_twin(-1, 0)
        self.to_twin(1, 0)

    def step3(self):
        self.b_relay(0)
        self.got(self.at(2, 0, 0), self.r2.at[0])
        self.got(self.at(2, 0, 1), self.r2.at[1])
        self.b_sends(2)
        self.to_twin(2, 0)

    def step4(self):
        for a in (-1, 1):
            self.b_relay(a)

    def step5(self):
        self.b_relay(2)

    def step6(self):
        for a in (0, -1, 1, 2):
            k = a % 4
            self.got(self.at(a, 2, 0), self.r4.at[k, 0])
            self.got(self.at(a, 2, 1), self.r4.at[k, 1])
            self.to_twin(a, 2)

    def step7(self):
        _, _, c, x, y = place()
        for a in range(4):
            for b in range(4):
                t = seq_at((y + a * (1 - c) + b * c) % 4, (x + a * c + b * (1 - c)) % 4, 1 - c)
                self.got(self.block(t, None), self.r5.at[a * 4 + b])
        for q in self.pend:
            q.wait_send()


GATHER_SCRATCH = [pltpu.VMEM((64, BLK, KV), BF), pltpu.SemaphoreType.DMA] + [
    pltpu.SemaphoreType.DMA(shape)
    for shape in ((3,), (3,), (2,), (2,), (2,), (2,), (4, 2), (4, 2), (4, 2), (4, 2), (16,), (16,))
]


def cache_stages(inv, flag, gk, gc, zr1, zr2, rz, send, recv, part, zss, zrs, xss, xrs, fss, frs):
    s, z, c, x, y = place()
    z1, z2, z3 = (z + 1) % 4, (z + 2) % 4, (z + 3) % 4

    def first(u):
        g, b = u // 2, u % 2 * 8
        return [
            rcopy(gk.at[g, b : b + 4, z2], zr1.at[u, 0], zss.at[u, 0, 0], zrs.at[u, 0, 0], s, z1),
            rcopy(gk.at[g, b + 4 : b + 8, z2], zr1.at[u, 1], zss.at[u, 0, 1], zrs.at[u, 0, 1], s, z3),
        ]

    def second(u):
        g, b = u // 2, u % 2 * 8
        return [
            rcopy(gk.at[g, b : b + 8, z1], zr2.at[u, 0], zss.at[u, 1, 0], zrs.at[u, 1, 0], s, z1),
            rcopy(gk.at[g, b : b + 8, z3], zr2.at[u, 1], zss.at[u, 1, 1], zrs.at[u, 1, 1], s, z3),
        ]

    def head_send(u):
        for q in first(u):
            q.start()

    def head_relay(u):
        g, b = u // 2, u % 2 * 8
        for q in first(u):
            q.wait()
        gk[g, b : b + 4, z1] = (gk[g, b : b + 4, z1].astype(F32) + zr1[u, 0].astype(F32)).astype(BF)
        gk[g, b + 4 : b + 8, z3] = (gk[g, b + 4 : b + 8, z3].astype(F32) + zr1[u, 1].astype(F32)).astype(BF)
        for q in second(u):
            q.start()

    def head_sum(u):
        g, b = u // 2, u % 2 * 8
        for q in second(u):
            q.wait()
        t = gk[g, b : b + 8, z].astype(F32) + zr2[u, 0].astype(F32) + zr2[u, 1].astype(F32)
        rz[g, b : b + 8] = t.astype(BF)
        if b:
            rz[g, 16] = jnp.zeros((16, KP), BF)

    col = lax.broadcasted_iota(jnp.int32, (16, KP), 1)

    def spread():
        for d in range(32):
            t = (s + d) % 32
            v = rz[0, inv[0, t]].astype(F32) + rz[1, inv[1, t]].astype(F32)
            v = jnp.where(col == KV, flag[t], v)
            send[d] = v.astype(BF)
            if d:
                rcopy(send.at[d], recv.at[d], xss.at[d], xrs.at[d], t, z).start()

    def collect():
        a = jnp.zeros((16, KP), F32)
        b = jnp.zeros((16, KP), F32)
        for d in range(32):
            if d:
                q = rcopy(send.at[d], recv.at[d], xss.at[d], xrs.at[d], (s + d) % 32, z)
                q.wait()
                v = recv[d].astype(F32)
            else:
                v = send[0].astype(F32)
            second_part = v * v[:, KV : KV + 1]
            b = b + second_part
            a = a + (v - second_part)
        part[0, 0] = a + rz[0, 0].astype(F32)
        part[0, 1] = b + rz[1, 0].astype(F32)
        for d in (1, 2, 3):
            rcopy(part.at[0], part.at[d], fss.at[d - 1], frs.at[d - 1], s, (z + d) % 4).start()

    def finish():
        for d in (1, 2, 3):
            rcopy(part.at[0], part.at[d], fss.at[d - 1], frs.at[d - 1], s, (z + d) % 4).wait()
        q = 2 * (z % 2)
        gc[0:16] = part[(z - q + 4) % 4, z // 2][:, :KV]
        gc[16:32] = part[(z - q + 3) % 4, z // 2][:, :KV]

    return head_send, head_relay, head_sum, spread, collect, finish


CACHE_SCRATCH = [
    pltpu.VMEM((4, 2, 4, 16, KP), BF),
    pltpu.VMEM((4, 2, 8, 16, KP), BF),
    pltpu.VMEM((2, 17, 16, KP), BF),
    pltpu.VMEM((32, 16, KP), BF),
    pltpu.VMEM((32, 16, KP), BF),
    pltpu.VMEM((4, 2, 16, KP), F32),
    pltpu.SemaphoreType.DMA((4, 2, 2)),
    pltpu.SemaphoreType.DMA((4, 2, 2)),
    pltpu.SemaphoreType.DMA((32,)),
    pltpu.SemaphoreType.DMA((32,)),
    pltpu.SemaphoreType.DMA((3,)),
    pltpu.SemaphoreType.DMA((3,)),
]

PHASES = [("fwd", 8, 4.0), ("ds0", 8, 0.6), ("kv0", 4, 1.6), ("ds1", 8, 0.6), ("kv1", 4, 1.6), ("dq", 8, 1.0)]
UV_GAP = 3.2
HEAD_GAP = 5.0


def plan():
    ends, now = [], 0.0
    for name, n, us in PHASES:
        for i in range(n):
            now += us
            ends.append((now, name, i))
    when = {(name, i): t for t, name, i in ends}
    todo = []
    for k in range(NCH):
        ready = when["fwd", 8 // NCH * (k + 1) - 1]
        for st in range(11):
            todo.append((ready + st * UV_GAP, "uv", (k, st)))
    for u in range(4):
        ready = when["kv%d" % (u // 2), 1 + 2 * (u % 2)]
        todo.append((ready, "head_send", (u,)))
        todo.append((ready + HEAD_GAP, "head_relay", (u,)))
        todo.append((ready + 2 * HEAD_GAP, "head_sum", (u,)))
    todo.sort(key=lambda e: e[0])
    at, late = {}, []
    for t, op, arg in todo:
        for end, name, i in ends:
            if end >= t - 1e-6:
                at.setdefault((name, i), []).append((op, arg))
                break
        else:
            late.append((op, arg))
    return at, late


def fused_body(lists, inv, flag, cache, qt, w_hbm, gout_hbm, ho_hbm, dq_hbm, uv_hbm, gc, *scr):
    qg, k, kt, mask, pt, do, cen, ot, gk, u, w, gout, hb, qb, lsem, hsem, qsem, osem = scr[:18]
    scr = scr[18:]
    gat = Gather(cache, *scr[: len(GATHER_SCRATCH)])
    full = gat.full
    scr = scr[len(GATHER_SCRATCH) :]
    stage = uv_stages(u, u, *scr[: len(UV_SCRATCH)])
    cs = cache_stages(inv, flag, gk, gc, *scr[len(UV_SCRATCH) :])
    head_send, head_relay, head_sum, spread, collect, finish = cs
    s, z, c, x, y = place()

    loads = [pltpu.make_async_copy(w_hbm, w, lsem.at[0]), pltpu.make_async_copy(gout_hbm, gout, lsem.at[1])]
    for q in loads:
        q.start()

    def q_load(i, slot):
        return pltpu.make_async_copy(qt.at[pl.ds(4 * i, 4)], qb.at[slot], qsem.at[slot])

    q_load(0, 0).start()
    q_load(1, 1).start()
    greet(range(1, 32), (1, 2, 3))
    gat.step0()
    make_mask(mask)
    row = lax.broadcasted_iota(jnp.int32, (64, ROWS), 0)
    one = jnp.where(row == 0, 1.0, 0.0).astype(BF)
    qg[0, KV:, :] = one
    qg[1, KV:, :] = one
    gat.step1()

    def prep_q(lo, hi):
        def body(i, _):
            q_load(i, i % 2).wait()
            for p in range(2):
                a, b = halves(qb[i % 2, 2 * p], qb[i % 2, 2 * p + 1])
                col = pl.ds(pl.multiple_of(i * TILE + p * 128, 128), 128)
                qg[0, :KV, col] = a
                qg[1, :KV, col] = b

            @pl.when(i + 2 < NT)
            def _():
                q_load(i + 2, i % 2).start()

            return 0

        lax.fori_loop(lo, hi, body, 0)

    def prep_do(lo, hi):
        def body(i, _):
            d0 = lax.dot_general(w[2 * i], gout[2 * i], NTD, preferred_element_type=F32).astype(BF)
            d1 = lax.dot_general(w[2 * i + 1], gout[2 * i + 1], NTD, preferred_element_type=F32).astype(BF)
            a, b = halves(d0, d1)
            col = pl.ds(pl.multiple_of(i * 128, 128), 128)
            do[0, :, col] = a
            do[1, :, col] = b
            return 0

        lax.fori_loop(lo, hi, body, 0)

    prep_q(0, 4)
    gat.step2()
    prep_q(4, 8)
    gat.step3()
    for q in loads:
        q.wait()
    prep_do(0, 8)
    gat.step4()
    prep_do(8, 16)
    gat.step5()
    gat.step6()
    gat.step7()

    colid = lax.broadcasted_iota(jnp.int32, (BLK, KP - DL), 1)
    for g in range(2):
        for j in range(SLOTS):
            if j == 0:
                blk = full[2 * s + g]
                bias = jnp.float32(0.0)
            else:
                e = lists[g, j - 1]
                blk = full[jnp.maximum(e, 0)]
                bias = jnp.where(e >= 0, 0.0, NEG).astype(F32)
            k[g, j * BLK : (j + 1) * BLK, :DL] = blk[:, :DL]
            rot = jnp.concatenate([blk[:, DL:].astype(F32), jnp.zeros((BLK, 64), F32)], 1)
            k[g, j * BLK : (j + 1) * BLK, DL:] = jnp.where(colid == 64, bias, rot).astype(BF)
        for b in range(8):
            kt[g, :, b * 128 : (b + 1) * 128] = jnp.swapaxes(k[g, b * 128 : (b + 1) * 128, :], 0, 1)

    uv_out = [pltpu.make_async_copy(u.at[q], uv_hbm.at[q], osem.at[q]) for q in range(NCH)]

    def run(op, arg):
        if op == "uv":
            stage(*arg)
            if arg[1] == 10:
                uv_out[arg[0]].start()
        else:
            {"head_send": head_send, "head_relay": head_relay, "head_sum": head_sum}[op](*arg)

    at, late = plan()

    def loop(name, body):
        n = {p[0]: p[1] for p in PHASES}[name]

        def step(i, _):
            body(i)
            for j in range(n):
                if (name, j) in at:

                    @pl.when(i == j)
                    def _():
                        for op, arg in at[name, j]:
                            run(op, arg)

            return 0

        lax.fori_loop(0, n, step, 0)

    def cols(i):
        return pl.ds(pl.multiple_of(i * TILE, TILE), TILE)

    def ho_store(i, slot):
        return pltpu.make_async_copy(hb.at[slot], ho_hbm.at[pl.ds(4 * i, 4)], hsem.at[slot])

    def fwd(i):
        col = cols(i)
        for g in range(2):
            sc = jnp.dot(k[g], qg[g, :, col], preferred_element_type=F32)
            sc = jnp.concatenate([sc[:BLK] + mask[...], sc[BLK:]], 0)
            m = jnp.max(sc, axis=0, keepdims=True)
            e = jnp.exp2((sc - m) * (SC * L2E))
            inv_l = 1.0 / jnp.sum(e, axis=0, keepdims=True)
            pb = e.astype(BF)
            pt[g, :, col] = pb
            o = jnp.dot(kt[g, :DL, :], pb, preferred_element_type=F32) * inv_l
            ot[g] = o.astype(BF)
            dn = (do[g, :, col].astype(F32) * inv_l).astype(BF)
            do[g, :, col] = dn
            centre = jnp.sum(o * dn.astype(F32), axis=0, keepdims=True)
            cen[g, :, col] = jnp.broadcast_to(centre, (8, TILE))

        @pl.when(i >= 2)
        def _():
            ho_store(i - 2, i % 2).wait()

        for p in range(2):
            hh = halves(ot[0, :, p * 128 : (p + 1) * 128], ot[1, :, p * 128 : (p + 1) * 128])
            for q in range(2):
                h = i * 4 + 2 * p + q
                part = jnp.dot(hh[q], gout[h], preferred_element_type=F32).astype(BF)
                per = CROWS // DL
                u[h // per, pl.ds(pl.multiple_of(h % per * DL, DL), DL)] = part
                hb[i % 2, 2 * p + q] = lax.dot_general(hh[q], w[h], TND, preferred_element_type=F32).astype(BF)
        ho_store(i, i % 2).start()

    loop("fwd", fwd)
    ho_store(6, 0).wait()
    ho_store(7, 1).wait()

    def back_ds(g, to):
        def body(i):
            col = cols(i)
            dp = jnp.dot(k[g, :, :DL], do[g, :, col], preferred_element_type=F32)
            t = pt[g, :, col].astype(F32) * (dp - cen[g, 0:1, col])
            pt[to, :, col] = t.astype(BF)

        return body

    def back_kv(g, d):
        def body(i):
            rows = cols(i)
            a = lax.dot_general(qg[g, :KV, :], pt[d, rows, :], NTD, preferred_element_type=F32) * SC
            b = lax.dot_general(do[g], pt[g, rows, :], NTD, preferred_element_type=F32)
            t = jnp.concatenate([a[:DL] + b, a[DL:], jnp.zeros((KP - KV, TILE), F32)], 0)
            t = jnp.swapaxes(t, 0, 1).astype(BF)
            gk[g, pl.ds(4 * i, 4)] = t.reshape(4, 4, 16, KP)

        return body

    loop("ds0", back_ds(0, 2))
    loop("kv0", back_kv(0, 2))
    loop("ds1", back_ds(1, 0))
    loop("kv1", back_kv(1, 0))

    def dq_store(i, slot):
        return pltpu.make_async_copy(qb.at[slot], dq_hbm.at[pl.ds(4 * i, 4)], qsem.at[slot])

    def back_q(i):
        col = cols(i)

        @pl.when(i >= 2)
        def _():
            dq_store(i - 2, i % 2).wait()

        r = []
        for g, d in ((0, 2), (1, 0)):
            r.append((jnp.dot(kt[g, :KV, :], pt[d, :, col], preferred_element_type=F32) * SC).astype(BF))
        for p in range(2):
            a, b = halves(r[0][:, p * 128 : (p + 1) * 128], r[1][:, p * 128 : (p + 1) * 128])
            qb[i % 2, 2 * p] = a
            qb[i % 2, 2 * p + 1] = b
        dq_store(i, i % 2).start()

    loop("dq", back_q)
    for op, arg in late:
        run(op, arg)
    spread()
    collect()
    finish()
    dq_store(6, 0).wait()
    dq_store(7, 1).wait()
    for q in uv_out:
        q.wait()


def attention(lists, inv, flag, cache, qt, w, gout):
    v = pl.BlockSpec(memory_space=pltpu.VMEM)
    m = pl.BlockSpec(memory_space=pltpu.SMEM)
    a = pl.BlockSpec(memory_space=pl.ANY)
    scratch = [
        pltpu.VMEM((2, KP, ROWS), BF),
        pltpu.VMEM((2, KEYS, KP), BF),
        pltpu.VMEM((2, KP, KEYS), BF),
        pltpu.VMEM((BLK, TILE), F32),
        pltpu.VMEM((3, KEYS, ROWS), BF),
        pltpu.VMEM((2, DL, ROWS), BF),
        pltpu.VMEM((2, 8, ROWS), F32),
        pltpu.VMEM((2, DL, TILE), BF),
        pltpu.VMEM((2, 16, 4, 16, KP), BF),
        pltpu.VMEM((NCH, CROWS, 128), BF),
        pltpu.VMEM((NH, DL, VH), BF),
        pltpu.VMEM((NH, TD, VH), BF),
        pltpu.VMEM((2, 4, TD, VH), BF),
        pltpu.VMEM((2, 4, KV, TD), BF),
        pltpu.SemaphoreType.DMA((2,)),
        pltpu.SemaphoreType.DMA((2,)),
        pltpu.SemaphoreType.DMA((2,)),
        pltpu.SemaphoreType.DMA((NCH,)),
    ]
    return pl.pallas_call(
        fused_body,
        out_shape=(
            jax.ShapeDtypeStruct((NH, TD, VH), BF),
            jax.ShapeDtypeStruct((NH, KV, TD), BF),
            jax.ShapeDtypeStruct((NCH, CROWS, 128), BF),
            jax.ShapeDtypeStruct((32, KV), F32),
        ),
        in_specs=[m, m, m, v, a, a, a],
        out_specs=(a, a, a, v),
        scratch_shapes=scratch + GATHER_SCRATCH + UV_SCRATCH + CACHE_SCRATCH,
        compiler_params=pltpu.CompilerParams(
            collective_id=0, has_side_effects=True, vmem_limit_bytes=63 * 2**20
        ),
        name="latent_attention",
    )(lists, inv, flag, cache, qt, w, gout)


def on_device(queries, cache, lists, w_uv, grad_out):
    shard = jnp.where(lists >= 0, lists // 2, -1)
    hit = shard[:, None, :] == jnp.arange(32)[None, :, None]
    inv = jnp.min(jnp.where(hit, jnp.arange(1, 16), 16), axis=-1).astype(jnp.int32)
    flag = jnp.max(jnp.where(hit, (lists % 2)[:, None, :], 0), axis=(0, 2)).astype(F32)
    ho, dq, uv, gc = attention(
        lists, inv, flag, cache, queries.transpose(1, 2, 0), w_uv, grad_out.transpose(1, 0, 2)
    )
    return ho.transpose(1, 0, 2), dq.transpose(2, 0, 1), gc, uv.reshape(NH, DL, VH)


def solution(mesh):
    return jax.shard_map(
        on_device,
        mesh=mesh,
        in_specs=(
            P("seq", "head", None),
            P(("seq", "head"), None),
            P("seq", None),
            P("head", None, None),
            P("seq", "head", None),
        ),
        out_specs=(
            P("seq", "head", None),
            P("seq", "head", None),
            P(("seq", "head"), None),
            P("head", None, None),
        ),
        check_vma=False,
    )
```

```python
import functools, jax, jax.numpy as jnp, numpy as np
from jax import lax
from jax.experimental import pallas as pl
from jax.experimental.pallas import tpu as pltpu
from jax.sharding import PartitionSpec as P

BLK=64; KEEP=15; SLOTS=16; KEYS=1024; DL=512; KV=576; KP=640; NH=32; VH=128; TD=128
ROWS=2048; TILE=256; NT=8
SC=192.0**-0.5
L2E=1.4426950408889634
NEG=-1e30
F32=jnp.float32; BF=jnp.bfloat16
NTD=(((1,),(1,)),((),()))
TND=(((0,),(0,)),((),()))

def halves(a,b):
    return (jnp.concatenate([a[:, :64], b[:, :64]],1), jnp.concatenate([a[:, 64:], b[:, 64:]],1))

def make_mask(mask_ref):
    r=lax.broadcasted_iota(jnp.int32,(BLK,TILE),0)
    c=lax.broadcasted_iota(jnp.int32,(BLK,TILE),1)
    mask_ref[...]=jnp.where(r<=(c%BLK),0.0,NEG).astype(F32)

MESH = pl.DeviceIdType.MESH
NCH = 4
CROWS = NH * DL // NCH
CH = CROWS // 2
QA = CH // 4
QB = QA // 4


def place():
    s = lax.axis_index("seq")
    z = lax.axis_index("head")
    return s, z, s % 2, (s // 2) % 4, s // 8


def seq_at(y, x, c):
    return (y * 4 + x) * 2 + c


def rcopy(src, dst, ssem, rsem, s, z):
    return pltpu.make_async_remote_copy(
        src_ref=src, dst_ref=dst, send_sem=ssem, recv_sem=rsem, device_id=(s, z), device_id_type=MESH
    )


def greet(seq_steps, head_steps):
    s, z, _, _, _ = place()
    barrier = pltpu.get_barrier_semaphore()
    for d in seq_steps:
        pl.semaphore_signal(barrier, inc=1, device_id=((s + d) % 32, z), device_id_type=MESH)
    for d in head_steps:
        pl.semaphore_signal(barrier, inc=1, device_id=(s, (z + d) % 4), device_id_type=MESH)
    pl.semaphore_wait(barrier, len(seq_steps) + len(head_steps))


def uv_stages(u, o, rc, ra1, ra2, rb, rb1, rb2, ss, rs):
    s, z, c, x, y = place()
    twin = seq_at(y, x, 1 - c)
    pa = x * (1 - c) + y * c
    pb = y * (1 - c) + x * c

    def nbr_a(d):
        return seq_at((y + d * c) % 4, (x + d * (1 - c)) % 4, c)

    def nbr_b(d):
        return seq_at((y + d * (1 - c)) % 4, (x + d * c) % 4, c)

    def ds(start, size):
        return pl.ds(pl.multiple_of(start, size), size)

    def add(dst, dst_ix, terms):
        t = terms[0][...].astype(F32)
        for r in terms[1:]:
            t = t + r[...].astype(F32)
        dst[dst_ix] = t.astype(BF)

    def pair(k, st, a, b, nbr):
        return [
            rcopy(a[0], a[1], ss.at[k, st, 0], rs.at[k, st, 0], nbr(1), z),
            rcopy(b[0], b[1], ss.at[k, st, 1], rs.at[k, st, 1], nbr(-1), z),
        ]

    base = c * CH

    def out(k, start, size):
        return o.at[k, pl.ds(pl.multiple_of(start, size), size)]

    def c0(k):
        return [rcopy(u.at[k, ds((1 - c) * CH, CH)], rc.at[k], ss.at[k, 0, 0], rs.at[k, 0, 0], twin, z)]

    def c1(k):
        q = ((pa + 2) % 4) * QA
        return pair(k, 1, (rc.at[k, ds(q, QA // 2)], ra1.at[k, 0]),
                    (rc.at[k, ds(q + QA // 2, QA // 2)], ra1.at[k, 1]), nbr_a)

    def c2(k):
        return pair(k, 2, (rc.at[k, ds((pa + 1) % 4 * QA, QA)], ra2.at[k, 0]),
                    (rc.at[k, ds((pa + 3) % 4 * QA, QA)], ra2.at[k, 1]), nbr_a)

    def c3(k):
        q = ((pb + 2) % 4) * QB
        return pair(k, 3, (rb.at[k, ds(q, QB // 2)], rb1.at[k, 0]),
                    (rb.at[k, ds(q + QB // 2, QB // 2)], rb1.at[k, 1]), nbr_b)

    def c4(k):
        return pair(k, 4, (rb.at[k, ds((pb + 1) % 4 * QB, QB)], rb2.at[k, 0]),
                    (rb.at[k, ds((pb + 3) % 4 * QB, QB)], rb2.at[k, 1]), nbr_b)

    def c5(k):
        m = out(k, base + pa * QA + pb * QB, QB)
        return pair(k, 5, (m, m), (m, m), nbr_b)

    def c6(k):
        lo = out(k, base + pa * QA + (pb + 3) % 4 * QB, QB // 2)
        hi = out(k, base + pa * QA + (pb + 1) % 4 * QB + QB // 2, QB // 2)
        return pair(k, 6, (lo, lo), (hi, hi), nbr_b)

    def c7(k):
        m = out(k, base + pa * QA, QA)
        return pair(k, 7, (m, m), (m, m), nbr_a)

    def c8(k):
        lo = out(k, base + (pa + 3) % 4 * QA, QA // 2)
        hi = out(k, base + (pa + 1) % 4 * QA + QA // 2, QA // 2)
        return pair(k, 8, (lo, lo), (hi, hi), nbr_a)

    def c9(k):
        m = out(k, base, CH)
        return [rcopy(m, m, ss.at[k, 9, 0], rs.at[k, 9, 0], twin, z)]

    def got5(k):
        return [out(k, base + pa * QA + (pb + 3) % 4 * QB, QB), out(k, base + pa * QA + (pb + 1) % 4 * QB, QB)]

    def got6(k):
        q = base + pa * QA + (pb + 2) % 4 * QB
        return [out(k, q, QB // 2), out(k, q + QB // 2, QB // 2)]

    def got7(k):
        return [out(k, base + (pa + 3) % 4 * QA, QA), out(k, base + (pa + 1) % 4 * QA, QA)]

    def got8(k):
        q = base + (pa + 2) % 4 * QA
        return [out(k, q, QA // 2), out(k, q + QA // 2, QA // 2)]

    def got9(k):
        return [out(k, (1 - c) * CH, CH)]

    makers = [c0, c1, c2, c3, c4, c5, c6, c7, c8, c9]

    def arrived(k, st):
        if st in (0, 1, 2, 3, 4):
            for q in makers[st](k):
                q.wait_recv()
        else:
            for i, dst in enumerate({5: got5, 6: got6, 7: got7, 8: got8, 9: got9}[st](k)):
                rcopy(dst, dst, ss.at[k, st, i], rs.at[k, st, i], twin, z).wait_recv()
        for q in makers[st](k):
            q.wait_send()

    def stage(k, st):
        if st > 0:
            arrived(k, st - 1)
        if st == 1:
            add(rc, (k,), [u.at[k, ds(base, CH)], rc.at[k]])
        elif st == 2:
            a = ds((pa + 1) % 4 * QA, QA // 2)
            b = ds((pa + 3) % 4 * QA + QA // 2, QA // 2)
            add(rc, (k, a), [rc.at[k, a], ra1.at[k, 0]])
            add(rc, (k, b), [rc.at[k, b], ra1.at[k, 1]])
        elif st == 3:
            add(rb, (k,), [rc.at[k, ds(pa * QA, QA)], ra2.at[k, 0], ra2.at[k, 1]])
        elif st == 4:
            a = ds((pb + 1) % 4 * QB, QB // 2)
            b = ds((pb + 3) % 4 * QB + QB // 2, QB // 2)
            add(rb, (k, a), [rb.at[k, a], rb1.at[k, 0]])
            add(rb, (k, b), [rb.at[k, b], rb1.at[k, 1]])
        elif st == 5:
            add(o, (k, ds(base + pa * QA + pb * QB, QB)),
                [rb.at[k, ds(pb * QB, QB)], rb2.at[k, 0], rb2.at[k, 1]])
        if st < 10:
            for q in makers[st](k):
                q.start()

    return stage


UV_SCRATCH = [
    pltpu.VMEM((NCH, CH, 128), BF),
    pltpu.VMEM((NCH, 2, QA // 2, 128), BF),
    pltpu.VMEM((NCH, 2, QA, 128), BF),
    pltpu.VMEM((NCH, QA, 128), BF),
    pltpu.VMEM((NCH, 2, QB // 2, 128), BF),
    pltpu.VMEM((NCH, 2, QB, 128), BF),
    pltpu.SemaphoreType.DMA((NCH, 10, 2)),
    pltpu.SemaphoreType.DMA((NCH, 10, 2)),
]


VMEM_LIMIT = 63 * 2**20
WIDE = 512


class Gather:
    def __init__(self, cache_ref, full, lsem, zs, zr, s1, r1, s2, r2, s3, r3, s4, r4, s5, r5):
        self.__dict__.update(locals())
        self.pend = []

    def at(self, a, b, part=None):
        _, _, c, x, y = place()
        t = seq_at((y + a * c + b * (1 - c)) % 4, (x + a * (1 - c) + b * c) % 4, c)
        return self.block(t, part)

    def block(self, t, part):
        if part is None:
            return self.full.at[pl.ds(2 * t, 2)]
        return self.full.at[2 * t + part]

    def nbr_a(self, d):
        _, _, c, x, y = place()
        return seq_at((y + d * c) % 4, (x + d * (1 - c)) % 4, c)

    def nbr_b(self, d):
        _, _, c, x, y = place()
        return seq_at((y + d * (1 - c)) % 4, (x + d * c) % 4, c)

    def start(self, src, ssem, rsem, dev):
        q = rcopy(src, src, ssem, rsem, dev, place()[1])
        q.start()
        self.pend.append(q)

    def got(self, dst, rsem):
        s, z, _, _, _ = place()
        rcopy(dst, dst, self.s5.at[0], rsem, s, (z + 1) % 4).wait_recv()

    def to_twin(self, a, b):
        _, _, c, x, y = place()
        k = (a % 4) * 4 + b % 4
        self.start(self.at(a, b), self.s5.at[k], self.r5.at[k], seq_at(y, x, 1 - c))

    def send_part(self, a, b, part, side, sems, nbr):
        ssem, rsem = sems
        self.start(self.at(a, b, part), ssem.at[side, part], rsem.at[side, part], nbr(1 - 2 * side))

    def first_sends(self, a, b, sems, nbr):
        self.send_part(a, b, 0, 0, sems, nbr)
        self.send_part(a, b, 1, 1, sems, nbr)
        self.send_part(a, b, 1, 0, sems, nbr)
        self.send_part(a, b, 0, 1, sems, nbr)

    def b_sends(self, a):
        k = a % 4
        self.first_sends(a, 0, (self.s3.at[k], self.r3.at[k]), self.nbr_b)

    def b_relay(self, a):
        k = a % 4
        self.got(self.at(a, -1, 0), self.r3.at[k, 0, 0])
        self.start(self.at(a, -1, 0), self.s4.at[k, 0], self.r4.at[k, 0], self.nbr_b(1))
        self.got(self.at(a, 1, 1), self.r3.at[k, 1, 1])
        self.start(self.at(a, 1, 1), self.s4.at[k, 1], self.r4.at[k, 1], self.nbr_b(-1))

    def b_rest(self, a):
        k = a % 4
        self.got(self.at(a, -1, 1), self.r3.at[k, 0, 1])
        self.to_twin(a, -1)
        self.got(self.at(a, 1, 0), self.r3.at[k, 1, 0])
        self.to_twin(a, 1)

    def step0(self):
        s, z, _, _, _ = place()
        mine = self.full.at[2 * s + z // 2, pl.ds(pl.multiple_of((z % 2) * 32, 32), 32)]
        self.local = pltpu.make_async_copy(self.cache_ref, mine, self.lsem)
        self.local.start()
        self.zc = [
            rcopy(self.cache_ref, mine, self.zs.at[d - 1], self.zr.at[d - 1], s, (z + d) % 4) for d in (1, 2, 3)
        ]
        for q in self.zc:
            q.start()
        self.pend += self.zc

    def step1(self):
        self.local.wait()
        for q in self.zc:
            q.wait_recv()
        self.first_sends(0, 0, (self.s1, self.r1), self.nbr_a)
        self.b_sends(0)
        self.to_twin(0, 0)

    def step2(self):
        self.got(self.at(-1, 0, 0), self.r1.at[0, 0])
        self.start(self.at(-1, 0, 0), self.s2.at[0], self.r2.at[0], self.nbr_a(1))
        self.got(self.at(1, 0, 1), self.r1.at[1, 1])
        self.start(self.at(1, 0, 1), self.s2.at[1], self.r2.at[1], self.nbr_a(-1))
        self.got(self.at(-1, 0, 1), self.r1.at[0, 1])
        self.got(self.at(1, 0, 0), self.r1.at[1, 0])
        self.b_sends(-1)
        self.b_sends(1)
        self.to_twin(-1, 0)
        self.to_twin(1, 0)

    def step3(self):
        self.b_relay(0)
        self.got(self.at(2, 0, 0), self.r2.at[0])
        self.got(self.at(2, 0, 1), self.r2.at[1])
        self.b_sends(2)
        self.b_rest(0)
        self.to_twin(2, 0)

    def step4(self):
        for a in (-1, 1):
            self.b_relay(a)
        for a in (-1, 1):
            self.b_rest(a)

    def step5(self):
        self.b_relay(2)
        self.b_rest(2)

    def step6(self):
        for a in (0, -1, 1, 2):
            k = a % 4
            self.got(self.at(a, 2, 0), self.r4.at[k, 0])
            self.got(self.at(a, 2, 1), self.r4.at[k, 1])
            self.to_twin(a, 2)

    def step7(self):
        _, _, c, x, y = place()
        for a in range(4):
            for b in range(4):
                t = seq_at((y + a * (1 - c) + b * c) % 4, (x + a * c + b * (1 - c)) % 4, 1 - c)
                self.got(self.block(t, None), self.r5.at[a * 4 + b])
        for q in self.pend:
            q.wait_send()


GATHER_SCRATCH = [pltpu.VMEM((64, BLK, KV), BF), pltpu.SemaphoreType.DMA] + [
    pltpu.SemaphoreType.DMA(shape)
    for shape in ((3,), (3,), (2, 2), (2, 2), (2,), (2,), (4, 2, 2), (4, 2, 2), (4, 2), (4, 2), (16,), (16,))
]


def cache_stages(inv, flag, gk, gc, zr1, zr2, rz, send, recv, part, zss, zrs, xss, xrs, fss, frs):
    s, z, c, x, y = place()
    z1, z2, z3 = (z + 1) % 4, (z + 2) % 4, (z + 3) % 4

    def quarter(b, n, q):
        return gk.at[pl.ds(b, n), pl.ds(pl.multiple_of(q * 16, 16), 16)]

    def first(u):
        b = 8 * u
        return [
            rcopy(quarter(b, 4, z2), zr1.at[u, 0], zss.at[u, 0, 0], zrs.at[u, 0, 0], s, z1),
            rcopy(quarter(b + 4, 4, z2), zr1.at[u, 1], zss.at[u, 0, 1], zrs.at[u, 0, 1], s, z3),
        ]

    def second(u):
        b = 8 * u
        return [
            rcopy(quarter(b, 8, z1), zr2.at[u, 0], zss.at[u, 1, 0], zrs.at[u, 1, 0], s, z1),
            rcopy(quarter(b, 8, z3), zr2.at[u, 1], zss.at[u, 1, 1], zrs.at[u, 1, 1], s, z3),
        ]

    def head_send(u):
        for q in first(u):
            q.start()

    def head_relay(u):
        b = 8 * u
        for q in first(u):
            q.wait()
        for r, b0, q in ((zr1.at[u, 0], b, z1), (zr1.at[u, 1], b + 4, z3)):
            t = quarter(b0, 4, q)
            t[...] = (t[...].astype(F32) + r[...].astype(F32)).astype(BF)
        for q in second(u):
            q.start()

    def head_sum(u):
        for q in second(u):
            q.wait()
        t = quarter(8 * u, 8, z)[...].astype(F32) + zr2[u, 0].astype(F32) + zr2[u, 1].astype(F32)
        rz[u // 2, 8 * (u % 2) : 8 * (u % 2) + 8] = t.astype(BF)
        if u % 2:
            rz[u // 2, 16] = jnp.zeros((16, KV), BF)

    def spread():
        for d in range(32):
            t = (s + d) % 32
            v = rz[0, inv[0, t]].astype(F32) + rz[1, inv[1, t]].astype(F32)
            mark = jnp.zeros((16, KP - KV), F32) + flag[t].astype(F32)
            send[d] = jnp.concatenate([v, mark], 1).astype(BF)
            if d:
                rcopy(send.at[d], recv.at[d], xss.at[d], xrs.at[d], t, z).start()

    def collect():
        a = jnp.zeros((16, KV), F32)
        b = jnp.zeros((16, KV), F32)
        for d in range(32):
            if d:
                rcopy(send.at[d], recv.at[d], xss.at[d], xrs.at[d], (s + d) % 32, z).wait()
                v = recv[d].astype(F32)
            else:
                v = send[0].astype(F32)
            v, mark = v[:, :KV], v[:, KV : KV + 1]
            second_part = v * mark
            b = b + second_part
            a = a + (v - second_part)
        part[0, 0] = a + rz[0, 0].astype(F32)
        part[0, 1] = b + rz[1, 0].astype(F32)
        for d in (1, 2, 3):
            rcopy(part.at[0], part.at[d], fss.at[d - 1], frs.at[d - 1], s, (z + d) % 4).start()

    def finish():
        for d in (1, 2, 3):
            rcopy(part.at[0], part.at[d], fss.at[d - 1], frs.at[d - 1], s, (z + d) % 4).wait()
        q = 2 * (z % 2)
        gc[0:16] = part[(z - q + 4) % 4, z // 2]
        gc[16:32] = part[(z - q + 3) % 4, z // 2]

    return head_send, head_relay, head_sum, spread, collect, finish


CACHE_SCRATCH = [
    pltpu.VMEM((4, 2, 4, 16, KV), BF),
    pltpu.VMEM((4, 2, 8, 16, KV), BF),
    pltpu.VMEM((2, 17, 16, KV), BF),
    pltpu.VMEM((32, 16, KP), BF),
    pltpu.VMEM((32, 16, KP), BF),
    pltpu.VMEM((4, 2, 16, KV), F32),
    pltpu.SemaphoreType.DMA((4, 2, 2)),
    pltpu.SemaphoreType.DMA((4, 2, 2)),
    pltpu.SemaphoreType.DMA((32,)),
    pltpu.SemaphoreType.DMA((32,)),
    pltpu.SemaphoreType.DMA((3,)),
    pltpu.SemaphoreType.DMA((3,)),
]

PHASES = [("fwd", 8, 2.3), ("ds0", 2, 1.3), ("kv0", 2, 2.6), ("ds1", 2, 1.3), ("kv1", 2, 2.6), ("dq", 4, 1.5)]
UV_GAP = 3.2
HEAD_GAP = 4.0


def plan():
    ends, now = [], 0.0
    for name, n, us in PHASES:
        for i in range(n):
            now += us
            ends.append((now, name, i))
    when = {(name, i): t for t, name, i in ends}
    todo = []
    for k in range(NCH):
        ready = when["fwd", 8 // NCH * (k + 1) - 1]
        for st in range(11):
            todo.append((ready + st * UV_GAP, "uv", (k, st)))
    for u in range(4):
        ready = when["kv%d" % (u // 2), u % 2]
        todo.append((ready, "head_send", (u,)))
        todo.append((ready + HEAD_GAP, "head_relay", (u,)))
        todo.append((ready + 2 * HEAD_GAP, "head_sum", (u,)))
    todo.sort(key=lambda e: e[0])
    at, late = {}, []
    for t, op, arg in todo:
        for end, name, i in ends:
            if end >= t - 1e-6:
                at.setdefault((name, i), []).append((op, arg))
                break
        else:
            late.append((op, arg))
    return at, late


def fused_body(lists, cache, qt, w_hbm, gout_hbm, ho_hbm, dq_hbm, uv_hbm, gc, *scr):
    (qg, k, kt, mask, pt, do, cen, ot, sa, sb, u, w, gout, hb, qb, inv, flag,
     lsem, hsem, qsem, osem) = scr[:21]
    scr = scr[21:]
    gat = Gather(cache, *scr[: len(GATHER_SCRATCH)])
    full = gat.full
    scr = scr[len(GATHER_SCRATCH) :]
    stage = uv_stages(u, u, *scr[: len(UV_SCRATCH)])
    gk = full
    cs = cache_stages(inv, flag, gk, gc, *scr[len(UV_SCRATCH) :])
    head_send, head_relay, head_sum, spread, collect, finish = cs
    s, z, c, x, y = place()

    barrier = pltpu.get_barrier_semaphore()
    for d in range(1, 32):
        pl.semaphore_signal(barrier, inc=1, device_id=((s + d) % 32, z), device_id_type=MESH)
    for d in range(1, 4):
        pl.semaphore_signal(barrier, inc=1, device_id=(s, (z + d) % 4), device_id_type=MESH)

    def q_load(i, slot):
        return pltpu.make_async_copy(qt.at[pl.ds(8 * i, 8)], qb.at[slot], qsem.at[slot])

    g_load = pltpu.make_async_copy(gout_hbm, u.at[0], lsem.at[1])
    w_load = pltpu.make_async_copy(w_hbm, w, lsem.at[0])
    g_load.start()
    q_load(0, 0).start()
    q_load(1, 1).start()
    w_load.start()

    r = lax.broadcasted_iota(jnp.int32, (BLK, WIDE), 0)
    cc = lax.broadcasted_iota(jnp.int32, (BLK, WIDE), 1)
    mask[...] = jnp.where(r <= (cc % BLK), 0.0, NEG).astype(F32)
    row = lax.broadcasted_iota(jnp.int32, (64, ROWS), 0)
    one = jnp.where(row == 0, 1.0, 0.0).astype(BF)
    qg[0, KV:, :] = one
    qg[1, KV:, :] = one
    pl.semaphore_wait(barrier, 34)
    gat.step0()

    def find(t, _):
        which = jnp.int32(0)
        for g in range(2):
            slot = jnp.int32(16)
            for j in range(KEEP):
                d = lists[g, j] - 2 * t
                hit = (d >= 0) & (d < 2)
                slot = jnp.where(hit, j + 1, slot)
                which = jnp.where(hit, d, which)
            inv[g, t] = slot
        flag[t] = which
        return 0

    g_load.wait()

    def turn(i, _):
        t = pl.ds(pl.multiple_of(i * 16, 16), 16)
        x = u[0, pl.ds(pl.multiple_of(i * 512, 512), 512)].reshape(16, NH, VH)
        gout[:, t, :] = jnp.swapaxes(x, 0, 1)
        return 0

    lax.fori_loop(0, TD // 16, turn, 0)
    gat.step1()

    def prep_q(lo, hi):
        def body(i, _):
            q_load(i, i % 2).wait()
            for p in range(4):
                a, b = halves(qb[i % 2, 2 * p], qb[i % 2, 2 * p + 1])
                col = pl.ds(pl.multiple_of(i * WIDE + p * 128, 128), 128)
                qg[0, :KV, col] = a
                qg[1, :KV, col] = b

            @pl.when(i + 2 < 4)
            def _():
                q_load(i + 2, i % 2).start()

            return 0

        lax.fori_loop(lo, hi, body, 0)

    def prep_do(lo, hi):
        def body(i, _):
            for p in range(4):
                h = 8 * i + 2 * p
                d0 = lax.dot_general(w[h], gout[h], NTD, preferred_element_type=F32).astype(BF)
                d1 = lax.dot_general(w[h + 1], gout[h + 1], NTD, preferred_element_type=F32).astype(BF)
                a, b = halves(d0, d1)
                col = pl.ds(pl.multiple_of(i * WIDE + p * 128, 128), 128)
                do[0, :, col] = a
                do[1, :, col] = b
            return 0

        lax.fori_loop(lo, hi, body, 0)

    prep_q(0, 2)
    gat.step2()
    prep_q(2, 4)
    gat.step3()
    w_load.wait()
    prep_do(0, 2)
    gat.step4()
    prep_do(2, 4)
    gat.step5()
    lax.fori_loop(0, 32, find, 0)
    gat.step6()
    gat.step7()

    colid = lax.broadcasted_iota(jnp.int32, (BLK, KP - DL), 1)
    for g in range(2):
        for j in range(SLOTS):
            if j == 0:
                blk = full[2 * s + g]
                bias = jnp.float32(0.0)
            else:
                e = lists[g, j - 1]
                blk = full[jnp.maximum(e, 0)]
                bias = jnp.where(e >= 0, 0.0, NEG).astype(F32)
            k[g, j * BLK : (j + 1) * BLK, :DL] = blk[:, :DL]
            rot = jnp.concatenate([blk[:, DL:].astype(F32), jnp.zeros((BLK, 64), F32)], 1)
            k[g, j * BLK : (j + 1) * BLK, DL:] = jnp.where(colid == 64, bias, rot).astype(BF)
        for b in range(8):
            t = jnp.swapaxes(k[g, b * 128 : (b + 1) * 128, :], 0, 1)
            kt[g, :, b * 128 : (b + 1) * 128] = t[:KV]

    uv_out = [pltpu.make_async_copy(u.at[q], uv_hbm.at[q], osem.at[q]) for q in range(NCH)]

    def run(op, arg):
        if op == "uv":
            stage(*arg)
            if arg[1] == 10:
                uv_out[arg[0]].start()
        else:
            {"head_send": head_send, "head_relay": head_relay, "head_sum": head_sum}[op](*arg)

    at, late = plan()
    steps = {p[0]: p[1] for p in PHASES}

    def hook(name, i, part=0, parts=1):
        for j in range(part, steps[name], parts):
            if (name, j) in at:

                @pl.when(i == j // parts)
                def _():
                    for op, arg in at[name, j]:
                        run(op, arg)

    def loop(name, body, parts=1):
        def step(i, _):
            body(i)
            hook(name, i, parts - 1, parts)
            return 0

        lax.fori_loop(0, steps[name] // parts, step, 0)

    def cols(i, n=WIDE):
        return pl.ds(pl.multiple_of(i * n, n), n)

    def ho_store(i, slot):
        return pltpu.make_async_copy(hb.at[slot], ho_hbm.at[pl.ds(8 * i, 8)], hsem.at[slot])

    def scores(to, g, i):
        to[...] = jnp.dot(k[g], qg[g, :, cols(i)], preferred_element_type=F32)

    def softmax(sc, g, col):
        sc[:BLK] = sc[:BLK] + mask[...]
        m = jnp.max(sc[...], axis=0, keepdims=True)
        total = jnp.zeros((8, WIDE), F32)
        for b in range(16):
            e = jnp.exp2((sc[b * 64 : (b + 1) * 64] - m) * (SC * L2E))
            total = total + jnp.sum(e.reshape(8, 8, WIDE), axis=0)
            pt[g, b * 64 : (b + 1) * 64, col] = e.astype(BF)
        return 1.0 / jnp.sum(total, axis=0, keepdims=True)

    def values(g, col, inv_l):
        o = jnp.dot(kt[g, :DL, :], pt[g, :, col], preferred_element_type=F32) * inv_l
        ot[g] = o.astype(BF)
        dn = (do[g, :, col].astype(F32) * inv_l).astype(BF)
        do[g, :, col] = dn
        centre = jnp.sum(o * dn.astype(F32), axis=0, keepdims=True)
        cen[g, :, col] = jnp.broadcast_to(centre, (8, WIDE))

    scores(sa, 0, 0)

    def fwd(i):
        col = cols(i)
        scores(sb, 1, i)
        values(0, col, softmax(sa, 0, col))
        hook("fwd", i, 0, 2)
        scores(sa, 0, jnp.minimum(i + 1, 3))
        values(1, col, softmax(sb, 1, col))

        @pl.when(i >= 2)
        def _():
            ho_store(i - 2, i % 2).wait()

        for p in range(4):
            hh = halves(ot[0, :, p * 128 : (p + 1) * 128], ot[1, :, p * 128 : (p + 1) * 128])
            for q in range(2):
                h = 2 * p + q
                part = jnp.dot(hh[q], gout[8 * i + h], preferred_element_type=F32).astype(BF)
                u[i, h * DL : (h + 1) * DL] = part
                hb[i % 2, h] = lax.dot_general(hh[q], w[8 * i + h], TND, preferred_element_type=F32).astype(BF)
        ho_store(i, i % 2).start()

    loop("fwd", fwd, 2)
    ho_store(2, 0).wait()
    ho_store(3, 1).wait()

    def back_ds(g, to):
        def body(i):
            for b, tmp in enumerate((sa, sb)):
                col = cols(2 * i + b)
                tmp[...] = jnp.dot(k[g, :, :DL], do[g, :, col], preferred_element_type=F32)
            for b, tmp in enumerate((sa, sb)):
                col = cols(2 * i + b)
                for q in range(8):
                    rows = slice(q * 128, (q + 1) * 128)
                    t = pt[g, rows, col].astype(F32) * (tmp[rows] - cen[g, 0:1, col])
                    pt[to, rows, col] = t.astype(BF)

        return body

    def back_kv(g, d):
        def body(i):
            rows = cols(i)
            sa[:KV] = lax.dot_general(qg[g, :KV, :], pt[d, rows, :], NTD, preferred_element_type=F32)
            sb[:DL] = lax.dot_general(do[g], pt[g, rows, :], NTD, preferred_element_type=F32)
            zero = jnp.zeros((KP - KV, WIDE), F32)
            t = jnp.concatenate([sa[:DL] * SC + sb[:DL], sa[DL:KV] * SC, zero], 0).astype(BF)
            t = jnp.swapaxes(t, 0, 1)
            gk[pl.ds(16 * g + 8 * i, 8)] = t[:, :KV].reshape(8, BLK, KV)

        return body

    loop("ds0", back_ds(0, 2))
    loop("kv0", back_kv(0, 2))
    loop("ds1", back_ds(1, 0))
    loop("kv1", back_kv(1, 0))

    def dq_store(i, slot):
        return pltpu.make_async_copy(qb.at[slot], dq_hbm.at[pl.ds(8 * i, 8)], qsem.at[slot])

    def back_q(i):
        col = cols(i)

        @pl.when(i >= 2)
        def _():
            dq_store(i - 2, i % 2).wait()

        r = []
        for g, d in ((0, 2), (1, 0)):
            r.append((jnp.dot(kt[g], pt[d, :, col], preferred_element_type=F32) * SC).astype(BF))
        for p in range(4):
            a, b = halves(r[0][:, p * 128 : (p + 1) * 128], r[1][:, p * 128 : (p + 1) * 128])
            qb[i % 2, 2 * p] = a
            qb[i % 2, 2 * p + 1] = b
        dq_store(i, i % 2).start()

    loop("dq", back_q)
    for op, arg in late:
        run(op, arg)
    spread()
    collect()
    finish()
    dq_store(2, 0).wait()
    dq_store(3, 1).wait()
    for q in uv_out:
        q.wait()


def attention(lists, cache, qt, w, gout):
    v = pl.BlockSpec(memory_space=pltpu.VMEM)
    m = pl.BlockSpec(memory_space=pltpu.SMEM)
    a = pl.BlockSpec(memory_space=pl.ANY)
    scratch = [
        pltpu.VMEM((2, KP, ROWS), BF),
        pltpu.VMEM((2, KEYS, KP), BF),
        pltpu.VMEM((2, KV, KEYS), BF),
        pltpu.VMEM((BLK, WIDE), F32),
        pltpu.VMEM((3, KEYS, ROWS), BF),
        pltpu.VMEM((2, DL, ROWS), BF),
        pltpu.VMEM((2, 8, ROWS), F32),
        pltpu.VMEM((2, DL, WIDE), BF),
        pltpu.VMEM((KEYS, WIDE), F32),
        pltpu.VMEM((KEYS, WIDE), F32),
        pltpu.VMEM((NCH, CROWS, 128), BF),
        pltpu.VMEM((NH, DL, VH), BF),
        pltpu.VMEM((NH, TD, VH), BF),
        pltpu.VMEM((2, 8, TD, VH), BF),
        pltpu.VMEM((2, 8, KV, TD), BF),
        pltpu.SMEM((2, 32), jnp.int32),
        pltpu.SMEM((32,), jnp.int32),
        pltpu.SemaphoreType.DMA((2,)),
        pltpu.SemaphoreType.DMA((2,)),
        pltpu.SemaphoreType.DMA((2,)),
        pltpu.SemaphoreType.DMA((NCH,)),
    ]
    return pl.pallas_call(
        fused_body,
        out_shape=(
            jax.ShapeDtypeStruct((NH, TD, VH), BF),
            jax.ShapeDtypeStruct((NH, KV, TD), BF),
            jax.ShapeDtypeStruct((NCH, CROWS, 128), BF),
            jax.ShapeDtypeStruct((32, KV), F32),
        ),
        in_specs=[m, v, a, a, a],
        out_specs=(a, a, a, v),
        scratch_shapes=scratch + GATHER_SCRATCH + UV_SCRATCH + CACHE_SCRATCH,
        compiler_params=pltpu.CompilerParams(
            collective_id=0, has_side_effects=True, vmem_limit_bytes=VMEM_LIMIT
        ),
        name="latent_attention",
    )(lists, cache, qt, w, gout)


def on_device(queries, cache, lists, w_uv, grad_out):
    ho, dq, uv, gc = attention(
        lists, cache, queries.transpose(1, 2, 0), w_uv, grad_out.reshape(TD * NH, VH)
    )
    return ho.transpose(1, 0, 2), dq.transpose(2, 0, 1), gc, uv.reshape(NH, DL, VH)


def solution(mesh):
    return jax.shard_map(
        on_device,
        mesh=mesh,
        in_specs=(
            P("seq", "head", None),
            P(("seq", "head"), None),
            P("seq", None),
            P("head", None, None),
            P("seq", "head", None),
        ),
        out_specs=(
            P("seq", "head", None),
            P("seq", "head", None),
            P(("seq", "head"), None),
            P("head", None, None),
        ),
        check_vma=False,
    )
```

```python
import functools, jax, jax.numpy as jnp, numpy as np
from jax import lax
from jax.experimental import pallas as pl
from jax.experimental.pallas import tpu as pltpu
from jax.sharding import PartitionSpec as P

BLK=64; KEEP=15; SLOTS=16; KEYS=1024; DL=512; KV=576; KP=640; NH=32; VH=128; TD=128
ROWS=2048; TILE=256; NT=8
SC=192.0**-0.5
L2E=1.4426950408889634
NEG=-1e30
F32=jnp.float32; BF=jnp.bfloat16
NTD=(((1,),(1,)),((),()))
TND=(((0,),(0,)),((),()))

def halves(a,b):
    return (jnp.concatenate([a[:, :64], b[:, :64]],1), jnp.concatenate([a[:, 64:], b[:, 64:]],1))

def make_mask(mask_ref):
    r=lax.broadcasted_iota(jnp.int32,(BLK,TILE),0)
    c=lax.broadcasted_iota(jnp.int32,(BLK,TILE),1)
    mask_ref[...]=jnp.where(r<=(c%BLK),0.0,NEG).astype(F32)

MESH = pl.DeviceIdType.MESH
NCH = 4
CROWS = NH * DL // NCH
CH = CROWS // 2
QA = CH // 4
QB = QA // 4


def place():
    s = lax.axis_index("seq")
    z = lax.axis_index("head")
    return s, z, s % 2, (s // 2) % 4, s // 8


def seq_at(y, x, c):
    return (y * 4 + x) * 2 + c


def rcopy(src, dst, ssem, rsem, s, z):
    return pltpu.make_async_remote_copy(
        src_ref=src, dst_ref=dst, send_sem=ssem, recv_sem=rsem, device_id=(s, z), device_id_type=MESH
    )


def greet(seq_steps, head_steps):
    s, z, _, _, _ = place()
    barrier = pltpu.get_barrier_semaphore()
    for d in seq_steps:
        pl.semaphore_signal(barrier, inc=1, device_id=((s + d) % 32, z), device_id_type=MESH)
    for d in head_steps:
        pl.semaphore_signal(barrier, inc=1, device_id=(s, (z + d) % 4), device_id_type=MESH)
    pl.semaphore_wait(barrier, len(seq_steps) + len(head_steps))


def uv_stages(u, o, rc, ra1, ra2, rb, rb1, rb2, ss, rs):
    s, z, c, x, y = place()
    twin = seq_at(y, x, 1 - c)
    pa = x * (1 - c) + y * c
    pb = y * (1 - c) + x * c

    def nbr_a(d):
        return seq_at((y + d * c) % 4, (x + d * (1 - c)) % 4, c)

    def nbr_b(d):
        return seq_at((y + d * (1 - c)) % 4, (x + d * c) % 4, c)

    def ds(start, size):
        return pl.ds(pl.multiple_of(start, size), size)

    def add(dst, dst_ix, terms):
        t = terms[0][...].astype(F32)
        for r in terms[1:]:
            t = t + r[...].astype(F32)
        dst[dst_ix] = t.astype(BF)

    def pair(k, st, a, b, nbr):
        return [
            rcopy(a[0], a[1], ss.at[k, st, 0], rs.at[k, st, 0], nbr(1), z),
            rcopy(b[0], b[1], ss.at[k, st, 1], rs.at[k, st, 1], nbr(-1), z),
        ]

    base = c * CH

    def out(k, start, size):
        return o.at[k, pl.ds(pl.multiple_of(start, size), size)]

    def c0(k):
        return [rcopy(u.at[k, ds((1 - c) * CH, CH)], rc.at[k], ss.at[k, 0, 0], rs.at[k, 0, 0], twin, z)]

    def c1(k):
        q = ((pa + 2) % 4) * QA
        return pair(k, 1, (rc.at[k, ds(q, QA // 2)], ra1.at[k, 0]),
                    (rc.at[k, ds(q + QA // 2, QA // 2)], ra1.at[k, 1]), nbr_a)

    def c2(k):
        return pair(k, 2, (rc.at[k, ds((pa + 1) % 4 * QA, QA)], ra2.at[k, 0]),
                    (rc.at[k, ds((pa + 3) % 4 * QA, QA)], ra2.at[k, 1]), nbr_a)

    def c3(k):
        q = ((pb + 2) % 4) * QB
        return pair(k, 3, (rb.at[k, ds(q, QB // 2)], rb1.at[k, 0]),
                    (rb.at[k, ds(q + QB // 2, QB // 2)], rb1.at[k, 1]), nbr_b)

    def c4(k):
        return pair(k, 4, (rb.at[k, ds((pb + 1) % 4 * QB, QB)], rb2.at[k, 0]),
                    (rb.at[k, ds((pb + 3) % 4 * QB, QB)], rb2.at[k, 1]), nbr_b)

    def c5(k):
        m = out(k, base + pa * QA + pb * QB, QB)
        return pair(k, 5, (m, m), (m, m), nbr_b)

    def c6(k):
        lo = out(k, base + pa * QA + (pb + 3) % 4 * QB, QB // 2)
        hi = out(k, base + pa * QA + (pb + 1) % 4 * QB + QB // 2, QB // 2)
        return pair(k, 6, (lo, lo), (hi, hi), nbr_b)

    def c7(k):
        m = out(k, base + pa * QA, QA)
        return pair(k, 7, (m, m), (m, m), nbr_a)

    def c8(k):
        lo = out(k, base + (pa + 3) % 4 * QA, QA // 2)
        hi = out(k, base + (pa + 1) % 4 * QA + QA // 2, QA // 2)
        return pair(k, 8, (lo, lo), (hi, hi), nbr_a)

    def c9(k):
        m = out(k, base, CH)
        return [rcopy(m, m, ss.at[k, 9, 0], rs.at[k, 9, 0], twin, z)]

    def got5(k):
        return [out(k, base + pa * QA + (pb + 3) % 4 * QB, QB), out(k, base + pa * QA + (pb + 1) % 4 * QB, QB)]

    def got6(k):
        q = base + pa * QA + (pb + 2) % 4 * QB
        return [out(k, q, QB // 2), out(k, q + QB // 2, QB // 2)]

    def got7(k):
        return [out(k, base + (pa + 3) % 4 * QA, QA), out(k, base + (pa + 1) % 4 * QA, QA)]

    def got8(k):
        q = base + (pa + 2) % 4 * QA
        return [out(k, q, QA // 2), out(k, q + QA // 2, QA // 2)]

    def got9(k):
        return [out(k, (1 - c) * CH, CH)]

    makers = [c0, c1, c2, c3, c4, c5, c6, c7, c8, c9]

    def arrived(k, st):
        if st in (0, 1, 2, 3, 4):
            for q in makers[st](k):
                q.wait_recv()
        else:
            for i, dst in enumerate({5: got5, 6: got6, 7: got7, 8: got8, 9: got9}[st](k)):
                rcopy(dst, dst, ss.at[k, st, i], rs.at[k, st, i], twin, z).wait_recv()
        for q in makers[st](k):
            q.wait_send()

    def stage(k, st):
        if st > 0:
            arrived(k, st - 1)
        if st == 1:
            add(rc, (k,), [u.at[k, ds(base, CH)], rc.at[k]])
        elif st == 2:
            a = ds((pa + 1) % 4 * QA, QA // 2)
            b = ds((pa + 3) % 4 * QA + QA // 2, QA // 2)
            add(rc, (k, a), [rc.at[k, a], ra1.at[k, 0]])
            add(rc, (k, b), [rc.at[k, b], ra1.at[k, 1]])
        elif st == 3:
            add(rb, (k,), [rc.at[k, ds(pa * QA, QA)], ra2.at[k, 0], ra2.at[k, 1]])
        elif st == 4:
            a = ds((pb + 1) % 4 * QB, QB // 2)
            b = ds((pb + 3) % 4 * QB + QB // 2, QB // 2)
            add(rb, (k, a), [rb.at[k, a], rb1.at[k, 0]])
            add(rb, (k, b), [rb.at[k, b], rb1.at[k, 1]])
        elif st == 5:
            add(o, (k, ds(base + pa * QA + pb * QB, QB)),
                [rb.at[k, ds(pb * QB, QB)], rb2.at[k, 0], rb2.at[k, 1]])
        if st < 10:
            for q in makers[st](k):
                q.start()

    return stage


UV_SCRATCH = [
    pltpu.VMEM((NCH, CH, 128), BF),
    pltpu.VMEM((NCH, 2, QA // 2, 128), BF),
    pltpu.VMEM((NCH, 2, QA, 128), BF),
    pltpu.VMEM((NCH, QA, 128), BF),
    pltpu.VMEM((NCH, 2, QB // 2, 128), BF),
    pltpu.VMEM((NCH, 2, QB, 128), BF),
    pltpu.SemaphoreType.DMA((NCH, 10, 2)),
    pltpu.SemaphoreType.DMA((NCH, 10, 2)),
]


VMEM_LIMIT = 63 * 2**20
WIDE = 512


class Gather:
    def __init__(self, cache_ref, full, lsem, zs, zr, s1, r1, s2, r2, s3, r3, s4, r4, s5, r5):
        self.__dict__.update(locals())
        self.pend = []

    def at(self, a, b, part=None):
        _, _, c, x, y = place()
        t = seq_at((y + a * c + b * (1 - c)) % 4, (x + a * (1 - c) + b * c) % 4, c)
        return self.block(t, part)

    def block(self, t, part):
        if part is None:
            return self.full.at[pl.ds(2 * t, 2)]
        return self.full.at[2 * t + part]

    def nbr_a(self, d):
        _, _, c, x, y = place()
        return seq_at((y + d * c) % 4, (x + d * (1 - c)) % 4, c)

    def nbr_b(self, d):
        _, _, c, x, y = place()
        return seq_at((y + d * (1 - c)) % 4, (x + d * c) % 4, c)

    def start(self, src, ssem, rsem, dev):
        q = rcopy(src, src, ssem, rsem, dev, place()[1])
        q.start()
        self.pend.append(q)

    def got(self, dst, rsem):
        s, z, _, _, _ = place()
        rcopy(dst, dst, self.s5.at[0], rsem, s, (z + 1) % 4).wait_recv()

    def to_twin(self, a, b):
        _, _, c, x, y = place()
        k = (a % 4) * 4 + b % 4
        self.start(self.at(a, b), self.s5.at[k], self.r5.at[k], seq_at(y, x, 1 - c))

    def send_part(self, a, b, part, side, sems, nbr):
        ssem, rsem = sems
        self.start(self.at(a, b, part), ssem.at[side, part], rsem.at[side, part], nbr(1 - 2 * side))

    def first_sends(self, a, b, sems, nbr):
        self.send_part(a, b, 0, 0, sems, nbr)
        self.send_part(a, b, 1, 1, sems, nbr)
        self.send_part(a, b, 1, 0, sems, nbr)
        self.send_part(a, b, 0, 1, sems, nbr)

    def b_sends(self, a):
        k = a % 4
        self.first_sends(a, 0, (self.s3.at[k], self.r3.at[k]), self.nbr_b)

    def b_relay(self, a):
        k = a % 4
        self.got(self.at(a, -1, 0), self.r3.at[k, 0, 0])
        self.start(self.at(a, -1, 0), self.s4.at[k, 0], self.r4.at[k, 0], self.nbr_b(1))
        self.got(self.at(a, 1, 1), self.r3.at[k, 1, 1])
        self.start(self.at(a, 1, 1), self.s4.at[k, 1], self.r4.at[k, 1], self.nbr_b(-1))

    def b_rest(self, a):
        k = a % 4
        self.got(self.at(a, -1, 1), self.r3.at[k, 0, 1])
        self.to_twin(a, -1)
        self.got(self.at(a, 1, 0), self.r3.at[k, 1, 0])
        self.to_twin(a, 1)

    def step0(self):
        s, z, _, _, _ = place()
        mine = self.full.at[2 * s + z // 2, pl.ds(pl.multiple_of((z % 2) * 32, 32), 32)]
        self.local = pltpu.make_async_copy(self.cache_ref, mine, self.lsem)
        self.local.start()
        self.zc = [
            rcopy(self.cache_ref, mine, self.zs.at[d - 1], self.zr.at[d - 1], s, (z + d) % 4) for d in (1, 2, 3)
        ]
        for q in self.zc:
            q.start()
        self.pend += self.zc

    def step1(self):
        self.local.wait()
        for q in self.zc:
            q.wait_recv()
        self.first_sends(0, 0, (self.s1, self.r1), self.nbr_a)
        self.b_sends(0)
        self.to_twin(0, 0)

    def step2(self):
        self.got(self.at(-1, 0, 0), self.r1.at[0, 0])
        self.start(self.at(-1, 0, 0), self.s2.at[0], self.r2.at[0], self.nbr_a(1))
        self.got(self.at(1, 0, 1), self.r1.at[1, 1])
        self.start(self.at(1, 0, 1), self.s2.at[1], self.r2.at[1], self.nbr_a(-1))
        self.got(self.at(-1, 0, 1), self.r1.at[0, 1])
        self.got(self.at(1, 0, 0), self.r1.at[1, 0])
        self.b_sends(-1)
        self.b_sends(1)
        self.to_twin(-1, 0)
        self.to_twin(1, 0)

    def step3(self):
        self.b_relay(0)
        self.got(self.at(2, 0, 0), self.r2.at[0])
        self.got(self.at(2, 0, 1), self.r2.at[1])
        self.b_sends(2)
        self.b_rest(0)
        self.to_twin(2, 0)

    def step4(self):
        for a in (-1, 1):
            self.b_relay(a)

    def step5(self):
        for a in (-1, 1):
            self.b_rest(a)
        self.b_relay(2)

    def step6(self):
        self.b_rest(2)
        for a in (0, -1, 1, 2):
            k = a % 4
            self.got(self.at(a, 2, 0), self.r4.at[k, 0])
            self.got(self.at(a, 2, 1), self.r4.at[k, 1])
            self.to_twin(a, 2)

    def step7(self):
        _, _, c, x, y = place()
        for a in range(4):
            for b in range(4):
                t = seq_at((y + a * (1 - c) + b * c) % 4, (x + a * c + b * (1 - c)) % 4, 1 - c)
                self.got(self.block(t, None), self.r5.at[a * 4 + b])
        for q in self.pend:
            q.wait_send()


GATHER_SCRATCH = [pltpu.VMEM((64, BLK, KV), BF), pltpu.SemaphoreType.DMA] + [
    pltpu.SemaphoreType.DMA(shape)
    for shape in ((3,), (3,), (2, 2), (2, 2), (2,), (2,), (4, 2, 2), (4, 2, 2), (4, 2), (4, 2), (16,), (16,))
]


def cache_stages(inv, flag, gk, gc, zr1, zr2, rz, send, recv, part, zss, zrs, xss, xrs, fss, frs):
    s, z, c, x, y = place()
    z1, z2, z3 = (z + 1) % 4, (z + 2) % 4, (z + 3) % 4

    def quarter(b, n, q):
        return gk.at[pl.ds(b, n), pl.ds(pl.multiple_of(q * 16, 16), 16)]

    def first(u):
        b = 8 * u
        return [
            rcopy(quarter(b, 4, z2), zr1.at[u, 0], zss.at[u, 0, 0], zrs.at[u, 0, 0], s, z1),
            rcopy(quarter(b + 4, 4, z2), zr1.at[u, 1], zss.at[u, 0, 1], zrs.at[u, 0, 1], s, z3),
        ]

    def second(u):
        b = 8 * u
        return [
            rcopy(quarter(b, 8, z1), zr2.at[u, 0], zss.at[u, 1, 0], zrs.at[u, 1, 0], s, z1),
            rcopy(quarter(b, 8, z3), zr2.at[u, 1], zss.at[u, 1, 1], zrs.at[u, 1, 1], s, z3),
        ]

    def head_send(u):
        for q in first(u):
            q.start()

    def head_relay(u):
        b = 8 * u
        for q in first(u):
            q.wait()
        for r, b0, q in ((zr1.at[u, 0], b, z1), (zr1.at[u, 1], b + 4, z3)):
            t = quarter(b0, 4, q)
            t[...] = (t[...].astype(F32) + r[...].astype(F32)).astype(BF)
        for q in second(u):
            q.start()

    def head_sum(u):
        for q in second(u):
            q.wait()
        t = quarter(8 * u, 8, z)[...].astype(F32) + zr2[u, 0].astype(F32) + zr2[u, 1].astype(F32)
        rz[u // 2, 8 * (u % 2) : 8 * (u % 2) + 8] = t.astype(BF)
        if u % 2:
            rz[u // 2, 16] = jnp.zeros((16, KV), BF)

    def spread():
        for d in range(32):
            t = (s + d) % 32
            v = rz[0, inv[0, t]].astype(F32) + rz[1, inv[1, t]].astype(F32)
            mark = jnp.zeros((16, KP - KV), F32) + flag[t].astype(F32)
            send[d] = jnp.concatenate([v, mark], 1).astype(BF)
            if d:
                rcopy(send.at[d], recv.at[d], xss.at[d], xrs.at[d], t, z).start()

    def collect():
        a = jnp.zeros((16, KV), F32)
        b = jnp.zeros((16, KV), F32)
        for d in range(32):
            if d:
                rcopy(send.at[d], recv.at[d], xss.at[d], xrs.at[d], (s + d) % 32, z).wait()
                v = recv[d].astype(F32)
            else:
                v = send[0].astype(F32)
            v, mark = v[:, :KV], v[:, KV : KV + 1]
            second_part = v * mark
            b = b + second_part
            a = a + (v - second_part)
        part[0, 0] = a + rz[0, 0].astype(F32)
        part[0, 1] = b + rz[1, 0].astype(F32)
        for d in (1, 2, 3):
            rcopy(part.at[0], part.at[d], fss.at[d - 1], frs.at[d - 1], s, (z + d) % 4).start()

    def finish():
        for d in (1, 2, 3):
            rcopy(part.at[0], part.at[d], fss.at[d - 1], frs.at[d - 1], s, (z + d) % 4).wait()
        q = 2 * (z % 2)
        gc[0:16] = part[(z - q + 4) % 4, z // 2]
        gc[16:32] = part[(z - q + 3) % 4, z // 2]

    return head_send, head_relay, head_sum, spread, collect, finish


CACHE_SCRATCH = [
    pltpu.VMEM((4, 2, 4, 16, KV), BF),
    pltpu.VMEM((4, 2, 8, 16, KV), BF),
    pltpu.VMEM((2, 17, 16, KV), BF),
    pltpu.VMEM((32, 16, KP), BF),
    pltpu.VMEM((32, 16, KP), BF),
    pltpu.VMEM((4, 2, 16, KV), F32),
    pltpu.SemaphoreType.DMA((4, 2, 2)),
    pltpu.SemaphoreType.DMA((4, 2, 2)),
    pltpu.SemaphoreType.DMA((32,)),
    pltpu.SemaphoreType.DMA((32,)),
    pltpu.SemaphoreType.DMA((3,)),
    pltpu.SemaphoreType.DMA((3,)),
]

PHASES = [("fwd", 8, 2.3), ("ds0", 2, 1.3), ("kv0", 4, 1.3), ("ds1", 2, 1.3), ("kv1", 4, 1.3), ("dq", 4, 1.5)]
UV_GAPS = [0.0, 2.6, 2.4, 3.4, 1.8, 2.0, 2.0, 1.8, 3.4, 2.4, 2.6]
HEAD_GAPS = [3.0, 4.0]
END_GAPS = [0.1, 10.0, 2.5]


def plan():
    ends, now = [], 0.0
    for name, n, us in PHASES:
        for i in range(n):
            now += us
            ends.append((now, name, i))
    when = {(name, i): t for t, name, i in ends}
    todo = []
    for k in range(NCH):
        t = when["fwd", 8 // NCH * (k + 1) - 1]
        for st in range(11):
            t += UV_GAPS[st]
            todo.append((t, "uv", (k, st)))
    for u in range(4):
        t = when["kv%d" % (u // 2), 2 * (u % 2) + 1]
        todo.append((t, "head_send", (u,)))
        todo.append((t + HEAD_GAPS[0], "head_relay", (u,)))
        t += sum(HEAD_GAPS)
        todo.append((t, "head_sum", (u,)))
    for op, gap in zip(("spread", "collect", "finish"), END_GAPS):
        t += gap
        todo.append((t, op, ()))
    todo.sort(key=lambda e: e[0])
    at, late = {}, []
    for t, op, arg in todo:
        for end, name, i in ends:
            if end >= t - 1e-6:
                at.setdefault((name, i), []).append((op, arg))
                break
        else:
            late.append((op, arg))
    return at, late


def fused_body(lists, cache, qt, w_hbm, gout_hbm, ho_hbm, dq_hbm, uv_hbm, gc, *scr):
    (qg, k, kt, mask, pt, do, cen, ot, sa, sb, u, w, gout, hb, qb, inv, flag,
     lsem, hsem, qsem, osem) = scr[:21]
    scr = scr[21:]
    gat = Gather(cache, *scr[: len(GATHER_SCRATCH)])
    full = gat.full
    scr = scr[len(GATHER_SCRATCH) :]
    stage = uv_stages(u, u, *scr[: len(UV_SCRATCH)])
    gk = full
    cs = cache_stages(inv, flag, gk, gc, *scr[len(UV_SCRATCH) :])
    head_send, head_relay, head_sum, spread, collect, finish = cs
    s, z, c, x, y = place()

    barrier = pltpu.get_barrier_semaphore()
    for d in range(1, 32):
        pl.semaphore_signal(barrier, inc=1, device_id=((s + d) % 32, z), device_id_type=MESH)
    for d in range(1, 4):
        pl.semaphore_signal(barrier, inc=1, device_id=(s, (z + d) % 4), device_id_type=MESH)

    def q_load(i, slot):
        return pltpu.make_async_copy(qt.at[pl.ds(8 * i, 8)], qb.at[slot], qsem.at[slot])

    g_load = pltpu.make_async_copy(gout_hbm, u.at[0], lsem.at[1])
    w_load = pltpu.make_async_copy(w_hbm, w, lsem.at[0])
    g_load.start()
    q_load(0, 0).start()
    q_load(1, 1).start()
    w_load.start()

    r = lax.broadcasted_iota(jnp.int32, (BLK, WIDE), 0)
    cc = lax.broadcasted_iota(jnp.int32, (BLK, WIDE), 1)
    mask[...] = jnp.where(r <= (cc % BLK), 0.0, NEG).astype(F32)
    row = lax.broadcasted_iota(jnp.int32, (64, ROWS), 0)
    one = jnp.where(row == 0, 1.0, 0.0).astype(BF)
    qg[0, KV:, :] = one
    qg[1, KV:, :] = one
    pl.semaphore_wait(barrier, 34)
    gat.step0()

    def find(t, _):
        which = jnp.int32(0)
        for g in range(2):
            slot = jnp.int32(16)
            for j in range(KEEP):
                d = lists[g, j] - 2 * t
                hit = (d >= 0) & (d < 2)
                slot = jnp.where(hit, j + 1, slot)
                which = jnp.where(hit, d, which)
            inv[g, t] = slot
        flag[t] = which
        return 0

    g_load.wait()

    def turn(i, _):
        t = pl.ds(pl.multiple_of(i * 16, 16), 16)
        x = u[0, pl.ds(pl.multiple_of(i * 512, 512), 512)].reshape(16, NH, VH)
        gout[:, t, :] = jnp.swapaxes(x, 0, 1)
        return 0

    lax.fori_loop(0, TD // 16, turn, 0)
    lax.fori_loop(0, 32, find, 0)
    gat.step1()

    def prep_q(lo, hi):
        def body(i, _):
            q_load(i, i % 2).wait()
            for p in range(4):
                a, b = halves(qb[i % 2, 2 * p], qb[i % 2, 2 * p + 1])
                col = pl.ds(pl.multiple_of(i * WIDE + p * 128, 128), 128)
                qg[0, :KV, col] = a
                qg[1, :KV, col] = b

            @pl.when(i + 2 < 4)
            def _():
                q_load(i + 2, i % 2).start()

            return 0

        lax.fori_loop(lo, hi, body, 0)

    def prep_do(lo, hi):
        def body(i, _):
            for p in range(4):
                h = 8 * i + 2 * p
                d0 = lax.dot_general(w[h], gout[h], NTD, preferred_element_type=F32).astype(BF)
                d1 = lax.dot_general(w[h + 1], gout[h + 1], NTD, preferred_element_type=F32).astype(BF)
                a, b = halves(d0, d1)
                col = pl.ds(pl.multiple_of(i * WIDE + p * 128, 128), 128)
                do[0, :, col] = a
                do[1, :, col] = b
            return 0

        lax.fori_loop(lo, hi, body, 0)

    prep_q(0, 2)
    gat.step2()
    prep_q(2, 3)
    gat.step3()
    prep_q(3, 4)
    gat.step4()
    w_load.wait()
    prep_do(0, 2)
    gat.step5()
    prep_do(2, 4)
    gat.step6()
    gat.step7()

    colid = lax.broadcasted_iota(jnp.int32, (BLK, KP - DL), 1)
    for g in range(2):
        for j in range(SLOTS):
            if j == 0:
                blk = full[2 * s + g]
                bias = jnp.float32(0.0)
            else:
                e = lists[g, j - 1]
                blk = full[jnp.maximum(e, 0)]
                bias = jnp.where(e >= 0, 0.0, NEG).astype(F32)
            k[g, j * BLK : (j + 1) * BLK, :DL] = blk[:, :DL]
            rot = jnp.concatenate([blk[:, DL:].astype(F32), jnp.zeros((BLK, 64), F32)], 1)
            k[g, j * BLK : (j + 1) * BLK, DL:] = jnp.where(colid == 64, bias, rot).astype(BF)
        for b in range(8):
            t = jnp.swapaxes(k[g, b * 128 : (b + 1) * 128, :], 0, 1)
            kt[g, :, b * 128 : (b + 1) * 128] = t[:KV]

    uv_out = [pltpu.make_async_copy(u.at[q], uv_hbm.at[q], osem.at[q]) for q in range(NCH)]

    def run(op, arg):
        if op == "uv":
            stage(*arg)
            if arg[1] == 10:
                uv_out[arg[0]].start()
        else:
            ops = {"head_send": head_send, "head_relay": head_relay, "head_sum": head_sum}
            ops.update({"spread": spread, "collect": collect, "finish": finish})
            ops[op](*arg)

    at, late = plan()
    steps = {p[0]: p[1] for p in PHASES}

    def hook(name, i, part=0, parts=1):
        for j in range(part, steps[name], parts):
            if (name, j) in at:

                @pl.when(i == j // parts)
                def _():
                    for op, arg in at[name, j]:
                        run(op, arg)

    def loop(name, body, parts=1):
        def step(i, _):
            body(i)
            hook(name, i, parts - 1, parts)
            return 0

        lax.fori_loop(0, steps[name] // parts, step, 0)

    def cols(i, n=WIDE):
        return pl.ds(pl.multiple_of(i * n, n), n)

    def ho_store(i, slot):
        return pltpu.make_async_copy(hb.at[slot], ho_hbm.at[pl.ds(8 * i, 8)], hsem.at[slot])

    def scores(to, g, i):
        to[...] = jnp.dot(k[g], qg[g, :, cols(i)], preferred_element_type=F32)

    def softmax(sc, g, col):
        sc[:BLK] = sc[:BLK] + mask[...]
        m = jnp.max(sc[...], axis=0, keepdims=True)
        total = jnp.zeros((8, WIDE), F32)
        for b in range(16):
            e = jnp.exp2((sc[b * 64 : (b + 1) * 64] - m) * (SC * L2E))
            total = total + jnp.sum(e.reshape(8, 8, WIDE), axis=0)
            pt[g, b * 64 : (b + 1) * 64, col] = e.astype(BF)
        return 1.0 / jnp.sum(total, axis=0, keepdims=True)

    def values(g, col, inv_l):
        o = jnp.dot(kt[g, :DL, :], pt[g, :, col], preferred_element_type=F32) * inv_l
        ot[g] = o.astype(BF)
        dn = (do[g, :, col].astype(F32) * inv_l).astype(BF)
        do[g, :, col] = dn
        centre = jnp.sum(o * dn.astype(F32), axis=0, keepdims=True)
        cen[g, :, col] = jnp.broadcast_to(centre, (8, WIDE))

    scores(sa, 0, 0)

    def fwd(i):
        col = cols(i)
        scores(sb, 1, i)
        values(0, col, softmax(sa, 0, col))
        hook("fwd", i, 0, 2)
        scores(sa, 0, jnp.minimum(i + 1, 3))
        values(1, col, softmax(sb, 1, col))

        @pl.when(i >= 2)
        def _():
            ho_store(i - 2, i % 2).wait()

        for p in range(4):
            hh = halves(ot[0, :, p * 128 : (p + 1) * 128], ot[1, :, p * 128 : (p + 1) * 128])
            for q in range(2):
                h = 2 * p + q
                part = jnp.dot(hh[q], gout[8 * i + h], preferred_element_type=F32).astype(BF)
                u[i, h * DL : (h + 1) * DL] = part
                hb[i % 2, h] = lax.dot_general(hh[q], w[8 * i + h], TND, preferred_element_type=F32).astype(BF)
        ho_store(i, i % 2).start()

    loop("fwd", fwd, 2)
    ho_store(2, 0).wait()
    ho_store(3, 1).wait()

    def back_ds(g, to):
        def body(i):
            for b, tmp in enumerate((sa, sb)):
                col = cols(2 * i + b)
                tmp[...] = jnp.dot(k[g, :, :DL], do[g, :, col], preferred_element_type=F32)
            for b, tmp in enumerate((sa, sb)):
                col = cols(2 * i + b)
                for q in range(8):
                    rows = slice(q * 128, (q + 1) * 128)
                    t = pt[g, rows, col].astype(F32) * (tmp[rows] - cen[g, 0:1, col])
                    pt[to, rows, col] = t.astype(BF)

        return body

    def back_kv(g, d):
        def body(i):
            rows = cols(i)
            sa[:KV] = lax.dot_general(qg[g, :KV, :], pt[d, rows, :], NTD, preferred_element_type=F32)
            hook("kv%d" % g, i, 0, 2)
            sb[:DL] = lax.dot_general(do[g], pt[g, rows, :], NTD, preferred_element_type=F32)
            zero = jnp.zeros((KP - KV, WIDE), F32)
            t = jnp.concatenate([sa[:DL] * SC + sb[:DL], sa[DL:KV] * SC, zero], 0).astype(BF)
            t = jnp.swapaxes(t, 0, 1)
            gk[pl.ds(16 * g + 8 * i, 8)] = t[:, :KV].reshape(8, BLK, KV)

        return body

    loop("ds0", back_ds(0, 2))
    loop("kv0", back_kv(0, 2), 2)
    loop("ds1", back_ds(1, 0))
    loop("kv1", back_kv(1, 0), 2)

    def dq_store(i, slot):
        return pltpu.make_async_copy(qb.at[slot], dq_hbm.at[pl.ds(8 * i, 8)], qsem.at[slot])

    def back_q(i):
        col = cols(i)

        @pl.when(i >= 2)
        def _():
            dq_store(i - 2, i % 2).wait()

        r = []
        for g, d in ((0, 2), (1, 0)):
            r.append((jnp.dot(kt[g], pt[d, :, col], preferred_element_type=F32) * SC).astype(BF))
        for p in range(4):
            a, b = halves(r[0][:, p * 128 : (p + 1) * 128], r[1][:, p * 128 : (p + 1) * 128])
            qb[i % 2, 2 * p] = a
            qb[i % 2, 2 * p + 1] = b
        dq_store(i, i % 2).start()

    loop("dq", back_q)
    for op, arg in late:
        run(op, arg)
    dq_store(2, 0).wait()
    dq_store(3, 1).wait()
    for q in uv_out:
        q.wait()


def attention(lists, cache, qt, w, gout):
    v = pl.BlockSpec(memory_space=pltpu.VMEM)
    m = pl.BlockSpec(memory_space=pltpu.SMEM)
    a = pl.BlockSpec(memory_space=pl.ANY)
    scratch = [
        pltpu.VMEM((2, KP, ROWS), BF),
        pltpu.VMEM((2, KEYS, KP), BF),
        pltpu.VMEM((2, KV, KEYS), BF),
        pltpu.VMEM((BLK, WIDE), F32),
        pltpu.VMEM((3, KEYS, ROWS), BF),
        pltpu.VMEM((2, DL, ROWS), BF),
        pltpu.VMEM((2, 8, ROWS), F32),
        pltpu.VMEM((2, DL, WIDE), BF),
        pltpu.VMEM((KEYS, WIDE), F32),
        pltpu.VMEM((KEYS, WIDE), F32),
        pltpu.VMEM((NCH, CROWS, 128), BF),
        pltpu.VMEM((NH, DL, VH), BF),
        pltpu.VMEM((NH, TD, VH), BF),
        pltpu.VMEM((2, 8, TD, VH), BF),
        pltpu.VMEM((2, 8, KV, TD), BF),
        pltpu.SMEM((2, 32), jnp.int32),
        pltpu.SMEM((32,), jnp.int32),
        pltpu.SemaphoreType.DMA((2,)),
        pltpu.SemaphoreType.DMA((2,)),
        pltpu.SemaphoreType.DMA((2,)),
        pltpu.SemaphoreType.DMA((NCH,)),
    ]
    return pl.pallas_call(
        fused_body,
        out_shape=(
            jax.ShapeDtypeStruct((NH, TD, VH), BF),
            jax.ShapeDtypeStruct((NH, KV, TD), BF),
            jax.ShapeDtypeStruct((NCH, CROWS, 128), BF),
            jax.ShapeDtypeStruct((32, KV), F32),
        ),
        in_specs=[m, v, a, a, a],
        out_specs=(a, a, a, v),
        scratch_shapes=scratch + GATHER_SCRATCH + UV_SCRATCH + CACHE_SCRATCH,
        compiler_params=pltpu.CompilerParams(
            collective_id=0, has_side_effects=True, vmem_limit_bytes=VMEM_LIMIT
        ),
        name="latent_attention",
    )(lists, cache, qt, w, gout)


def on_device(queries, cache, lists, w_uv, grad_out):
    ho, dq, uv, gc = attention(
        lists, cache, queries.transpose(1, 2, 0), w_uv, grad_out.reshape(TD * NH, VH)
    )
    return ho.transpose(1, 0, 2), dq.transpose(2, 0, 1), gc, uv.reshape(NH, DL, VH)


def solution(mesh):
    return jax.shard_map(
        on_device,
        mesh=mesh,
        in_specs=(
            P("seq", "head", None),
            P(("seq", "head"), None),
            P("seq", None),
            P("head", None, None),
            P("seq", "head", None),
        ),
        out_specs=(
            P("seq", "head", None),
            P("seq", "head", None),
            P(("seq", "head"), None),
            P("head", None, None),
        ),
        check_vma=False,
    )
```

```python
import functools, jax, jax.numpy as jnp, numpy as np
from jax import lax
from jax.experimental import pallas as pl
from jax.experimental.pallas import tpu as pltpu
from jax.sharding import PartitionSpec as P

BLK=64; KEEP=15; SLOTS=16; KEYS=1024; DL=512; KV=576; KP=640; NH=32; VH=128; TD=128
ROWS=2048; TILE=256; NT=8
SC=192.0**-0.5
L2E=1.4426950408889634
NEG=-1e30
F32=jnp.float32; BF=jnp.bfloat16
NTD=(((1,),(1,)),((),()))
TND=(((0,),(0,)),((),()))

def halves(a,b):
    return (jnp.concatenate([a[:, :64], b[:, :64]],1), jnp.concatenate([a[:, 64:], b[:, 64:]],1))

def make_mask(mask_ref):
    r=lax.broadcasted_iota(jnp.int32,(BLK,TILE),0)
    c=lax.broadcasted_iota(jnp.int32,(BLK,TILE),1)
    mask_ref[...]=jnp.where(r<=(c%BLK),0.0,NEG).astype(F32)

MESH = pl.DeviceIdType.MESH
NCH = 4
CROWS = NH * DL // NCH
CH = CROWS // 2
QA = CH // 4
QB = QA // 4


def place():
    s = lax.axis_index("seq")
    z = lax.axis_index("head")
    return s, z, s % 2, (s // 2) % 4, s // 8


def seq_at(y, x, c):
    return (y * 4 + x) * 2 + c


def rcopy(src, dst, ssem, rsem, s, z):
    return pltpu.make_async_remote_copy(
        src_ref=src, dst_ref=dst, send_sem=ssem, recv_sem=rsem, device_id=(s, z), device_id_type=MESH
    )


def greet(seq_steps, head_steps):
    s, z, _, _, _ = place()
    barrier = pltpu.get_barrier_semaphore()
    for d in seq_steps:
        pl.semaphore_signal(barrier, inc=1, device_id=((s + d) % 32, z), device_id_type=MESH)
    for d in head_steps:
        pl.semaphore_signal(barrier, inc=1, device_id=(s, (z + d) % 4), device_id_type=MESH)
    pl.semaphore_wait(barrier, len(seq_steps) + len(head_steps))


def uv_stages(u, rc, ra, rb, ri, ss, rs):
    s, z, c, x, y = place()
    twin = seq_at(y, x, 1 - c)
    pa = x * (1 - c) + y * c
    pb = y * (1 - c) + x * c
    base = c * CH

    def nbr_a(d):
        return seq_at((y + d * c) % 4, (x + d * (1 - c)) % 4, c)

    def nbr_b(d):
        return seq_at((y + d * (1 - c)) % 4, (x + d * c) % 4, c)

    def ds(start, size):
        return pl.ds(pl.multiple_of(start, size), size)

    def add(terms):
        t = terms[0][...].astype(F32)
        for r in terms[1:]:
            t = t + r[...].astype(F32)
        return t.astype(BF)

    def quarter_a(k, q):
        return u.at[k, ds(base + q % 4 * QA, QA)]

    def quarter_b(k, q):
        return u.at[k, ds(base + pa * QA + q % 4 * QB, QB)]

    def half(k, h):
        return u.at[k, ds(h * CH, CH)]

    def copies(k, st):
        if st == 0:
            return [(half(k, 1 - c), rc.at[k], twin)]
        if st == 1:
            return [(rc.at[k, ds((pa + d) % 4 * QA, QA)], ra.at[k, d - 1], nbr_a(d)) for d in (1, 2, 3)]
        if st == 2:
            return [(rb.at[k, ds((pb + d) % 4 * QB, QB)], ri.at[k, d - 1], nbr_b(d)) for d in (1, 2, 3)]
        if st == 3:
            return [(quarter_b(k, pb), quarter_b(k, pb), nbr_b(d)) for d in (1, 2, 3)]
        if st == 4:
            return [(quarter_a(k, pa), quarter_a(k, pa), nbr_a(d)) for d in (1, 2, 3)]
        return [(half(k, c), half(k, c), twin)]

    def landed(k, st):
        if st == 3:
            return [quarter_b(k, pb + 4 - d) for d in (1, 2, 3)]
        if st == 4:
            return [quarter_a(k, pa + 4 - d) for d in (1, 2, 3)]
        if st == 5:
            return [half(k, 1 - c)]
        return [q[1] for q in copies(k, st)]

    def stage(k, st):
        if st > 0:
            for i, dst in enumerate(landed(k, st - 1)):
                rcopy(dst, dst, ss.at[k, st - 1, i], rs.at[k, st - 1, i], twin, z).wait_recv()
            for i, (src, dst, to) in enumerate(copies(k, st - 1)):
                rcopy(src, dst, ss.at[k, st - 1, i], rs.at[k, st - 1, i], to, z).wait_send()
        if st == 1:
            rc[k] = add([half(k, c), rc.at[k]])
        elif st == 2:
            rb[k] = add([rc.at[k, ds(pa * QA, QA)]] + [ra.at[k, d] for d in range(3)])
        elif st == 3:
            quarter_b(k, pb)[...] = add([rb.at[k, ds(pb * QB, QB)]] + [ri.at[k, d] for d in range(3)])
        if st < UV_STAGES - 1:
            for i, (src, dst, to) in enumerate(copies(k, st)):
                rcopy(src, dst, ss.at[k, st, i], rs.at[k, st, i], to, z).start()

    return stage


UV_STAGES = 7
UV_SCRATCH = [
    pltpu.VMEM((NCH, CH, 128), BF),
    pltpu.VMEM((NCH, 3, QA, 128), BF),
    pltpu.VMEM((NCH, QA, 128), BF),
    pltpu.VMEM((NCH, 3, QB, 128), BF),
    pltpu.SemaphoreType.DMA((NCH, UV_STAGES - 1, 3)),
    pltpu.SemaphoreType.DMA((NCH, UV_STAGES - 1, 3)),
]


VMEM_LIMIT = 63 * 2**20
WIDE = 512


class Gather:
    def __init__(self, cache_ref, full, lsem, zs, zr, s1, r1, s2, r2, s3, r3, s4, r4, s5, r5):
        self.__dict__.update(locals())
        self.pend = []

    def at(self, a, b, part=None):
        _, _, c, x, y = place()
        t = seq_at((y + a * c + b * (1 - c)) % 4, (x + a * (1 - c) + b * c) % 4, c)
        return self.block(t, part)

    def block(self, t, part):
        if part is None:
            return self.full.at[pl.ds(2 * t, 2)]
        return self.full.at[2 * t + part]

    def nbr_a(self, d):
        _, _, c, x, y = place()
        return seq_at((y + d * c) % 4, (x + d * (1 - c)) % 4, c)

    def nbr_b(self, d):
        _, _, c, x, y = place()
        return seq_at((y + d * (1 - c)) % 4, (x + d * c) % 4, c)

    def start(self, src, ssem, rsem, dev):
        q = rcopy(src, src, ssem, rsem, dev, place()[1])
        q.start()
        self.pend.append(q)

    def got(self, dst, rsem):
        s, z, _, _, _ = place()
        rcopy(dst, dst, self.s5.at[0], rsem, s, (z + 1) % 4).wait_recv()

    def to_twin(self, a, b):
        _, _, c, x, y = place()
        k = (a % 4) * 4 + b % 4
        self.start(self.at(a, b), self.s5.at[k], self.r5.at[k], seq_at(y, x, 1 - c))

    def send_part(self, a, b, part, side, sems, nbr):
        ssem, rsem = sems
        self.start(self.at(a, b, part), ssem.at[side, part], rsem.at[side, part], nbr(1 - 2 * side))

    def first_sends(self, a, b, sems, nbr):
        self.send_part(a, b, 0, 0, sems, nbr)
        self.send_part(a, b, 1, 1, sems, nbr)
        self.send_part(a, b, 1, 0, sems, nbr)
        self.send_part(a, b, 0, 1, sems, nbr)

    def b_sends(self, a):
        k = a % 4
        self.first_sends(a, 0, (self.s3.at[k], self.r3.at[k]), self.nbr_b)

    def b_relay(self, a):
        k = a % 4
        self.got(self.at(a, -1, 0), self.r3.at[k, 0, 0])
        self.start(self.at(a, -1, 0), self.s4.at[k, 0], self.r4.at[k, 0], self.nbr_b(1))
        self.got(self.at(a, 1, 1), self.r3.at[k, 1, 1])
        self.start(self.at(a, 1, 1), self.s4.at[k, 1], self.r4.at[k, 1], self.nbr_b(-1))

    def b_rest(self, a):
        k = a % 4
        self.got(self.at(a, -1, 1), self.r3.at[k, 0, 1])
        self.to_twin(a, -1)
        self.got(self.at(a, 1, 0), self.r3.at[k, 1, 0])
        self.to_twin(a, 1)

    def step0(self):
        s, z, _, _, _ = place()
        mine = self.full.at[2 * s + z // 2, pl.ds(pl.multiple_of((z % 2) * 32, 32), 32)]
        self.local = pltpu.make_async_copy(self.cache_ref, mine, self.lsem)
        self.local.start()
        self.zc = [
            rcopy(self.cache_ref, mine, self.zs.at[d - 1], self.zr.at[d - 1], s, (z + d) % 4) for d in (1, 2, 3)
        ]
        for q in self.zc:
            q.start()
        self.pend += self.zc

    def step1(self):
        self.local.wait()
        for q in self.zc:
            q.wait_recv()
        self.first_sends(0, 0, (self.s1, self.r1), self.nbr_a)
        self.b_sends(0)
        self.to_twin(0, 0)

    def step2(self):
        self.got(self.at(-1, 0, 0), self.r1.at[0, 0])
        self.start(self.at(-1, 0, 0), self.s2.at[0], self.r2.at[0], self.nbr_a(1))
        self.got(self.at(1, 0, 1), self.r1.at[1, 1])
        self.start(self.at(1, 0, 1), self.s2.at[1], self.r2.at[1], self.nbr_a(-1))
        self.got(self.at(-1, 0, 1), self.r1.at[0, 1])
        self.got(self.at(1, 0, 0), self.r1.at[1, 0])
        self.b_sends(-1)
        self.b_sends(1)
        self.to_twin(-1, 0)
        self.to_twin(1, 0)

    def step3(self):
        self.b_relay(0)
        self.got(self.at(2, 0, 0), self.r2.at[0])
        self.got(self.at(2, 0, 1), self.r2.at[1])
        self.b_sends(2)
        self.b_rest(0)
        self.to_twin(2, 0)

    def step4(self):
        for a in (-1, 1):
            self.b_relay(a)

    def step5(self):
        for a in (-1, 1):
            self.b_rest(a)
        self.b_relay(2)

    def step6(self):
        self.b_rest(2)
        for a in (0, -1, 1, 2):
            k = a % 4
            self.got(self.at(a, 2, 0), self.r4.at[k, 0])
            self.got(self.at(a, 2, 1), self.r4.at[k, 1])
            self.to_twin(a, 2)

    def step7(self):
        _, _, c, x, y = place()
        for a in range(4):
            for b in range(4):
                t = seq_at((y + a * (1 - c) + b * c) % 4, (x + a * c + b * (1 - c)) % 4, 1 - c)
                self.got(self.block(t, None), self.r5.at[a * 4 + b])
        for q in self.pend:
            q.wait_send()


GATHER_SCRATCH = [pltpu.VMEM((64, BLK, KV), BF), pltpu.SemaphoreType.DMA] + [
    pltpu.SemaphoreType.DMA(shape)
    for shape in ((3,), (3,), (2, 2), (2, 2), (2,), (2,), (4, 2, 2), (4, 2, 2), (4, 2), (4, 2), (16,), (16,))
]


def cache_stages(inv, flag, gk, gc, zr1, zr2, rz, send, recv, part, zss, zrs, xss, xrs, fss, frs):
    s, z, c, x, y = place()
    z1, z2, z3 = (z + 1) % 4, (z + 2) % 4, (z + 3) % 4

    def quarter(b, n, q):
        return gk.at[pl.ds(b, n), pl.ds(pl.multiple_of(q * 16, 16), 16)]

    def first(u):
        b = 8 * u
        return [
            rcopy(quarter(b, 4, z2), zr1.at[u, 0], zss.at[u, 0, 0], zrs.at[u, 0, 0], s, z1),
            rcopy(quarter(b + 4, 4, z2), zr1.at[u, 1], zss.at[u, 0, 1], zrs.at[u, 0, 1], s, z3),
        ]

    def second(u):
        b = 8 * u
        return [
            rcopy(quarter(b, 8, z1), zr2.at[u, 0], zss.at[u, 1, 0], zrs.at[u, 1, 0], s, z1),
            rcopy(quarter(b, 8, z3), zr2.at[u, 1], zss.at[u, 1, 1], zrs.at[u, 1, 1], s, z3),
        ]

    def head_send(u):
        for q in first(u):
            q.start()

    def head_relay(u):
        b = 8 * u
        for q in first(u):
            q.wait()
        for r, b0, q in ((zr1.at[u, 0], b, z1), (zr1.at[u, 1], b + 4, z3)):
            t = quarter(b0, 4, q)
            t[...] = (t[...].astype(F32) + r[...].astype(F32)).astype(BF)
        for q in second(u):
            q.start()

    def head_sum(u):
        for q in second(u):
            q.wait()
        t = quarter(8 * u, 8, z)[...].astype(F32) + zr2[u, 0].astype(F32) + zr2[u, 1].astype(F32)
        rz[u // 2, 8 * (u % 2) : 8 * (u % 2) + 8] = t.astype(BF)
        if u % 2:
            rz[u // 2, 16] = jnp.zeros((16, KV), BF)

    def packed(t):
        v = rz[0, inv[0, t]].astype(F32) + rz[1, inv[1, t]].astype(F32)
        mark = jnp.zeros((16, KP - KV), F32) + flag[t].astype(F32)
        return jnp.concatenate([v, mark], 1).astype(BF)

    def message(d):
        return rcopy(send.at[d], recv.at[d], xss.at[d], xrs.at[d], (s + d) % 32, z)

    def spread():
        send[0] = packed(s)

        def one(d, _):
            @pl.when(s + d >= 32)
            def _():
                send[d] = packed((s + d) % 32)
                message(d).start()

            return 0

        lax.fori_loop(1, 32, one, 0)

    def take(v):
        v = v.astype(F32)
        v, mark = v[:, :KV], v[:, KV : KV + 1]
        second_part = v * mark
        part[0, 0] = part[0, 0] + (v - second_part)
        part[0, 1] = part[0, 1] + second_part

    def collect():
        part[0, 0] = rz[0, 0].astype(F32)
        part[0, 1] = rz[1, 0].astype(F32)
        take(send[0])

        def one(d, _):
            @pl.when(d > s)
            def _():
                message(d).wait_recv()
                take(recv[d])

            @pl.when(s + d >= 32)
            def _():
                message(d).wait_send()

            return 0

        lax.fori_loop(1, 32, one, 0)
        for d in (1, 2, 3):
            rcopy(part.at[0], part.at[d], fss.at[d - 1], frs.at[d - 1], s, (z + d) % 4).start()

    def finish():
        for d in (1, 2, 3):
            rcopy(part.at[0], part.at[d], fss.at[d - 1], frs.at[d - 1], s, (z + d) % 4).wait()
        q = 2 * (z % 2)
        gc[0:16] = part[(z - q + 4) % 4, z // 2]
        gc[16:32] = part[(z - q + 3) % 4, z // 2]

    return head_send, head_relay, head_sum, spread, collect, finish


CACHE_SCRATCH = [
    pltpu.VMEM((4, 2, 4, 16, KV), BF),
    pltpu.VMEM((4, 2, 8, 16, KV), BF),
    pltpu.VMEM((2, 17, 16, KV), BF),
    pltpu.VMEM((32, 16, KP), BF),
    pltpu.VMEM((32, 16, KP), BF),
    pltpu.VMEM((4, 2, 16, KV), F32),
    pltpu.SemaphoreType.DMA((4, 2, 2)),
    pltpu.SemaphoreType.DMA((4, 2, 2)),
    pltpu.SemaphoreType.DMA((32,)),
    pltpu.SemaphoreType.DMA((32,)),
    pltpu.SemaphoreType.DMA((3,)),
    pltpu.SemaphoreType.DMA((3,)),
]

PHASES = [("fwd", 8, 2.3), ("ds0", 2, 1.3), ("kv0", 4, 1.3), ("ds1", 2, 1.3), ("kv1", 4, 1.3), ("dq", 4, 1.5)]
UV_GAPS = [0.0, 2.8, 4.6, 2.8, 2.8, 4.6, 2.8]
HEAD_GAPS = [3.0, 4.0]
END_GAPS = [0.1, 8.0, 2.5]


def plan():
    ends, now = [], 0.0
    for name, n, us in PHASES:
        for i in range(n):
            now += us
            ends.append((now, name, i))
    when = {(name, i): t for t, name, i in ends}
    todo = []
    for k in range(NCH):
        t = when["fwd", 8 // NCH * (k + 1) - 1]
        for st in range(UV_STAGES):
            t += UV_GAPS[st]
            todo.append((t, "uv", (k, st)))
    for u in range(4):
        t = when["kv%d" % (u // 2), 2 * (u % 2) + 1]
        todo.append((t, "head_send", (u,)))
        todo.append((t + HEAD_GAPS[0], "head_relay", (u,)))
        t += sum(HEAD_GAPS)
        todo.append((t, "head_sum", (u,)))
    for op, gap in zip(("spread", "collect", "finish"), END_GAPS):
        t += gap
        todo.append((t, op, ()))
    todo.sort(key=lambda e: e[0])
    at, late = {}, []
    for t, op, arg in todo:
        for end, name, i in ends:
            if end >= t - 1e-6:
                at.setdefault((name, i), []).append((op, arg))
                break
        else:
            late.append((op, arg))
    return at, late


def fused_body(lists, cache, qt, w_hbm, gout_hbm, ho_hbm, dq_hbm, uv_hbm, gc, *scr):
    (qg, k, kt, mask, pt, do, cen, ot, sa, sb, u, w, gout, hb, qb, inv, flag,
     lsem, hsem, qsem, osem) = scr[:21]
    scr = scr[21:]
    gat = Gather(cache, *scr[: len(GATHER_SCRATCH)])
    full = gat.full
    scr = scr[len(GATHER_SCRATCH) :]
    stage = uv_stages(u, *scr[: len(UV_SCRATCH)])
    gk = full
    cs = cache_stages(inv, flag, gk, gc, *scr[len(UV_SCRATCH) :])
    head_send, head_relay, head_sum, spread, collect, finish = cs
    s, z, c, x, y = place()

    barrier = pltpu.get_barrier_semaphore()
    for d in range(1, 32):
        pl.semaphore_signal(barrier, inc=1, device_id=((s + d) % 32, z), device_id_type=MESH)
    for d in range(1, 4):
        pl.semaphore_signal(barrier, inc=1, device_id=(s, (z + d) % 4), device_id_type=MESH)

    def q_load(i, slot):
        return pltpu.make_async_copy(qt.at[pl.ds(8 * i, 8)], qb.at[slot], qsem.at[slot])

    g_load = pltpu.make_async_copy(gout_hbm, u.at[0], lsem.at[1])
    w_load = pltpu.make_async_copy(w_hbm, w, lsem.at[0])
    g_load.start()
    q_load(0, 0).start()
    q_load(1, 1).start()
    w_load.start()

    r = lax.broadcasted_iota(jnp.int32, (BLK, WIDE), 0)
    cc = lax.broadcasted_iota(jnp.int32, (BLK, WIDE), 1)
    mask[...] = jnp.where(r <= (cc % BLK), 0.0, NEG).astype(F32)
    row = lax.broadcasted_iota(jnp.int32, (64, ROWS), 0)
    one = jnp.where(row == 0, 1.0, 0.0).astype(BF)
    qg[0, KV:, :] = one
    qg[1, KV:, :] = one
    pl.semaphore_wait(barrier, 34)
    gat.step0()

    def find(t, _):
        which = jnp.int32(0)
        for g in range(2):
            slot = jnp.int32(16)
            for j in range(KEEP):
                d = lists[g, j] - 2 * t
                hit = (d >= 0) & (d < 2)
                slot = jnp.where(hit, j + 1, slot)
                which = jnp.where(hit, d, which)
            inv[g, t] = slot
        flag[t] = which
        return 0

    g_load.wait()

    def turn(i, _):
        t = pl.ds(pl.multiple_of(i * 16, 16), 16)
        x = u[0, pl.ds(pl.multiple_of(i * 512, 512), 512)].reshape(16, NH, VH)
        gout[:, t, :] = jnp.swapaxes(x, 0, 1)
        return 0

    lax.fori_loop(0, TD // 16, turn, 0)
    lax.fori_loop(0, 32, find, 0)
    gat.step1()

    def prep_q(lo, hi):
        def body(i, _):
            q_load(i, i % 2).wait()
            for p in range(4):
                a, b = halves(qb[i % 2, 2 * p], qb[i % 2, 2 * p + 1])
                col = pl.ds(pl.multiple_of(i * WIDE + p * 128, 128), 128)
                qg[0, :KV, col] = a
                qg[1, :KV, col] = b

            @pl.when(i + 2 < 4)
            def _():
                q_load(i + 2, i % 2).start()

            return 0

        lax.fori_loop(lo, hi, body, 0)

    def prep_do(lo, hi):
        def body(i, _):
            for p in range(4):
                h = 8 * i + 2 * p
                d0 = lax.dot_general(w[h], gout[h], NTD, preferred_element_type=F32).astype(BF)
                d1 = lax.dot_general(w[h + 1], gout[h + 1], NTD, preferred_element_type=F32).astype(BF)
                a, b = halves(d0, d1)
                col = pl.ds(pl.multiple_of(i * WIDE + p * 128, 128), 128)
                do[0, :, col] = a
                do[1, :, col] = b
            return 0

        lax.fori_loop(lo, hi, body, 0)

    prep_q(0, 2)
    gat.step2()
    prep_q(2, 3)
    gat.step3()
    prep_q(3, 4)
    gat.step4()
    w_load.wait()
    prep_do(0, 2)
    gat.step5()
    prep_do(2, 4)
    gat.step6()
    gat.step7()

    colid = lax.broadcasted_iota(jnp.int32, (BLK, KP - DL), 1)
    for g in range(2):
        for j in range(SLOTS):
            if j == 0:
                blk = full[2 * s + g]
                bias = jnp.float32(0.0)
            else:
                e = lists[g, j - 1]
                blk = full[jnp.maximum(e, 0)]
                bias = jnp.where(e >= 0, 0.0, NEG).astype(F32)
            k[g, j * BLK : (j + 1) * BLK, :DL] = blk[:, :DL]
            rot = jnp.concatenate([blk[:, DL:].astype(F32), jnp.zeros((BLK, 64), F32)], 1)
            k[g, j * BLK : (j + 1) * BLK, DL:] = jnp.where(colid == 64, bias, rot).astype(BF)
        for b in range(8):
            t = jnp.swapaxes(k[g, b * 128 : (b + 1) * 128, :], 0, 1)
            kt[g, :, b * 128 : (b + 1) * 128] = t[:KV]

    uv_out = [pltpu.make_async_copy(u.at[q], uv_hbm.at[q], osem.at[q]) for q in range(NCH)]

    def run(op, arg):
        if op == "uv":
            stage(*arg)
            if arg[1] == UV_STAGES - 1:
                uv_out[arg[0]].start()
        else:
            ops = {"head_send": head_send, "head_relay": head_relay, "head_sum": head_sum}
            ops.update({"spread": spread, "collect": collect, "finish": finish})
            ops[op](*arg)

    at, late = plan()
    steps = {p[0]: p[1] for p in PHASES}

    def hook(name, i, part=0, parts=1):
        for j in range(part, steps[name], parts):
            if (name, j) in at:

                @pl.when(i == j // parts)
                def _():
                    for op, arg in at[name, j]:
                        run(op, arg)

    def loop(name, body, parts=1):
        def step(i, _):
            body(i)
            hook(name, i, parts - 1, parts)
            return 0

        lax.fori_loop(0, steps[name] // parts, step, 0)

    def cols(i, n=WIDE):
        return pl.ds(pl.multiple_of(i * n, n), n)

    def ho_store(i, slot):
        return pltpu.make_async_copy(hb.at[slot], ho_hbm.at[pl.ds(8 * i, 8)], hsem.at[slot])

    def scores(to, g, i):
        to[...] = jnp.dot(k[g], qg[g, :, cols(i)], preferred_element_type=F32)

    def softmax(sc, g, col):
        sc[:BLK] = sc[:BLK] + mask[...]
        m = jnp.max(sc[...], axis=0, keepdims=True)
        total = jnp.zeros((8, WIDE), F32)
        for b in range(16):
            e = jnp.exp2((sc[b * 64 : (b + 1) * 64] - m) * (SC * L2E))
            total = total + jnp.sum(e.reshape(8, 8, WIDE), axis=0)
            pt[g, b * 64 : (b + 1) * 64, col] = e.astype(BF)
        return 1.0 / jnp.sum(total, axis=0, keepdims=True)

    def values(g, col, inv_l):
        o = jnp.dot(kt[g, :DL, :], pt[g, :, col], preferred_element_type=F32) * inv_l
        ot[g] = o.astype(BF)
        dn = (do[g, :, col].astype(F32) * inv_l).astype(BF)
        do[g, :, col] = dn
        centre = jnp.sum(o * dn.astype(F32), axis=0, keepdims=True)
        cen[g, :, col] = jnp.broadcast_to(centre, (8, WIDE))

    scores(sa, 0, 0)

    def fwd(i):
        col = cols(i)
        scores(sb, 1, i)
        values(0, col, softmax(sa, 0, col))
        hook("fwd", i, 0, 2)
        scores(sa, 0, jnp.minimum(i + 1, 3))
        values(1, col, softmax(sb, 1, col))

        @pl.when(i >= 2)
        def _():
            ho_store(i - 2, i % 2).wait()

        for p in range(4):
            hh = halves(ot[0, :, p * 128 : (p + 1) * 128], ot[1, :, p * 128 : (p + 1) * 128])
            for q in range(2):
                h = 2 * p + q
                part = jnp.dot(hh[q], gout[8 * i + h], preferred_element_type=F32).astype(BF)
                u[i, h * DL : (h + 1) * DL] = part
                hb[i % 2, h] = lax.dot_general(hh[q], w[8 * i + h], TND, preferred_element_type=F32).astype(BF)
        ho_store(i, i % 2).start()

    loop("fwd", fwd, 2)
    ho_store(2, 0).wait()
    ho_store(3, 1).wait()

    def back_ds(g, to):
        def body(i):
            for b, tmp in enumerate((sa, sb)):
                col = cols(2 * i + b)
                tmp[...] = jnp.dot(k[g, :, :DL], do[g, :, col], preferred_element_type=F32)
            for b, tmp in enumerate((sa, sb)):
                col = cols(2 * i + b)
                for q in range(8):
                    rows = slice(q * 128, (q + 1) * 128)
                    t = pt[g, rows, col].astype(F32) * (tmp[rows] - cen[g, 0:1, col])
                    pt[to, rows, col] = t.astype(BF)

        return body

    def back_kv(g, d):
        def body(i):
            rows = cols(i)
            sa[:KV] = lax.dot_general(qg[g, :KV, :], pt[d, rows, :], NTD, preferred_element_type=F32)
            hook("kv%d" % g, i, 0, 2)
            sb[:DL] = lax.dot_general(do[g], pt[g, rows, :], NTD, preferred_element_type=F32)
            zero = jnp.zeros((KP - KV, WIDE), F32)
            t = jnp.concatenate([sa[:DL] * SC + sb[:DL], sa[DL:KV] * SC, zero], 0).astype(BF)
            t = jnp.swapaxes(t, 0, 1)
            gk[pl.ds(16 * g + 8 * i, 8)] = t[:, :KV].reshape(8, BLK, KV)

        return body

    loop("ds0", back_ds(0, 2))
    loop("kv0", back_kv(0, 2), 2)
    loop("ds1", back_ds(1, 0))
    loop("kv1", back_kv(1, 0), 2)

    def dq_store(i, slot):
        return pltpu.make_async_copy(qb.at[slot], dq_hbm.at[pl.ds(8 * i, 8)], qsem.at[slot])

    def back_q(i):
        col = cols(i)

        @pl.when(i >= 2)
        def _():
            dq_store(i - 2, i % 2).wait()

        r = []
        for g, d in ((0, 2), (1, 0)):
            r.append((jnp.dot(kt[g], pt[d, :, col], preferred_element_type=F32) * SC).astype(BF))
        for p in range(4):
            a, b = halves(r[0][:, p * 128 : (p + 1) * 128], r[1][:, p * 128 : (p + 1) * 128])
            qb[i % 2, 2 * p] = a
            qb[i % 2, 2 * p + 1] = b
        dq_store(i, i % 2).start()

    loop("dq", back_q)
    for op, arg in late:
        run(op, arg)
    dq_store(2, 0).wait()
    dq_store(3, 1).wait()
    for q in uv_out:
        q.wait()


def attention(lists, cache, qt, w, gout):
    v = pl.BlockSpec(memory_space=pltpu.VMEM)
    m = pl.BlockSpec(memory_space=pltpu.SMEM)
    a = pl.BlockSpec(memory_space=pl.ANY)
    scratch = [
        pltpu.VMEM((2, KP, ROWS), BF),
        pltpu.VMEM((2, KEYS, KP), BF),
        pltpu.VMEM((2, KV, KEYS), BF),
        pltpu.VMEM((BLK, WIDE), F32),
        pltpu.VMEM((3, KEYS, ROWS), BF),
        pltpu.VMEM((2, DL, ROWS), BF),
        pltpu.VMEM((2, 8, ROWS), F32),
        pltpu.VMEM((2, DL, WIDE), BF),
        pltpu.VMEM((KEYS, WIDE), F32),
        pltpu.VMEM((KEYS, WIDE), F32),
        pltpu.VMEM((NCH, CROWS, 128), BF),
        pltpu.VMEM((NH, DL, VH), BF),
        pltpu.VMEM((NH, TD, VH), BF),
        pltpu.VMEM((2, 8, TD, VH), BF),
        pltpu.VMEM((2, 8, KV, TD), BF),
        pltpu.SMEM((2, 32), jnp.int32),
        pltpu.SMEM((32,), jnp.int32),
        pltpu.SemaphoreType.DMA((2,)),
        pltpu.SemaphoreType.DMA((2,)),
        pltpu.SemaphoreType.DMA((2,)),
        pltpu.SemaphoreType.DMA((NCH,)),
    ]
    return pl.pallas_call(
        fused_body,
        out_shape=(
            jax.ShapeDtypeStruct((NH, TD, VH), BF),
            jax.ShapeDtypeStruct((NH, KV, TD), BF),
            jax.ShapeDtypeStruct((NCH, CROWS, 128), BF),
            jax.ShapeDtypeStruct((32, KV), F32),
        ),
        in_specs=[m, v, a, a, a],
        out_specs=(a, a, a, v),
        scratch_shapes=scratch + GATHER_SCRATCH + UV_SCRATCH + CACHE_SCRATCH,
        compiler_params=pltpu.CompilerParams(
            collective_id=0, has_side_effects=True, vmem_limit_bytes=VMEM_LIMIT
        ),
        name="latent_attention",
    )(lists, cache, qt, w, gout)


def on_device(queries, cache, lists, w_uv, grad_out):
    ho, dq, uv, gc = attention(
        lists, cache, queries.transpose(1, 2, 0), w_uv, grad_out.reshape(TD * NH, VH)
    )
    return ho.transpose(1, 0, 2), dq.transpose(2, 0, 1), gc, uv.reshape(NH, DL, VH)


def solution(mesh):
    return jax.shard_map(
        on_device,
        mesh=mesh,
        in_specs=(
            P("seq", "head", None),
            P(("seq", "head"), None),
            P("seq", None),
            P("head", None, None),
            P("seq", "head", None),
        ),
        out_specs=(
            P("seq", "head", None),
            P("seq", "head", None),
            P(("seq", "head"), None),
            P("head", None, None),
        ),
        check_vma=False,
    )
```

```python
import functools, jax, jax.numpy as jnp, numpy as np
from jax import lax
from jax.experimental import pallas as pl
from jax.experimental.pallas import tpu as pltpu
from jax.sharding import PartitionSpec as P

BLK=64; KEEP=15; SLOTS=16; KEYS=1024; DL=512; KV=576; KP=640; NH=32; VH=128; TD=128
ROWS=2048; TILE=256; NT=8
SC=192.0**-0.5
L2E=1.4426950408889634
NEG=-1e30
F32=jnp.float32; BF=jnp.bfloat16
NTD=(((1,),(1,)),((),()))
TND=(((0,),(0,)),((),()))

def halves(a,b):
    return (jnp.concatenate([a[:, :64], b[:, :64]],1), jnp.concatenate([a[:, 64:], b[:, 64:]],1))

def make_mask(mask_ref):
    r=lax.broadcasted_iota(jnp.int32,(BLK,TILE),0)
    c=lax.broadcasted_iota(jnp.int32,(BLK,TILE),1)
    mask_ref[...]=jnp.where(r<=(c%BLK),0.0,NEG).astype(F32)

MESH = pl.DeviceIdType.MESH
NCH = 4
CROWS = NH * DL // NCH
CH = CROWS // 2
QA = CH // 4
QB = QA // 4


def place():
    s = lax.axis_index("seq")
    z = lax.axis_index("head")
    return s, z, s % 2, (s // 2) % 4, s // 8


def seq_at(y, x, c):
    return (y * 4 + x) * 2 + c


def rcopy(src, dst, ssem, rsem, s, z):
    return pltpu.make_async_remote_copy(
        src_ref=src, dst_ref=dst, send_sem=ssem, recv_sem=rsem, device_id=(s, z), device_id_type=MESH
    )


def greet(seq_steps, head_steps):
    s, z, _, _, _ = place()
    barrier = pltpu.get_barrier_semaphore()
    for d in seq_steps:
        pl.semaphore_signal(barrier, inc=1, device_id=((s + d) % 32, z), device_id_type=MESH)
    for d in head_steps:
        pl.semaphore_signal(barrier, inc=1, device_id=(s, (z + d) % 4), device_id_type=MESH)
    pl.semaphore_wait(barrier, len(seq_steps) + len(head_steps))


def uv_stages(u, rc, ra, rb, ri, ss, rs):
    s, z, c, x, y = place()
    twin = seq_at(y, x, 1 - c)
    pa = x * (1 - c) + y * c
    pb = y * (1 - c) + x * c
    base = c * CH

    def nbr_a(d):
        return seq_at((y + d * c) % 4, (x + d * (1 - c)) % 4, c)

    def nbr_b(d):
        return seq_at((y + d * (1 - c)) % 4, (x + d * c) % 4, c)

    def ds(start, size):
        return pl.ds(pl.multiple_of(start, size), size)

    def add(terms):
        t = terms[0][...].astype(F32)
        for r in terms[1:]:
            t = t + r[...].astype(F32)
        return t.astype(BF)

    def quarter_a(k, q):
        return u.at[k, ds(base + q % 4 * QA, QA)]

    def quarter_b(k, q):
        return u.at[k, ds(base + pa * QA + q % 4 * QB, QB)]

    def half(k, h):
        return u.at[k, ds(h * CH, CH)]

    def copies(k, st):
        if st == 0:
            return [(half(k, 1 - c), rc.at[k], twin)]
        if st == 1:
            return [(rc.at[k, ds((pa + d) % 4 * QA, QA)], ra.at[k, d - 1], nbr_a(d)) for d in (1, 2, 3)]
        if st == 2:
            return [(rb.at[k, ds((pb + d) % 4 * QB, QB)], ri.at[k, d - 1], nbr_b(d)) for d in (1, 2, 3)]
        if st == 3:
            return [(quarter_b(k, pb), quarter_b(k, pb), nbr_b(d)) for d in (1, 2, 3)]
        if st == 4:
            return [(quarter_a(k, pa), quarter_a(k, pa), nbr_a(d)) for d in (1, 2, 3)]
        return [(half(k, c), half(k, c), twin)]

    def landed(k, st):
        if st == 3:
            return [quarter_b(k, pb + 4 - d) for d in (1, 2, 3)]
        if st == 4:
            return [quarter_a(k, pa + 4 - d) for d in (1, 2, 3)]
        if st == 5:
            return [half(k, 1 - c)]
        return [q[1] for q in copies(k, st)]

    def stage(k, st):
        if st > 0:
            for i, dst in enumerate(landed(k, st - 1)):
                rcopy(dst, dst, ss.at[k, st - 1, i], rs.at[k, st - 1, i], twin, z).wait_recv()
            for i, (src, dst, to) in enumerate(copies(k, st - 1)):
                rcopy(src, dst, ss.at[k, st - 1, i], rs.at[k, st - 1, i], to, z).wait_send()
        if st == 1:
            rc[k] = add([half(k, c), rc.at[k]])
        elif st == 2:
            rb[k] = add([rc.at[k, ds(pa * QA, QA)]] + [ra.at[k, d] for d in range(3)])
        elif st == 3:
            quarter_b(k, pb)[...] = add([rb.at[k, ds(pb * QB, QB)]] + [ri.at[k, d] for d in range(3)])
        if st < UV_STAGES - 1:
            for i, (src, dst, to) in enumerate(copies(k, st)):
                rcopy(src, dst, ss.at[k, st, i], rs.at[k, st, i], to, z).start()

    return stage


UV_STAGES = 7
UV_SCRATCH = [
    pltpu.VMEM((NCH, CH, 128), BF),
    pltpu.VMEM((NCH, 3, QA, 128), BF),
    pltpu.VMEM((NCH, QA, 128), BF),
    pltpu.VMEM((NCH, 3, QB, 128), BF),
    pltpu.SemaphoreType.DMA((NCH, UV_STAGES - 1, 3)),
    pltpu.SemaphoreType.DMA((NCH, UV_STAGES - 1, 3)),
]


VMEM_LIMIT = 63 * 2**20
WIDE = 512


class Gather:
    def __init__(self, cache_ref, full, lsem, zs, zr, s1, r1, s2, r2, s3, r3, s4, r4, s5, r5):
        self.__dict__.update(locals())
        self.pend = []

    def at(self, a, b, part=None):
        _, _, c, x, y = place()
        t = seq_at((y + a * c + b * (1 - c)) % 4, (x + a * (1 - c) + b * c) % 4, c)
        return self.block(t, part)

    def block(self, t, part):
        if part is None:
            return self.full.at[pl.ds(2 * t, 2)]
        return self.full.at[2 * t + part]

    def nbr_a(self, d):
        _, _, c, x, y = place()
        return seq_at((y + d * c) % 4, (x + d * (1 - c)) % 4, c)

    def nbr_b(self, d):
        _, _, c, x, y = place()
        return seq_at((y + d * (1 - c)) % 4, (x + d * c) % 4, c)

    def start(self, src, ssem, rsem, dev):
        q = rcopy(src, src, ssem, rsem, dev, place()[1])
        q.start()
        self.pend.append(q)

    def got(self, dst, rsem):
        s, z, _, _, _ = place()
        rcopy(dst, dst, self.s5.at[0], rsem, s, (z + 1) % 4).wait_recv()

    def to_twin(self, a, b):
        _, _, c, x, y = place()
        k = (a % 4) * 4 + b % 4
        self.start(self.at(a, b), self.s5.at[k], self.r5.at[k], seq_at(y, x, 1 - c))

    def send_part(self, a, b, part, side, sems, nbr):
        ssem, rsem = sems
        self.start(self.at(a, b, part), ssem.at[side, part], rsem.at[side, part], nbr(1 - 2 * side))

    def first_sends(self, a, b, sems, nbr):
        self.send_part(a, b, 0, 0, sems, nbr)
        self.send_part(a, b, 1, 1, sems, nbr)
        self.send_part(a, b, 1, 0, sems, nbr)
        self.send_part(a, b, 0, 1, sems, nbr)

    def b_sends(self, a):
        k = a % 4
        self.first_sends(a, 0, (self.s3.at[k], self.r3.at[k]), self.nbr_b)

    def b_relay(self, a):
        k = a % 4
        self.got(self.at(a, -1, 0), self.r3.at[k, 0, 0])
        self.start(self.at(a, -1, 0), self.s4.at[k, 0], self.r4.at[k, 0], self.nbr_b(1))
        self.got(self.at(a, 1, 1), self.r3.at[k, 1, 1])
        self.start(self.at(a, 1, 1), self.s4.at[k, 1], self.r4.at[k, 1], self.nbr_b(-1))

    def b_rest(self, a):
        k = a % 4
        self.got(self.at(a, -1, 1), self.r3.at[k, 0, 1])
        self.to_twin(a, -1)
        self.got(self.at(a, 1, 0), self.r3.at[k, 1, 0])
        self.to_twin(a, 1)

    def step0(self):
        s, z, _, _, _ = place()
        mine = self.full.at[2 * s + z // 2, pl.ds(pl.multiple_of((z % 2) * 32, 32), 32)]
        self.local = pltpu.make_async_copy(self.cache_ref, mine, self.lsem)
        self.local.start()
        self.zc = [
            rcopy(self.cache_ref, mine, self.zs.at[d - 1], self.zr.at[d - 1], s, (z + d) % 4) for d in (1, 2, 3)
        ]
        for q in self.zc:
            q.start()
        self.pend += self.zc

    def step1(self):
        self.local.wait()
        for q in self.zc:
            q.wait_recv()
        self.first_sends(0, 0, (self.s1, self.r1), self.nbr_a)
        self.b_sends(0)
        self.to_twin(0, 0)

    def step2(self):
        self.got(self.at(-1, 0, 0), self.r1.at[0, 0])
        self.start(self.at(-1, 0, 0), self.s2.at[0], self.r2.at[0], self.nbr_a(1))
        self.got(self.at(1, 0, 1), self.r1.at[1, 1])
        self.start(self.at(1, 0, 1), self.s2.at[1], self.r2.at[1], self.nbr_a(-1))
        self.got(self.at(-1, 0, 1), self.r1.at[0, 1])
        self.got(self.at(1, 0, 0), self.r1.at[1, 0])
        self.b_sends(-1)
        self.b_sends(1)
        self.to_twin(-1, 0)
        self.to_twin(1, 0)

    def step3(self):
        self.b_relay(0)
        self.got(self.at(2, 0, 0), self.r2.at[0])
        self.got(self.at(2, 0, 1), self.r2.at[1])
        self.b_sends(2)
        self.b_rest(0)
        self.to_twin(2, 0)

    def step4(self):
        for a in (-1, 1):
            self.b_relay(a)

    def step5(self):
        for a in (-1, 1):
            self.b_rest(a)
        self.b_relay(2)

    def step6(self):
        self.b_rest(2)
        for a in (0, -1, 1, 2):
            k = a % 4
            self.got(self.at(a, 2, 0), self.r4.at[k, 0])
            self.got(self.at(a, 2, 1), self.r4.at[k, 1])
            self.to_twin(a, 2)

    def step7(self):
        _, _, c, x, y = place()
        for a in range(4):
            for b in range(4):
                t = seq_at((y + a * (1 - c) + b * c) % 4, (x + a * c + b * (1 - c)) % 4, 1 - c)
                self.got(self.block(t, None), self.r5.at[a * 4 + b])
        for q in self.pend:
            q.wait_send()


GATHER_SCRATCH = [pltpu.VMEM((64, BLK, KV), BF), pltpu.SemaphoreType.DMA] + [
    pltpu.SemaphoreType.DMA(shape)
    for shape in ((3,), (3,), (2, 2), (2, 2), (2,), (2,), (4, 2, 2), (4, 2, 2), (4, 2), (4, 2), (16,), (16,))
]


def cache_stages(inv, flag, gk, gc, zr1, zr2, rz, send, recv, part, zss, zrs, xss, xrs, fss, frs):
    s, z, c, x, y = place()
    z1, z2, z3 = (z + 1) % 4, (z + 2) % 4, (z + 3) % 4

    def quarter(b, n, q):
        return gk.at[pl.ds(b, n), pl.ds(pl.multiple_of(q * 16, 16), 16)]

    def first(u):
        b = 8 * u
        return [
            rcopy(quarter(b, 4, z2), zr1.at[u, 0], zss.at[u, 0, 0], zrs.at[u, 0, 0], s, z1),
            rcopy(quarter(b + 4, 4, z2), zr1.at[u, 1], zss.at[u, 0, 1], zrs.at[u, 0, 1], s, z3),
        ]

    def second(u):
        b = 8 * u
        return [
            rcopy(quarter(b, 8, z1), zr2.at[u, 0], zss.at[u, 1, 0], zrs.at[u, 1, 0], s, z1),
            rcopy(quarter(b, 8, z3), zr2.at[u, 1], zss.at[u, 1, 1], zrs.at[u, 1, 1], s, z3),
        ]

    def head_send(u):
        for q in first(u):
            q.start()

    def head_relay(u):
        b = 8 * u
        for q in first(u):
            q.wait()
        for r, b0, q in ((zr1.at[u, 0], b, z1), (zr1.at[u, 1], b + 4, z3)):
            t = quarter(b0, 4, q)
            t[...] = (t[...].astype(F32) + r[...].astype(F32)).astype(BF)
        for q in second(u):
            q.start()

    def head_sum(u):
        for q in second(u):
            q.wait()
        t = quarter(8 * u, 8, z)[...].astype(F32) + zr2[u, 0].astype(F32) + zr2[u, 1].astype(F32)
        rz[u // 2, 8 * (u % 2) : 8 * (u % 2) + 8] = t.astype(BF)
        if u % 2:
            rz[u // 2, 16] = jnp.zeros((16, KV), BF)

    def packed(t):
        v = rz[0, inv[0, t]].astype(F32) + rz[1, inv[1, t]].astype(F32)
        mark = jnp.zeros((16, KP - KV), F32) + flag[t].astype(F32)
        return jnp.concatenate([v, mark], 1).astype(BF)

    def message(d):
        return rcopy(send.at[d], recv.at[d], xss.at[d], xrs.at[d], (s + d) % 32, z)

    def spread():
        for d in range(32):
            send[d] = packed((s + d) % 32)

        def one(d, _):
            @pl.when(s + d >= 32)
            def _():
                message(d).start()

            return 0

        lax.fori_loop(1, 32, one, 0)

    def last(b):
        h = 2 * b + z // 2
        return h, rcopy(part.at[b], part.at[2 + z % 2], fss.at[b], frs.at[z % 2], s, h)

    def collect():
        def one(d, _):
            @pl.when(d > s)
            def _():
                message(d).wait_recv()

            @pl.when(s + d >= 32)
            def _():
                message(d).wait_send()

            return 0

        lax.fori_loop(1, 32, one, 0)
        first = rz[0, 0].astype(F32)
        other = rz[1, 0].astype(F32)
        for d in range(32):
            v = (recv[d] if d else send[0]).astype(F32)
            if d:
                v = jnp.where(d > s, v, 0.0)
            v, mark = v[:, :KV], v[:, KV : KV + 1]
            moved = v * mark
            other = other + moved
            first = first + (v - moved)
        part[0] = first
        part[1] = other
        for b in range(2):
            h, q = last(b)

            @pl.when(h != z)
            def _():
                q.start()

    def finish():
        for i in range(2):
            src = 2 * (z % 2) + i

            @pl.when(src == z)
            def _():
                gc[16 * i : 16 * i + 16] = part[z // 2]

            @pl.when(src != z)
            def _():
                rcopy(part.at[2 + i], part.at[2 + i], fss.at[0], frs.at[i], s, (z + 1) % 4).wait_recv()
                gc[16 * i : 16 * i + 16] = part[2 + i]

        for b in range(2):
            h, q = last(b)

            @pl.when(h != z)
            def _():
                q.wait_send()

    return head_send, head_relay, head_sum, spread, collect, finish


CACHE_SCRATCH = [
    pltpu.VMEM((4, 2, 4, 16, KV), BF),
    pltpu.VMEM((4, 2, 8, 16, KV), BF),
    pltpu.VMEM((2, 17, 16, KV), BF),
    pltpu.VMEM((32, 16, KP), BF),
    pltpu.VMEM((32, 16, KP), BF),
    pltpu.VMEM((4, 16, KV), F32),
    pltpu.SemaphoreType.DMA((4, 2, 2)),
    pltpu.SemaphoreType.DMA((4, 2, 2)),
    pltpu.SemaphoreType.DMA((32,)),
    pltpu.SemaphoreType.DMA((32,)),
    pltpu.SemaphoreType.DMA((2,)),
    pltpu.SemaphoreType.DMA((2,)),
]

PHASES = [("fwd", 8, 2.3), ("ds0", 2, 1.3), ("kv0", 4, 1.3), ("ds1", 2, 1.3), ("kv1", 4, 1.3), ("dq", 4, 1.5)]
UV_GAPS = [0.0, 2.8, 4.6, 2.8, 2.8, 4.6, 2.8]
HEAD_GAPS = [3.0, 4.0]
END_GAPS = [0.1, 8.0, 2.5]


def plan():
    ends, now = [], 0.0
    for name, n, us in PHASES:
        for i in range(n):
            now += us
            ends.append((now, name, i))
    when = {(name, i): t for t, name, i in ends}
    todo = []
    for k in range(NCH):
        t = when["fwd", 8 // NCH * (k + 1) - 1]
        for st in range(UV_STAGES):
            t += UV_GAPS[st]
            todo.append((t, "uv", (k, st)))
    for u in range(4):
        t = when["kv%d" % (u // 2), 2 * (u % 2) + 1]
        todo.append((t, "head_send", (u,)))
        todo.append((t + HEAD_GAPS[0], "head_relay", (u,)))
        t += sum(HEAD_GAPS)
        todo.append((t, "head_sum", (u,)))
    for op, gap in zip(("spread", "collect", "finish"), END_GAPS):
        t += gap
        todo.append((t, op, ()))
    todo.sort(key=lambda e: e[0])
    at, late = {}, []
    for t, op, arg in todo:
        for end, name, i in ends:
            if end >= t - 1e-6:
                at.setdefault((name, i), []).append((op, arg))
                break
        else:
            late.append((op, arg))
    return at, late


def fused_body(lists, cache, qt, w_hbm, gout_hbm, ho_hbm, dq_hbm, uv_hbm, gc, *scr):
    (qg, k, kt, mask, pt, do, cen, ot, sa, sb, u, w, gout, hb, qb, inv, flag,
     lsem, hsem, qsem, osem) = scr[:21]
    scr = scr[21:]
    gat = Gather(cache, *scr[: len(GATHER_SCRATCH)])
    full = gat.full
    scr = scr[len(GATHER_SCRATCH) :]
    stage = uv_stages(u, *scr[: len(UV_SCRATCH)])
    gk = full
    cs = cache_stages(inv, flag, gk, gc, *scr[len(UV_SCRATCH) :])
    head_send, head_relay, head_sum, spread, collect, finish = cs
    s, z, c, x, y = place()

    barrier = pltpu.get_barrier_semaphore()
    for d in range(1, 32):
        pl.semaphore_signal(barrier, inc=1, device_id=((s + d) % 32, z), device_id_type=MESH)
    for d in range(1, 4):
        pl.semaphore_signal(barrier, inc=1, device_id=(s, (z + d) % 4), device_id_type=MESH)

    def q_load(i, slot):
        return pltpu.make_async_copy(qt.at[pl.ds(8 * i, 8)], qb.at[slot], qsem.at[slot])

    g_load = pltpu.make_async_copy(gout_hbm, u.at[0], lsem.at[1])
    w_load = pltpu.make_async_copy(w_hbm, w, lsem.at[0])
    g_load.start()
    q_load(0, 0).start()
    q_load(1, 1).start()
    w_load.start()

    r = lax.broadcasted_iota(jnp.int32, (BLK, WIDE), 0)
    cc = lax.broadcasted_iota(jnp.int32, (BLK, WIDE), 1)
    mask[...] = jnp.where(r <= (cc % BLK), 0.0, NEG).astype(F32)
    row = lax.broadcasted_iota(jnp.int32, (64, ROWS), 0)
    one = jnp.where(row == 0, 1.0, 0.0).astype(BF)
    qg[0, KV:, :] = one
    qg[1, KV:, :] = one
    pl.semaphore_wait(barrier, 34)
    gat.step0()

    def find(t, _):
        which = jnp.int32(0)
        for g in range(2):
            slot = jnp.int32(16)
            for j in range(KEEP):
                d = lists[g, j] - 2 * t
                hit = (d >= 0) & (d < 2)
                slot = jnp.where(hit, j + 1, slot)
                which = jnp.where(hit, d, which)
            inv[g, t] = slot
        flag[t] = which
        return 0

    g_load.wait()

    def turn(i, _):
        t = pl.ds(pl.multiple_of(i * 16, 16), 16)
        x = u[0, pl.ds(pl.multiple_of(i * 512, 512), 512)].reshape(16, NH, VH)
        gout[:, t, :] = jnp.swapaxes(x, 0, 1)
        return 0

    lax.fori_loop(0, TD // 16, turn, 0)
    lax.fori_loop(0, 32, find, 0)
    gat.step1()

    def prep_q(lo, hi):
        def body(i, _):
            q_load(i, i % 2).wait()
            for p in range(4):
                a, b = halves(qb[i % 2, 2 * p], qb[i % 2, 2 * p + 1])
                col = pl.ds(pl.multiple_of(i * WIDE + p * 128, 128), 128)
                qg[0, :KV, col] = a
                qg[1, :KV, col] = b

            @pl.when(i + 2 < 4)
            def _():
                q_load(i + 2, i % 2).start()

            return 0

        lax.fori_loop(lo, hi, body, 0)

    def prep_do(lo, hi):
        def body(i, _):
            for p in range(4):
                h = 8 * i + 2 * p
                d0 = lax.dot_general(w[h], gout[h], NTD, preferred_element_type=F32).astype(BF)
                d1 = lax.dot_general(w[h + 1], gout[h + 1], NTD, preferred_element_type=F32).astype(BF)
                a, b = halves(d0, d1)
                col = pl.ds(pl.multiple_of(i * WIDE + p * 128, 128), 128)
                do[0, :, col] = a
                do[1, :, col] = b
            return 0

        lax.fori_loop(lo, hi, body, 0)

    prep_q(0, 2)
    gat.step2()
    prep_q(2, 3)
    gat.step3()
    prep_q(3, 4)
    gat.step4()
    w_load.wait()
    prep_do(0, 2)
    gat.step5()
    prep_do(2, 4)
    gat.step6()
    gat.step7()

    colid = lax.broadcasted_iota(jnp.int32, (BLK, KP - DL), 1)
    for g in range(2):
        for j in range(SLOTS):
            if j == 0:
                blk = full[2 * s + g]
                bias = jnp.float32(0.0)
            else:
                e = lists[g, j - 1]
                blk = full[jnp.maximum(e, 0)]
                bias = jnp.where(e >= 0, 0.0, NEG).astype(F32)
            k[g, j * BLK : (j + 1) * BLK, :DL] = blk[:, :DL]
            rot = jnp.concatenate([blk[:, DL:].astype(F32), jnp.zeros((BLK, 64), F32)], 1)
            k[g, j * BLK : (j + 1) * BLK, DL:] = jnp.where(colid == 64, bias, rot).astype(BF)
        for b in range(8):
            t = jnp.swapaxes(k[g, b * 128 : (b + 1) * 128, :], 0, 1)
            kt[g, :, b * 128 : (b + 1) * 128] = t[:KV]

    uv_out = [pltpu.make_async_copy(u.at[q], uv_hbm.at[q], osem.at[q]) for q in range(NCH)]

    def run(op, arg):
        if op == "uv":
            stage(*arg)
            if arg[1] == UV_STAGES - 1:
                uv_out[arg[0]].start()
        else:
            ops = {"head_send": head_send, "head_relay": head_relay, "head_sum": head_sum}
            ops.update({"spread": spread, "collect": collect, "finish": finish})
            ops[op](*arg)

    at, late = plan()
    steps = {p[0]: p[1] for p in PHASES}

    def hook(name, i, part=0, parts=1):
        for j in range(part, steps[name], parts):
            if (name, j) in at:

                @pl.when(i == j // parts)
                def _():
                    for op, arg in at[name, j]:
                        run(op, arg)

    def loop(name, body, parts=1):
        def step(i, _):
            body(i)
            hook(name, i, parts - 1, parts)
            return 0

        lax.fori_loop(0, steps[name] // parts, step, 0)

    def cols(i, n=WIDE):
        return pl.ds(pl.multiple_of(i * n, n), n)

    def ho_store(i, slot):
        return pltpu.make_async_copy(hb.at[slot], ho_hbm.at[pl.ds(8 * i, 8)], hsem.at[slot])

    def scores(to, g, i):
        to[...] = jnp.dot(k[g], qg[g, :, cols(i)], preferred_element_type=F32)

    def softmax(sc, g, col):
        sc[:BLK] = sc[:BLK] + mask[...]
        m = jnp.max(sc[...], axis=0, keepdims=True)
        total = jnp.zeros((8, WIDE), F32)
        for b in range(16):
            e = jnp.exp2((sc[b * 64 : (b + 1) * 64] - m) * (SC * L2E))
            total = total + jnp.sum(e.reshape(8, 8, WIDE), axis=0)
            pt[g, b * 64 : (b + 1) * 64, col] = e.astype(BF)
        return 1.0 / jnp.sum(total, axis=0, keepdims=True)

    def values(g, col, inv_l):
        o = jnp.dot(kt[g, :DL, :], pt[g, :, col], preferred_element_type=F32) * inv_l
        ot[g] = o.astype(BF)
        dn = (do[g, :, col].astype(F32) * inv_l).astype(BF)
        do[g, :, col] = dn
        centre = jnp.sum(o * dn.astype(F32), axis=0, keepdims=True)
        cen[g, :, col] = jnp.broadcast_to(centre, (8, WIDE))

    scores(sa, 0, 0)

    def fwd(i):
        col = cols(i)
        scores(sb, 1, i)
        values(0, col, softmax(sa, 0, col))
        hook("fwd", i, 0, 2)
        scores(sa, 0, jnp.minimum(i + 1, 3))
        values(1, col, softmax(sb, 1, col))

        @pl.when(i >= 2)
        def _():
            ho_store(i - 2, i % 2).wait()

        for p in range(4):
            hh = halves(ot[0, :, p * 128 : (p + 1) * 128], ot[1, :, p * 128 : (p + 1) * 128])
            for q in range(2):
                h = 2 * p + q
                part = jnp.dot(hh[q], gout[8 * i + h], preferred_element_type=F32).astype(BF)
                u[i, h * DL : (h + 1) * DL] = part
                hb[i % 2, h] = lax.dot_general(hh[q], w[8 * i + h], TND, preferred_element_type=F32).astype(BF)
        ho_store(i, i % 2).start()

    loop("fwd", fwd, 2)
    ho_store(2, 0).wait()
    ho_store(3, 1).wait()

    def back_ds(g, to):
        def body(i):
            for b, tmp in enumerate((sa, sb)):
                col = cols(2 * i + b)
                tmp[...] = jnp.dot(k[g, :, :DL], do[g, :, col], preferred_element_type=F32)
            for b, tmp in enumerate((sa, sb)):
                col = cols(2 * i + b)
                for q in range(8):
                    rows = slice(q * 128, (q + 1) * 128)
                    t = pt[g, rows, col].astype(F32) * (tmp[rows] - cen[g, 0:1, col])
                    pt[to, rows, col] = t.astype(BF)

        return body

    def back_kv(g, d):
        def body(i):
            rows = cols(i)
            sa[:KV] = lax.dot_general(qg[g, :KV, :], pt[d, rows, :], NTD, preferred_element_type=F32)
            hook("kv%d" % g, i, 0, 2)
            sb[:DL] = lax.dot_general(do[g], pt[g, rows, :], NTD, preferred_element_type=F32)
            zero = jnp.zeros((KP - KV, WIDE), F32)
            t = jnp.concatenate([sa[:DL] * SC + sb[:DL], sa[DL:KV] * SC, zero], 0).astype(BF)
            t = jnp.swapaxes(t, 0, 1)
            gk[pl.ds(16 * g + 8 * i, 8)] = t[:, :KV].reshape(8, BLK, KV)

        return body

    loop("ds0", back_ds(0, 2))
    loop("kv0", back_kv(0, 2), 2)
    loop("ds1", back_ds(1, 0))
    loop("kv1", back_kv(1, 0), 2)

    def dq_store(i, slot):
        return pltpu.make_async_copy(qb.at[slot], dq_hbm.at[pl.ds(8 * i, 8)], qsem.at[slot])

    def back_q(i):
        col = cols(i)

        @pl.when(i >= 2)
        def _():
            dq_store(i - 2, i % 2).wait()

        r = []
        for g, d in ((0, 2), (1, 0)):
            r.append((jnp.dot(kt[g], pt[d, :, col], preferred_element_type=F32) * SC).astype(BF))
        for p in range(4):
            a, b = halves(r[0][:, p * 128 : (p + 1) * 128], r[1][:, p * 128 : (p + 1) * 128])
            qb[i % 2, 2 * p] = a
            qb[i % 2, 2 * p + 1] = b
        dq_store(i, i % 2).start()

    loop("dq", back_q)
    for op, arg in late:
        run(op, arg)
    dq_store(2, 0).wait()
    dq_store(3, 1).wait()
    for q in uv_out:
        q.wait()


def attention(lists, cache, qt, w, gout):
    v = pl.BlockSpec(memory_space=pltpu.VMEM)
    m = pl.BlockSpec(memory_space=pltpu.SMEM)
    a = pl.BlockSpec(memory_space=pl.ANY)
    scratch = [
        pltpu.VMEM((2, KP, ROWS), BF),
        pltpu.VMEM((2, KEYS, KP), BF),
        pltpu.VMEM((2, KV, KEYS), BF),
        pltpu.VMEM((BLK, WIDE), F32),
        pltpu.VMEM((3, KEYS, ROWS), BF),
        pltpu.VMEM((2, DL, ROWS), BF),
        pltpu.VMEM((2, 8, ROWS), F32),
        pltpu.VMEM((2, DL, WIDE), BF),
        pltpu.VMEM((KEYS, WIDE), F32),
        pltpu.VMEM((KEYS, WIDE), F32),
        pltpu.VMEM((NCH, CROWS, 128), BF),
        pltpu.VMEM((NH, DL, VH), BF),
        pltpu.VMEM((NH, TD, VH), BF),
        pltpu.VMEM((2, 8, TD, VH), BF),
        pltpu.VMEM((2, 8, KV, TD), BF),
        pltpu.SMEM((2, 32), jnp.int32),
        pltpu.SMEM((32,), jnp.int32),
        pltpu.SemaphoreType.DMA((2,)),
        pltpu.SemaphoreType.DMA((2,)),
        pltpu.SemaphoreType.DMA((2,)),
        pltpu.SemaphoreType.DMA((NCH,)),
    ]
    return pl.pallas_call(
        fused_body,
        out_shape=(
            jax.ShapeDtypeStruct((NH, TD, VH), BF),
            jax.ShapeDtypeStruct((NH, KV, TD), BF),
            jax.ShapeDtypeStruct((NCH, CROWS, 128), BF),
            jax.ShapeDtypeStruct((32, KV), F32),
        ),
        in_specs=[m, v, a, a, a],
        out_specs=(a, a, a, v),
        scratch_shapes=scratch + GATHER_SCRATCH + UV_SCRATCH + CACHE_SCRATCH,
        compiler_params=pltpu.CompilerParams(
            collective_id=0, has_side_effects=True, vmem_limit_bytes=VMEM_LIMIT
        ),
        name="latent_attention",
    )(lists, cache, qt, w, gout)


def hand_on_body(ho, dq, uv, gc, ho_out, dq_out, uv_out, gc_out, vh, vt, vq, vu, vg, si, so):
    def part(ref, i):
        return ref.at[pl.ds(8 * i, 8)]

    gc_in = pltpu.make_async_copy(gc, vg, si.at[3, 0])
    gc_copy = pltpu.make_async_copy(vg, gc_out, so.at[3, 0])
    ins, outs = [], []
    for i in range(4):
        ins.append(pltpu.make_async_copy(part(ho, i), part(vh, i), si.at[0, i]))
    for i in range(4):
        ins.append(pltpu.make_async_copy(part(dq, i), part(vq, i), si.at[1, i]))
        outs.append(pltpu.make_async_copy(part(vq, i), part(dq_out, i), so.at[1, i]))
        ins.append(pltpu.make_async_copy(part(uv, i), part(vu, i), si.at[2, i]))
        outs.append(pltpu.make_async_copy(part(vu, i), part(uv_out, i), so.at[2, i]))
    gc_in.start()
    for q in ins:
        q.start()
    gc_in.wait()
    gc_copy.start()
    for q in ins[:4]:
        q.wait()
    turns = []
    for i in range(4):
        for q, out in zip(ins[4 + 2 * i : 6 + 2 * i], outs[2 * i : 2 * i + 2]):
            q.wait()
            out.start()
        t = pl.ds(32 * i, 32)
        vt[t] = jnp.swapaxes(vh[:, t, :], 0, 1)
        turns.append(pltpu.make_async_copy(vt.at[t], ho_out.at[t], so.at[0, i]))
        turns[-1].start()
    for q in outs + turns:
        q.wait()
    gc_copy.wait()


def hand_on(ho, dq, uv, gc):
    a = pl.BlockSpec(memory_space=pl.ANY)
    return pl.pallas_call(
        hand_on_body,
        out_shape=(
            jax.ShapeDtypeStruct((TD, NH, VH), BF),
            jax.ShapeDtypeStruct((NH, KV, TD), BF),
            jax.ShapeDtypeStruct((NH, DL, VH), BF),
            jax.ShapeDtypeStruct((32, KV), F32),
        ),
        in_specs=[a] * 4,
        out_specs=(a,) * 4,
        scratch_shapes=[
            pltpu.VMEM((NH, TD, VH), BF),
            pltpu.VMEM((TD, NH, VH), BF),
            pltpu.VMEM((NH, KV, TD), BF),
            pltpu.VMEM((NH, DL, VH), BF),
            pltpu.VMEM((32, KV), F32),
            pltpu.SemaphoreType.DMA((4, 4)),
            pltpu.SemaphoreType.DMA((4, 4)),
        ],
        compiler_params=pltpu.CompilerParams(vmem_limit_bytes=VMEM_LIMIT),
        name="hand_on",
    )(ho, dq, uv, gc)


def on_device(queries, cache, lists, w_uv, grad_out):
    ho, dq, uv, gc = attention(
        lists, cache, queries.transpose(1, 2, 0), w_uv, grad_out.reshape(TD * NH, VH)
    )
    ho, dq, uv, gc = hand_on(ho, dq, uv.reshape(NH, DL, VH), gc)
    return ho, dq.transpose(2, 0, 1), gc, uv


def solution(mesh):
    return jax.shard_map(
        on_device,
        mesh=mesh,
        in_specs=(
            P("seq", "head", None),
            P(("seq", "head"), None),
            P("seq", None),
            P("head", None, None),
            P("seq", "head", None),
        ),
        out_specs=(
            P("seq", "head", None),
            P("seq", "head", None),
            P(("seq", "head"), None),
            P("head", None, None),
        ),
        check_vma=False,
    )
```

```python
import functools, jax, jax.numpy as jnp, numpy as np
from jax import lax
from jax.experimental import pallas as pl
from jax.experimental.pallas import tpu as pltpu
from jax.sharding import PartitionSpec as P

BLK=64; KEEP=15; SLOTS=16; KEYS=1024; DL=512; KV=576; KP=640; NH=32; VH=128; TD=128
ROWS=2048; TILE=256; NT=8
SC=192.0**-0.5
L2E=1.4426950408889634
NEG=-1e30
F32=jnp.float32; BF=jnp.bfloat16
NTD=(((1,),(1,)),((),()))
TND=(((0,),(0,)),((),()))

def halves(a,b):
    return (jnp.concatenate([a[:, :64], b[:, :64]],1), jnp.concatenate([a[:, 64:], b[:, 64:]],1))

def make_mask(mask_ref):
    r=lax.broadcasted_iota(jnp.int32,(BLK,TILE),0)
    c=lax.broadcasted_iota(jnp.int32,(BLK,TILE),1)
    mask_ref[...]=jnp.where(r<=(c%BLK),0.0,NEG).astype(F32)

MESH = pl.DeviceIdType.MESH
NCH = 4
CROWS = NH * DL // NCH
CH = CROWS // 2
QA = CH // 4
QB = QA // 4


def place():
    s = lax.axis_index("seq")
    z = lax.axis_index("head")
    return s, z, s % 2, (s // 2) % 4, s // 8


def seq_at(y, x, c):
    return (y * 4 + x) * 2 + c


def rcopy(src, dst, ssem, rsem, s, z):
    return pltpu.make_async_remote_copy(
        src_ref=src, dst_ref=dst, send_sem=ssem, recv_sem=rsem, device_id=(s, z), device_id_type=MESH
    )


def greet(seq_steps, head_steps):
    s, z, _, _, _ = place()
    barrier = pltpu.get_barrier_semaphore()
    for d in seq_steps:
        pl.semaphore_signal(barrier, inc=1, device_id=((s + d) % 32, z), device_id_type=MESH)
    for d in head_steps:
        pl.semaphore_signal(barrier, inc=1, device_id=(s, (z + d) % 4), device_id_type=MESH)
    pl.semaphore_wait(barrier, len(seq_steps) + len(head_steps))


def uv_stages(u, rc, ra, rb, ri, ss, rs):
    s, z, c, x, y = place()
    twin = seq_at(y, x, 1 - c)
    pa = x * (1 - c) + y * c
    pb = y * (1 - c) + x * c
    base = c * CH

    def nbr_a(d):
        return seq_at((y + d * c) % 4, (x + d * (1 - c)) % 4, c)

    def nbr_b(d):
        return seq_at((y + d * (1 - c)) % 4, (x + d * c) % 4, c)

    def ds(start, size):
        return pl.ds(pl.multiple_of(start, size), size)

    def add(terms):
        t = terms[0][...].astype(F32)
        for r in terms[1:]:
            t = t + r[...].astype(F32)
        return t.astype(BF)

    def quarter_a(k, q):
        return u.at[k, ds(base + q % 4 * QA, QA)]

    def quarter_b(k, q):
        return u.at[k, ds(base + pa * QA + q % 4 * QB, QB)]

    def half(k, h):
        return u.at[k, ds(h * CH, CH)]

    def copies(k, st):
        if st == 0:
            return [(half(k, 1 - c), rc.at[k], twin)]
        if st == 1:
            return [(rc.at[k, ds((pa + d) % 4 * QA, QA)], ra.at[k, d - 1], nbr_a(d)) for d in (1, 2, 3)]
        if st == 2:
            return [(rb.at[k, ds((pb + d) % 4 * QB, QB)], ri.at[k, d - 1], nbr_b(d)) for d in (1, 2, 3)]
        if st == 3:
            return [(quarter_b(k, pb), quarter_b(k, pb), nbr_b(d)) for d in (1, 2, 3)]
        if st == 4:
            return [(quarter_a(k, pa), quarter_a(k, pa), nbr_a(d)) for d in (1, 2, 3)]
        return [(half(k, c), half(k, c), twin)]

    def landed(k, st):
        if st == 3:
            return [quarter_b(k, pb + 4 - d) for d in (1, 2, 3)]
        if st == 4:
            return [quarter_a(k, pa + 4 - d) for d in (1, 2, 3)]
        if st == 5:
            return [half(k, 1 - c)]
        return [q[1] for q in copies(k, st)]

    def stage(k, st):
        if st > 0:
            for i, dst in enumerate(landed(k, st - 1)):
                rcopy(dst, dst, ss.at[k, st - 1, i], rs.at[k, st - 1, i], twin, z).wait_recv()
            for i, (src, dst, to) in enumerate(copies(k, st - 1)):
                rcopy(src, dst, ss.at[k, st - 1, i], rs.at[k, st - 1, i], to, z).wait_send()
        if st == 1:
            rc[k] = add([half(k, c), rc.at[k]])
        elif st == 2:
            rb[k] = add([rc.at[k, ds(pa * QA, QA)]] + [ra.at[k, d] for d in range(3)])
        elif st == 3:
            quarter_b(k, pb)[...] = add([rb.at[k, ds(pb * QB, QB)]] + [ri.at[k, d] for d in range(3)])
        if st < UV_STAGES - 1:
            for i, (src, dst, to) in enumerate(copies(k, st)):
                rcopy(src, dst, ss.at[k, st, i], rs.at[k, st, i], to, z).start()

    return stage


UV_STAGES = 7
UV_SCRATCH = [
    pltpu.VMEM((NCH, CH, 128), BF),
    pltpu.VMEM((NCH, 3, QA, 128), BF),
    pltpu.VMEM((NCH, QA, 128), BF),
    pltpu.VMEM((NCH, 3, QB, 128), BF),
    pltpu.SemaphoreType.DMA((NCH, UV_STAGES - 1, 3)),
    pltpu.SemaphoreType.DMA((NCH, UV_STAGES - 1, 3)),
]


VMEM_LIMIT = 63 * 2**20
WIDE = 512


class Gather:
    def __init__(self, cache_ref, full, lsem, zs, zr, s1, r1, s2, r2, s3, r3, s4, r4, s5, r5):
        self.__dict__.update(locals())
        self.pend = []

    def at(self, a, b, part=None):
        _, _, c, x, y = place()
        t = seq_at((y + a * c + b * (1 - c)) % 4, (x + a * (1 - c) + b * c) % 4, c)
        return self.block(t, part)

    def block(self, t, part):
        if part is None:
            return self.full.at[pl.ds(2 * t, 2)]
        return self.full.at[2 * t + part]

    def nbr_a(self, d):
        _, _, c, x, y = place()
        return seq_at((y + d * c) % 4, (x + d * (1 - c)) % 4, c)

    def nbr_b(self, d):
        _, _, c, x, y = place()
        return seq_at((y + d * (1 - c)) % 4, (x + d * c) % 4, c)

    def start(self, src, ssem, rsem, dev):
        q = rcopy(src, src, ssem, rsem, dev, place()[1])
        q.start()
        self.pend.append(q)

    def got(self, dst, rsem):
        s, z, _, _, _ = place()
        rcopy(dst, dst, self.s5.at[0], rsem, s, (z + 1) % 4).wait_recv()

    def to_twin(self, a, b):
        _, _, c, x, y = place()
        k = (a % 4) * 4 + b % 4
        self.start(self.at(a, b), self.s5.at[k], self.r5.at[k], seq_at(y, x, 1 - c))

    def send_part(self, a, b, part, side, sems, nbr):
        ssem, rsem = sems
        self.start(self.at(a, b, part), ssem.at[side, part], rsem.at[side, part], nbr(1 - 2 * side))

    def first_sends(self, a, b, sems, nbr):
        self.send_part(a, b, 0, 0, sems, nbr)
        self.send_part(a, b, 1, 1, sems, nbr)
        self.send_part(a, b, 1, 0, sems, nbr)
        self.send_part(a, b, 0, 1, sems, nbr)

    def b_sends(self, a):
        k = a % 4
        self.first_sends(a, 0, (self.s3.at[k], self.r3.at[k]), self.nbr_b)

    def b_relay(self, a):
        k = a % 4
        self.got(self.at(a, -1, 0), self.r3.at[k, 0, 0])
        self.start(self.at(a, -1, 0), self.s4.at[k, 0], self.r4.at[k, 0], self.nbr_b(1))
        self.got(self.at(a, 1, 1), self.r3.at[k, 1, 1])
        self.start(self.at(a, 1, 1), self.s4.at[k, 1], self.r4.at[k, 1], self.nbr_b(-1))

    def b_rest(self, a):
        k = a % 4
        self.got(self.at(a, -1, 1), self.r3.at[k, 0, 1])
        self.to_twin(a, -1)
        self.got(self.at(a, 1, 0), self.r3.at[k, 1, 0])
        self.to_twin(a, 1)

    def step0(self):
        s, z, _, _, _ = place()
        mine = self.full.at[2 * s + z // 2, pl.ds(pl.multiple_of((z % 2) * 32, 32), 32)]
        self.local = pltpu.make_async_copy(self.cache_ref, mine, self.lsem)
        self.local.start()
        self.zc = [
            rcopy(self.cache_ref, mine, self.zs.at[d - 1], self.zr.at[d - 1], s, (z + d) % 4) for d in (1, 2, 3)
        ]
        for q in self.zc:
            q.start()
        self.pend += self.zc

    def step1(self):
        self.local.wait()
        for q in self.zc:
            q.wait_recv()
        self.first_sends(0, 0, (self.s1, self.r1), self.nbr_a)
        self.b_sends(0)
        self.to_twin(0, 0)

    def step2(self):
        self.got(self.at(-1, 0, 0), self.r1.at[0, 0])
        self.start(self.at(-1, 0, 0), self.s2.at[0], self.r2.at[0], self.nbr_a(1))
        self.got(self.at(1, 0, 1), self.r1.at[1, 1])
        self.start(self.at(1, 0, 1), self.s2.at[1], self.r2.at[1], self.nbr_a(-1))
        self.got(self.at(-1, 0, 1), self.r1.at[0, 1])
        self.got(self.at(1, 0, 0), self.r1.at[1, 0])
        self.b_sends(-1)
        self.b_sends(1)
        self.to_twin(-1, 0)
        self.to_twin(1, 0)

    def step3(self):
        self.b_relay(0)
        self.got(self.at(2, 0, 0), self.r2.at[0])
        self.got(self.at(2, 0, 1), self.r2.at[1])
        self.b_sends(2)
        self.b_rest(0)
        self.to_twin(2, 0)

    def step4(self):
        for a in (-1, 1):
            self.b_relay(a)

    def step5(self):
        for a in (-1, 1):
            self.b_rest(a)
        self.b_relay(2)

    def step6(self):
        self.b_rest(2)
        for a in (0, -1, 1, 2):
            k = a % 4
            self.got(self.at(a, 2, 0), self.r4.at[k, 0])
            self.got(self.at(a, 2, 1), self.r4.at[k, 1])
            self.to_twin(a, 2)

    def step7(self):
        _, _, c, x, y = place()
        for a in range(4):
            for b in range(4):
                t = seq_at((y + a * (1 - c) + b * c) % 4, (x + a * c + b * (1 - c)) % 4, 1 - c)
                self.got(self.block(t, None), self.r5.at[a * 4 + b])
        for q in self.pend:
            q.wait_send()


GATHER_SCRATCH = [pltpu.VMEM((64, BLK, KV), BF), pltpu.SemaphoreType.DMA] + [
    pltpu.SemaphoreType.DMA(shape)
    for shape in ((3,), (3,), (2, 2), (2, 2), (2,), (2,), (4, 2, 2), (4, 2, 2), (4, 2), (4, 2), (16,), (16,))
]


def cache_stages(inv, flag, gk, gc, zr1, zr2, rz, send, recv, part, zss, zrs, xss, xrs, fss, frs):
    s, z, c, x, y = place()
    z1, z2, z3 = (z + 1) % 4, (z + 2) % 4, (z + 3) % 4

    def quarter(b, n, q):
        return gk.at[pl.ds(b, n), pl.ds(pl.multiple_of(q * 16, 16), 16)]

    def first(u):
        b = 8 * u
        return [
            rcopy(quarter(b, 4, z2), zr1.at[u, 0], zss.at[u, 0, 0], zrs.at[u, 0, 0], s, z1),
            rcopy(quarter(b + 4, 4, z2), zr1.at[u, 1], zss.at[u, 0, 1], zrs.at[u, 0, 1], s, z3),
        ]

    def second(u):
        b = 8 * u
        return [
            rcopy(quarter(b, 8, z1), zr2.at[u, 0], zss.at[u, 1, 0], zrs.at[u, 1, 0], s, z1),
            rcopy(quarter(b, 8, z3), zr2.at[u, 1], zss.at[u, 1, 1], zrs.at[u, 1, 1], s, z3),
        ]

    def head_send(u):
        for q in first(u):
            q.start()

    def head_relay(u):
        b = 8 * u
        for q in first(u):
            q.wait()
        for r, b0, q in ((zr1.at[u, 0], b, z1), (zr1.at[u, 1], b + 4, z3)):
            t = quarter(b0, 4, q)
            t[...] = (t[...].astype(F32) + r[...].astype(F32)).astype(BF)
        for q in second(u):
            q.start()

    def head_sum(u):
        for q in second(u):
            q.wait()
        t = quarter(8 * u, 8, z)[...].astype(F32) + zr2[u, 0].astype(F32) + zr2[u, 1].astype(F32)
        rz[u // 2, 8 * (u % 2) : 8 * (u % 2) + 8] = t.astype(BF)
        if u % 2:
            rz[u // 2, 16] = jnp.zeros((16, KV), BF)

    def packed(t):
        v = rz[0, inv[0, t]].astype(F32) + rz[1, inv[1, t]].astype(F32)
        mark = jnp.zeros((16, KP - KV), F32) + flag[t].astype(F32)
        return jnp.concatenate([v, mark], 1).astype(BF)

    def message(d):
        return rcopy(send.at[d], recv.at[d], xss.at[d], xrs.at[d], (s + d) % 32, z)

    def spread():
        for d in range(32):
            send[d] = packed((s + d) % 32)

        def one(d, _):
            @pl.when(s + d >= 32)
            def _():
                message(d).start()

            return 0

        lax.fori_loop(1, 32, one, 0)

    def last(b):
        h = 2 * b + z // 2
        return h, rcopy(part.at[b], part.at[2 + z % 2], fss.at[b], frs.at[z % 2], s, h)

    def collect():
        def one(d, _):
            @pl.when(d > s)
            def _():
                message(d).wait_recv()

            @pl.when(s + d >= 32)
            def _():
                message(d).wait_send()

            return 0

        lax.fori_loop(1, 32, one, 0)
        first = rz[0, 0].astype(F32)
        other = rz[1, 0].astype(F32)
        for d in range(32):
            v = (recv[d] if d else send[0]).astype(F32)
            if d:
                v = jnp.where(d > s, v, 0.0)
            v, mark = v[:, :KV], v[:, KV : KV + 1]
            moved = v * mark
            other = other + moved
            first = first + (v - moved)
        part[0] = first
        part[1] = other
        for b in range(2):
            h, q = last(b)

            @pl.when(h != z)
            def _():
                q.start()

    def finish():
        for i in range(2):
            src = 2 * (z % 2) + i

            @pl.when(src == z)
            def _():
                gc[16 * i : 16 * i + 16] = part[z // 2]

            @pl.when(src != z)
            def _():
                rcopy(part.at[2 + i], part.at[2 + i], fss.at[0], frs.at[i], s, (z + 1) % 4).wait_recv()
                gc[16 * i : 16 * i + 16] = part[2 + i]

        for b in range(2):
            h, q = last(b)

            @pl.when(h != z)
            def _():
                q.wait_send()

    return head_send, head_relay, head_sum, spread, collect, finish


CACHE_SCRATCH = [
    pltpu.VMEM((4, 2, 4, 16, KV), BF),
    pltpu.VMEM((4, 2, 8, 16, KV), BF),
    pltpu.VMEM((2, 17, 16, KV), BF),
    pltpu.VMEM((32, 16, KP), BF),
    pltpu.VMEM((32, 16, KP), BF),
    pltpu.VMEM((4, 16, KV), F32),
    pltpu.SemaphoreType.DMA((4, 2, 2)),
    pltpu.SemaphoreType.DMA((4, 2, 2)),
    pltpu.SemaphoreType.DMA((32,)),
    pltpu.SemaphoreType.DMA((32,)),
    pltpu.SemaphoreType.DMA((2,)),
    pltpu.SemaphoreType.DMA((2,)),
]

PHASES = [("fwd", 8, 2.3), ("ds0", 2, 1.3), ("kv0", 4, 1.3), ("ds1", 2, 1.3), ("kv1", 4, 1.3), ("dq", 4, 1.5)]
UV_GAPS = [0.0, 4.8, 7.8, 4.8, 4.8, 7.8, 4.8]
HEAD_GAPS = [5.1, 6.8]
END_GAPS = [0.1, 8.0, 2.5]


def plan():
    ends, now = [], 0.0
    for name, n, us in PHASES:
        for i in range(n):
            now += us
            ends.append((now, name, i))
    when = {(name, i): t for t, name, i in ends}
    todo = []
    for k in range(NCH):
        t = when["fwd", 8 // NCH * (k + 1) - 1]
        for st in range(UV_STAGES):
            t += UV_GAPS[st]
            todo.append((t, "uv", (k, st)))
    for u in range(4):
        t = when["kv%d" % (u // 2), 2 * (u % 2) + 1]
        todo.append((t, "head_send", (u,)))
        todo.append((t + HEAD_GAPS[0], "head_relay", (u,)))
        t += sum(HEAD_GAPS)
        todo.append((t, "head_sum", (u,)))
    for op, gap in zip(("spread", "collect", "finish"), END_GAPS):
        t += gap
        todo.append((t, op, ()))
    todo.sort(key=lambda e: e[0])
    at, late = {}, []
    for t, op, arg in todo:
        for end, name, i in ends:
            if end >= t - 1e-6:
                at.setdefault((name, i), []).append((op, arg))
                break
        else:
            late.append((op, arg))
    return at, late


def fused_body(lists, cache, qt, w_hbm, gout_hbm, ho_hbm, dq_hbm, uv_hbm, gc, *scr):
    (qg, k, kt, mask, pt, do, cen, ot, sa, sb, u, w, gout, hb, qb, inv, flag,
     lsem, hsem, qsem, osem) = scr[:21]
    scr = scr[21:]
    gat = Gather(cache, *scr[: len(GATHER_SCRATCH)])
    full = gat.full
    scr = scr[len(GATHER_SCRATCH) :]
    stage = uv_stages(u, *scr[: len(UV_SCRATCH)])
    gk = full
    cs = cache_stages(inv, flag, gk, gc, *scr[len(UV_SCRATCH) :])
    head_send, head_relay, head_sum, spread, collect, finish = cs
    s, z, c, x, y = place()

    barrier = pltpu.get_barrier_semaphore()
    for d in range(1, 32):
        pl.semaphore_signal(barrier, inc=1, device_id=((s + d) % 32, z), device_id_type=MESH)
    for d in range(1, 4):
        pl.semaphore_signal(barrier, inc=1, device_id=(s, (z + d) % 4), device_id_type=MESH)

    def q_load(i, slot):
        return pltpu.make_async_copy(qt.at[pl.ds(8 * i, 8)], qb.at[slot], qsem.at[slot])

    g_load = pltpu.make_async_copy(gout_hbm, u.at[0], lsem.at[1])
    w_load = pltpu.make_async_copy(w_hbm, w, lsem.at[0])
    g_load.start()
    q_load(0, 0).start()
    q_load(1, 1).start()
    w_load.start()

    r = lax.broadcasted_iota(jnp.int32, (BLK, WIDE), 0)
    cc = lax.broadcasted_iota(jnp.int32, (BLK, WIDE), 1)
    mask[...] = jnp.where(r <= (cc % BLK), 0.0, NEG).astype(F32)
    row = lax.broadcasted_iota(jnp.int32, (64, ROWS), 0)
    one = jnp.where(row == 0, 1.0, 0.0).astype(BF)
    qg[0, KV:, :] = one
    qg[1, KV:, :] = one
    pl.semaphore_wait(barrier, 34)
    gat.step0()

    def find(t, _):
        which = jnp.int32(0)
        for g in range(2):
            slot = jnp.int32(16)
            for j in range(KEEP):
                d = lists[g, j] - 2 * t
                hit = (d >= 0) & (d < 2)
                slot = jnp.where(hit, j + 1, slot)
                which = jnp.where(hit, d, which)
            inv[g, t] = slot
        flag[t] = which
        return 0

    g_load.wait()

    def turn(i, _):
        t = pl.ds(pl.multiple_of(i * 16, 16), 16)
        x = u[0, pl.ds(pl.multiple_of(i * 512, 512), 512)].reshape(16, NH, VH)
        gout[:, t, :] = jnp.swapaxes(x, 0, 1)
        return 0

    lax.fori_loop(0, TD // 16, turn, 0)
    lax.fori_loop(0, 32, find, 0)
    gat.step1()

    def prep_q(lo, hi):
        def body(i, _):
            q_load(i, i % 2).wait()
            for p in range(4):
                a, b = halves(qb[i % 2, 2 * p], qb[i % 2, 2 * p + 1])
                col = pl.ds(pl.multiple_of(i * WIDE + p * 128, 128), 128)
                qg[0, :KV, col] = a
                qg[1, :KV, col] = b

            @pl.when(i + 2 < 4)
            def _():
                q_load(i + 2, i % 2).start()

            return 0

        lax.fori_loop(lo, hi, body, 0)

    def prep_do(lo, hi):
        def body(i, _):
            for p in range(4):
                h = 8 * i + 2 * p
                d0 = lax.dot_general(w[h], gout[h], NTD, preferred_element_type=F32).astype(BF)
                d1 = lax.dot_general(w[h + 1], gout[h + 1], NTD, preferred_element_type=F32).astype(BF)
                a, b = halves(d0, d1)
                col = pl.ds(pl.multiple_of(i * WIDE + p * 128, 128), 128)
                do[0, :, col] = a
                do[1, :, col] = b
            return 0

        lax.fori_loop(lo, hi, body, 0)

    prep_q(0, 2)
    gat.step2()
    prep_q(2, 3)
    gat.step3()
    prep_q(3, 4)
    gat.step4()
    w_load.wait()
    prep_do(0, 2)
    gat.step5()
    prep_do(2, 4)
    gat.step6()
    gat.step7()

    colid = lax.broadcasted_iota(jnp.int32, (BLK, KP - DL), 1)
    for g in range(2):
        for j in range(SLOTS):
            if j == 0:
                blk = full[2 * s + g]
                bias = jnp.float32(0.0)
            else:
                e = lists[g, j - 1]
                blk = full[jnp.maximum(e, 0)]
                bias = jnp.where(e >= 0, 0.0, NEG).astype(F32)
            k[g, j * BLK : (j + 1) * BLK, :DL] = blk[:, :DL]
            rot = jnp.concatenate([blk[:, DL:].astype(F32), jnp.zeros((BLK, 64), F32)], 1)
            k[g, j * BLK : (j + 1) * BLK, DL:] = jnp.where(colid == 64, bias, rot).astype(BF)
        for b in range(8):
            t = jnp.swapaxes(k[g, b * 128 : (b + 1) * 128, :], 0, 1)
            kt[g, :, b * 128 : (b + 1) * 128] = t[:KV]

    uv_out = [pltpu.make_async_copy(u.at[q], uv_hbm.at[q], osem.at[q]) for q in range(NCH)]

    def run(op, arg):
        if op == "uv":
            stage(*arg)
            if arg[1] == UV_STAGES - 1:
                uv_out[arg[0]].start()
        else:
            ops = {"head_send": head_send, "head_relay": head_relay, "head_sum": head_sum}
            ops.update({"spread": spread, "collect": collect, "finish": finish})
            ops[op](*arg)

    at, late = plan()
    steps = {p[0]: p[1] for p in PHASES}

    def hook(name, i, part=0, parts=1):
        for j in range(part, steps[name], parts):
            if (name, j) in at:

                @pl.when(i == j // parts)
                def _():
                    for op, arg in at[name, j]:
                        run(op, arg)

    def loop(name, body, parts=1):
        def step(i, _):
            body(i)
            hook(name, i, parts - 1, parts)
            return 0

        lax.fori_loop(0, steps[name] // parts, step, 0)

    def cols(i, n=WIDE):
        return pl.ds(pl.multiple_of(i * n, n), n)

    def ho_store(i, slot):
        return pltpu.make_async_copy(hb.at[slot], ho_hbm.at[pl.ds(8 * i, 8)], hsem.at[slot])

    def scores(to, g, i):
        to[...] = jnp.dot(k[g], qg[g, :, cols(i)], preferred_element_type=F32)

    def softmax(sc, g, col):
        sc[:BLK] = sc[:BLK] + mask[...]
        m = jnp.max(sc[...], axis=0, keepdims=True)
        total = jnp.zeros((8, WIDE), F32)
        for b in range(16):
            e = jnp.exp2((sc[b * 64 : (b + 1) * 64] - m) * (SC * L2E))
            total = total + jnp.sum(e.reshape(8, 8, WIDE), axis=0)
            pt[g, b * 64 : (b + 1) * 64, col] = e.astype(BF)
        return 1.0 / jnp.sum(total, axis=0, keepdims=True)

    def values(g, col, inv_l):
        o = jnp.dot(kt[g, :DL, :], pt[g, :, col], preferred_element_type=F32) * inv_l
        ot[g] = o.astype(BF)
        dn = (do[g, :, col].astype(F32) * inv_l).astype(BF)
        do[g, :, col] = dn
        centre = jnp.sum(o * dn.astype(F32), axis=0, keepdims=True)
        cen[g, :, col] = jnp.broadcast_to(centre, (8, WIDE))

    scores(sa, 0, 0)

    def fwd(i):
        col = cols(i)
        scores(sb, 1, i)
        values(0, col, softmax(sa, 0, col))
        hook("fwd", i, 0, 2)
        scores(sa, 0, jnp.minimum(i + 1, 3))
        values(1, col, softmax(sb, 1, col))

        @pl.when(i >= 2)
        def _():
            ho_store(i - 2, i % 2).wait()

        for p in range(4):
            hh = halves(ot[0, :, p * 128 : (p + 1) * 128], ot[1, :, p * 128 : (p + 1) * 128])
            for q in range(2):
                h = 2 * p + q
                part = jnp.dot(hh[q], gout[8 * i + h], preferred_element_type=F32).astype(BF)
                u[i, h * DL : (h + 1) * DL] = part
                hb[i % 2, h] = lax.dot_general(hh[q], w[8 * i + h], TND, preferred_element_type=F32).astype(BF)
        ho_store(i, i % 2).start()

    loop("fwd", fwd, 2)
    ho_store(2, 0).wait()
    ho_store(3, 1).wait()

    def back_ds(g, to):
        def body(i):
            for b, tmp in enumerate((sa, sb)):
                col = cols(2 * i + b)
                tmp[...] = jnp.dot(k[g, :, :DL], do[g, :, col], preferred_element_type=F32)
            for b, tmp in enumerate((sa, sb)):
                col = cols(2 * i + b)
                for q in range(8):
                    rows = slice(q * 128, (q + 1) * 128)
                    t = pt[g, rows, col].astype(F32) * (tmp[rows] - cen[g, 0:1, col])
                    pt[to, rows, col] = t.astype(BF)

        return body

    def back_kv(g, d):
        def body(i):
            rows = cols(i)
            sa[:KV] = lax.dot_general(qg[g, :KV, :], pt[d, rows, :], NTD, preferred_element_type=F32)
            hook("kv%d" % g, i, 0, 2)
            sb[:DL] = lax.dot_general(do[g], pt[g, rows, :], NTD, preferred_element_type=F32)
            zero = jnp.zeros((KP - KV, WIDE), F32)
            t = jnp.concatenate([sa[:DL] * SC + sb[:DL], sa[DL:KV] * SC, zero], 0).astype(BF)
            t = jnp.swapaxes(t, 0, 1)
            gk[pl.ds(16 * g + 8 * i, 8)] = t[:, :KV].reshape(8, BLK, KV)

        return body

    loop("ds0", back_ds(0, 2))
    loop("kv0", back_kv(0, 2), 2)
    loop("ds1", back_ds(1, 0))
    loop("kv1", back_kv(1, 0), 2)

    def dq_store(i, slot):
        return pltpu.make_async_copy(qb.at[slot], dq_hbm.at[pl.ds(8 * i, 8)], qsem.at[slot])

    def back_q(i):
        col = cols(i)

        @pl.when(i >= 2)
        def _():
            dq_store(i - 2, i % 2).wait()

        r = []
        for g, d in ((0, 2), (1, 0)):
            r.append((jnp.dot(kt[g], pt[d, :, col], preferred_element_type=F32) * SC).astype(BF))
        for p in range(4):
            a, b = halves(r[0][:, p * 128 : (p + 1) * 128], r[1][:, p * 128 : (p + 1) * 128])
            qb[i % 2, 2 * p] = a
            qb[i % 2, 2 * p + 1] = b
        dq_store(i, i % 2).start()

    loop("dq", back_q)
    for op, arg in late:
        run(op, arg)
    dq_store(2, 0).wait()
    dq_store(3, 1).wait()
    for q in uv_out:
        q.wait()


def attention(lists, cache, qt, w, gout):
    v = pl.BlockSpec(memory_space=pltpu.VMEM)
    m = pl.BlockSpec(memory_space=pltpu.SMEM)
    a = pl.BlockSpec(memory_space=pl.ANY)
    scratch = [
        pltpu.VMEM((2, KP, ROWS), BF),
        pltpu.VMEM((2, KEYS, KP), BF),
        pltpu.VMEM((2, KV, KEYS), BF),
        pltpu.VMEM((BLK, WIDE), F32),
        pltpu.VMEM((3, KEYS, ROWS), BF),
        pltpu.VMEM((2, DL, ROWS), BF),
        pltpu.VMEM((2, 8, ROWS), F32),
        pltpu.VMEM((2, DL, WIDE), BF),
        pltpu.VMEM((KEYS, WIDE), F32),
        pltpu.VMEM((KEYS, WIDE), F32),
        pltpu.VMEM((NCH, CROWS, 128), BF),
        pltpu.VMEM((NH, DL, VH), BF),
        pltpu.VMEM((NH, TD, VH), BF),
        pltpu.VMEM((2, 8, TD, VH), BF),
        pltpu.VMEM((2, 8, KV, TD), BF),
        pltpu.SMEM((2, 32), jnp.int32),
        pltpu.SMEM((32,), jnp.int32),
        pltpu.SemaphoreType.DMA((2,)),
        pltpu.SemaphoreType.DMA((2,)),
        pltpu.SemaphoreType.DMA((2,)),
        pltpu.SemaphoreType.DMA((NCH,)),
    ]
    return pl.pallas_call(
        fused_body,
        out_shape=(
            jax.ShapeDtypeStruct((NH, TD, VH), BF),
            jax.ShapeDtypeStruct((NH, KV, TD), BF),
            jax.ShapeDtypeStruct((NCH, CROWS, 128), BF),
            jax.ShapeDtypeStruct((32, KV), F32),
        ),
        in_specs=[m, v, a, a, a],
        out_specs=(a, a, a, v),
        scratch_shapes=scratch + GATHER_SCRATCH + UV_SCRATCH + CACHE_SCRATCH,
        compiler_params=pltpu.CompilerParams(
            collective_id=0, has_side_effects=True, vmem_limit_bytes=VMEM_LIMIT
        ),
        name="latent_attention",
    )(lists, cache, qt, w, gout)


def hand_on_body(ho, dq, uv, gc, ho_out, dq_out, uv_out, gc_out, vh, vt, vq, vu, vg, si, so):
    def part(ref, i):
        return ref.at[pl.ds(8 * i, 8)]

    gc_in = pltpu.make_async_copy(gc, vg, si.at[3, 0])
    gc_copy = pltpu.make_async_copy(vg, gc_out, so.at[3, 0])
    ins, outs = [], []
    for i in range(4):
        ins.append(pltpu.make_async_copy(part(ho, i), part(vh, i), si.at[0, i]))
    for i in range(4):
        ins.append(pltpu.make_async_copy(part(dq, i), part(vq, i), si.at[1, i]))
        outs.append(pltpu.make_async_copy(part(vq, i), part(dq_out, i), so.at[1, i]))
        ins.append(pltpu.make_async_copy(part(uv, i), part(vu, i), si.at[2, i]))
        outs.append(pltpu.make_async_copy(part(vu, i), part(uv_out, i), so.at[2, i]))
    gc_in.start()
    for q in ins:
        q.start()
    gc_in.wait()
    gc_copy.start()
    for q in ins[:4]:
        q.wait()
    turns = []
    for i in range(4):
        for q, out in zip(ins[4 + 2 * i : 6 + 2 * i], outs[2 * i : 2 * i + 2]):
            q.wait()
            out.start()
        t = pl.ds(32 * i, 32)
        vt[t] = jnp.swapaxes(vh[:, t, :], 0, 1)
        turns.append(pltpu.make_async_copy(vt.at[t], ho_out.at[t], so.at[0, i]))
        turns[-1].start()
    for q in outs + turns:
        q.wait()
    gc_copy.wait()


def hand_on(ho, dq, uv, gc):
    a = pl.BlockSpec(memory_space=pl.ANY)
    return pl.pallas_call(
        hand_on_body,
        out_shape=(
            jax.ShapeDtypeStruct((TD, NH, VH), BF),
            jax.ShapeDtypeStruct((NH, KV, TD), BF),
            jax.ShapeDtypeStruct((NH, DL, VH), BF),
            jax.ShapeDtypeStruct((32, KV), F32),
        ),
        in_specs=[a] * 4,
        out_specs=(a,) * 4,
        scratch_shapes=[
            pltpu.VMEM((NH, TD, VH), BF),
            pltpu.VMEM((TD, NH, VH), BF),
            pltpu.VMEM((NH, KV, TD), BF),
            pltpu.VMEM((NH, DL, VH), BF),
            pltpu.VMEM((32, KV), F32),
            pltpu.SemaphoreType.DMA((4, 4)),
            pltpu.SemaphoreType.DMA((4, 4)),
        ],
        compiler_params=pltpu.CompilerParams(vmem_limit_bytes=VMEM_LIMIT),
        name="hand_on",
    )(ho, dq, uv, gc)


def on_device(queries, cache, lists, w_uv, grad_out):
    ho, dq, uv, gc = attention(
        lists, cache, queries.transpose(1, 2, 0), w_uv, grad_out.reshape(TD * NH, VH)
    )
    ho, dq, uv, gc = hand_on(ho, dq, uv.reshape(NH, DL, VH), gc)
    return ho, dq.transpose(2, 0, 1), gc, uv


def solution(mesh):
    return jax.shard_map(
        on_device,
        mesh=mesh,
        in_specs=(
            P("seq", "head", None),
            P(("seq", "head"), None),
            P("seq", None),
            P("head", None, None),
            P("seq", "head", None),
        ),
        out_specs=(
            P("seq", "head", None),
            P("seq", "head", None),
            P(("seq", "head"), None),
            P("head", None, None),
        ),
        check_vma=False,
    )
```

```python
import functools, jax, jax.numpy as jnp, numpy as np
from jax import lax
from jax.experimental import pallas as pl
from jax.experimental.pallas import tpu as pltpu
from jax.sharding import PartitionSpec as P

BLK=64; KEEP=15; SLOTS=16; KEYS=1024; DL=512; KV=576; KP=640; NH=32; VH=128; TD=128
ROWS=2048; TILE=256; NT=8
SC=192.0**-0.5
L2E=1.4426950408889634
NEG=-1e30
F32=jnp.float32; BF=jnp.bfloat16
NTD=(((1,),(1,)),((),()))
TND=(((0,),(0,)),((),()))

def halves(a,b):
    return (jnp.concatenate([a[:, :64], b[:, :64]],1), jnp.concatenate([a[:, 64:], b[:, 64:]],1))

def make_mask(mask_ref):
    r=lax.broadcasted_iota(jnp.int32,(BLK,TILE),0)
    c=lax.broadcasted_iota(jnp.int32,(BLK,TILE),1)
    mask_ref[...]=jnp.where(r<=(c%BLK),0.0,NEG).astype(F32)

MESH = pl.DeviceIdType.MESH
NCH = 4
CROWS = NH * DL // NCH
CH = CROWS // 2
QA = CH // 4
QB = QA // 4


def place():
    s = lax.axis_index("seq")
    z = lax.axis_index("head")
    return s, z, s % 2, (s // 2) % 4, s // 8


def seq_at(y, x, c):
    return (y * 4 + x) * 2 + c


def rcopy(src, dst, ssem, rsem, s, z):
    return pltpu.make_async_remote_copy(
        src_ref=src, dst_ref=dst, send_sem=ssem, recv_sem=rsem, device_id=(s, z), device_id_type=MESH
    )


def greet(seq_steps, head_steps):
    s, z, _, _, _ = place()
    barrier = pltpu.get_barrier_semaphore()
    for d in seq_steps:
        pl.semaphore_signal(barrier, inc=1, device_id=((s + d) % 32, z), device_id_type=MESH)
    for d in head_steps:
        pl.semaphore_signal(barrier, inc=1, device_id=(s, (z + d) % 4), device_id_type=MESH)
    pl.semaphore_wait(barrier, len(seq_steps) + len(head_steps))


def uv_stages(u, rc, ra, rb, ri, ss, rs):
    s, z, c, x, y = place()
    twin = seq_at(y, x, 1 - c)
    pa = x * (1 - c) + y * c
    pb = y * (1 - c) + x * c
    base = c * CH

    def nbr_a(d):
        return seq_at((y + d * c) % 4, (x + d * (1 - c)) % 4, c)

    def nbr_b(d):
        return seq_at((y + d * (1 - c)) % 4, (x + d * c) % 4, c)

    def ds(start, size):
        return pl.ds(pl.multiple_of(start, size), size)

    def add(terms):
        t = terms[0][...].astype(F32)
        for r in terms[1:]:
            t = t + r[...].astype(F32)
        return t.astype(BF)

    def quarter_a(k, q):
        return u.at[k, ds(base + q % 4 * QA, QA)]

    def quarter_b(k, q):
        return u.at[k, ds(base + pa * QA + q % 4 * QB, QB)]

    def half(k, h):
        return u.at[k, ds(h * CH, CH)]

    def copies(k, st):
        if st == 0:
            return [(half(k, 1 - c), rc.at[k], twin)]
        if st == 1:
            return [(rc.at[k, ds((pa + d) % 4 * QA, QA)], ra.at[k, d - 1], nbr_a(d)) for d in (1, 2, 3)]
        if st == 2:
            return [(rb.at[k, ds((pb + d) % 4 * QB, QB)], ri.at[k, d - 1], nbr_b(d)) for d in (1, 2, 3)]
        if st == 3:
            return [(quarter_b(k, pb), quarter_b(k, pb), nbr_b(d)) for d in (1, 2, 3)]
        if st == 4:
            return [(quarter_a(k, pa), quarter_a(k, pa), nbr_a(d)) for d in (1, 2, 3)]
        return [(half(k, c), half(k, c), twin)]

    def landed(k, st):
        if st == 3:
            return [quarter_b(k, pb + 4 - d) for d in (1, 2, 3)]
        if st == 4:
            return [quarter_a(k, pa + 4 - d) for d in (1, 2, 3)]
        if st == 5:
            return [half(k, 1 - c)]
        return [q[1] for q in copies(k, st)]

    def stage(k, st):
        if st > 0:
            for i, dst in enumerate(landed(k, st - 1)):
                rcopy(dst, dst, ss.at[k, st - 1, i], rs.at[k, st - 1, i], twin, z).wait_recv()
            for i, (src, dst, to) in enumerate(copies(k, st - 1)):
                rcopy(src, dst, ss.at[k, st - 1, i], rs.at[k, st - 1, i], to, z).wait_send()
        if st == 1:
            rc[k] = add([half(k, c), rc.at[k]])
        elif st == 2:
            rb[k] = add([rc.at[k, ds(pa * QA, QA)]] + [ra.at[k, d] for d in range(3)])
        elif st == 3:
            quarter_b(k, pb)[...] = add([rb.at[k, ds(pb * QB, QB)]] + [ri.at[k, d] for d in range(3)])
        if st < UV_STAGES - 1:
            for i, (src, dst, to) in enumerate(copies(k, st)):
                rcopy(src, dst, ss.at[k, st, i], rs.at[k, st, i], to, z).start()

    return stage


UV_STAGES = 7
UV_SCRATCH = [
    pltpu.VMEM((NCH, CH, 128), BF),
    pltpu.VMEM((NCH, 3, QA, 128), BF),
    pltpu.VMEM((NCH, QA, 128), BF),
    pltpu.VMEM((NCH, 3, QB, 128), BF),
    pltpu.SemaphoreType.DMA((NCH, UV_STAGES - 1, 3)),
    pltpu.SemaphoreType.DMA((NCH, UV_STAGES - 1, 3)),
]


VMEM_LIMIT = 63 * 2**20
WIDE = 512


class Gather:
    def __init__(self, cache_ref, full, lsem, zs, zr, s1, r1, s2, r2, s3, r3, s4, r4, s5, r5):
        self.__dict__.update(locals())
        self.pend = []

    def at(self, a, b, part=None):
        _, _, c, x, y = place()
        t = seq_at((y + a * c + b * (1 - c)) % 4, (x + a * (1 - c) + b * c) % 4, c)
        return self.block(t, part)

    def block(self, t, part):
        if part is None:
            return self.full.at[pl.ds(2 * t, 2)]
        return self.full.at[2 * t + part]

    def nbr_a(self, d):
        _, _, c, x, y = place()
        return seq_at((y + d * c) % 4, (x + d * (1 - c)) % 4, c)

    def nbr_b(self, d):
        _, _, c, x, y = place()
        return seq_at((y + d * (1 - c)) % 4, (x + d * c) % 4, c)

    def start(self, src, ssem, rsem, dev):
        q = rcopy(src, src, ssem, rsem, dev, place()[1])
        q.start()
        self.pend.append(q)

    def got(self, dst, rsem):
        s, z, _, _, _ = place()
        rcopy(dst, dst, self.s5.at[0], rsem, s, (z + 1) % 4).wait_recv()

    def to_twin(self, a, b):
        _, _, c, x, y = place()
        k = (a % 4) * 4 + b % 4
        self.start(self.at(a, b), self.s5.at[k], self.r5.at[k], seq_at(y, x, 1 - c))

    def send_part(self, a, b, part, side, sems, nbr):
        ssem, rsem = sems
        self.start(self.at(a, b, part), ssem.at[side, part], rsem.at[side, part], nbr(1 - 2 * side))

    def first_sends(self, a, b, sems, nbr):
        self.send_part(a, b, 0, 0, sems, nbr)
        self.send_part(a, b, 1, 1, sems, nbr)
        self.send_part(a, b, 1, 0, sems, nbr)
        self.send_part(a, b, 0, 1, sems, nbr)

    def b_sends(self, a):
        k = a % 4
        self.first_sends(a, 0, (self.s3.at[k], self.r3.at[k]), self.nbr_b)

    def b_relay(self, a):
        k = a % 4
        self.got(self.at(a, -1, 0), self.r3.at[k, 0, 0])
        self.start(self.at(a, -1, 0), self.s4.at[k, 0], self.r4.at[k, 0], self.nbr_b(1))
        self.got(self.at(a, 1, 1), self.r3.at[k, 1, 1])
        self.start(self.at(a, 1, 1), self.s4.at[k, 1], self.r4.at[k, 1], self.nbr_b(-1))

    def b_rest(self, a):
        k = a % 4
        self.got(self.at(a, -1, 1), self.r3.at[k, 0, 1])
        self.to_twin(a, -1)
        self.got(self.at(a, 1, 0), self.r3.at[k, 1, 0])
        self.to_twin(a, 1)

    def step0(self):
        s, z, _, _, _ = place()
        mine = self.full.at[2 * s + z // 2, pl.ds(pl.multiple_of((z % 2) * 32, 32), 32)]
        self.local = pltpu.make_async_copy(self.cache_ref, mine, self.lsem)
        self.local.start()
        self.zc = [
            rcopy(self.cache_ref, mine, self.zs.at[d - 1], self.zr.at[d - 1], s, (z + d) % 4) for d in (1, 2, 3)
        ]
        for q in self.zc:
            q.start()
        self.pend += self.zc

    def step1(self):
        self.local.wait()
        for q in self.zc:
            q.wait_recv()
        self.first_sends(0, 0, (self.s1, self.r1), self.nbr_a)
        self.b_sends(0)
        self.to_twin(0, 0)

    def step2(self):
        self.got(self.at(-1, 0, 0), self.r1.at[0, 0])
        self.start(self.at(-1, 0, 0), self.s2.at[0], self.r2.at[0], self.nbr_a(1))
        self.got(self.at(1, 0, 1), self.r1.at[1, 1])
        self.start(self.at(1, 0, 1), self.s2.at[1], self.r2.at[1], self.nbr_a(-1))
        self.got(self.at(-1, 0, 1), self.r1.at[0, 1])
        self.got(self.at(1, 0, 0), self.r1.at[1, 0])
        self.b_sends(-1)
        self.b_sends(1)
        self.to_twin(-1, 0)
        self.to_twin(1, 0)

    def step3(self):
        self.b_relay(0)
        self.got(self.at(2, 0, 0), self.r2.at[0])
        self.got(self.at(2, 0, 1), self.r2.at[1])
        self.b_sends(2)
        self.b_rest(0)
        self.to_twin(2, 0)

    def step4(self):
        for a in (-1, 1):
            self.b_relay(a)

    def step5(self):
        for a in (-1, 1):
            self.b_rest(a)
        self.b_relay(2)

    def step6(self):
        self.b_rest(2)
        for a in (0, -1, 1, 2):
            k = a % 4
            self.got(self.at(a, 2, 0), self.r4.at[k, 0])
            self.got(self.at(a, 2, 1), self.r4.at[k, 1])
            self.to_twin(a, 2)

    def step7(self):
        _, _, c, x, y = place()
        for a in range(4):
            for b in range(4):
                t = seq_at((y + a * (1 - c) + b * c) % 4, (x + a * c + b * (1 - c)) % 4, 1 - c)
                self.got(self.block(t, None), self.r5.at[a * 4 + b])
        for q in self.pend:
            q.wait_send()


GATHER_SCRATCH = [pltpu.VMEM((64, BLK, KV), BF), pltpu.SemaphoreType.DMA] + [
    pltpu.SemaphoreType.DMA(shape)
    for shape in ((3,), (3,), (2, 2), (2, 2), (2,), (2,), (4, 2, 2), (4, 2, 2), (4, 2), (4, 2), (16,), (16,))
]


def cache_stages(inv, flag, gk, gc, zr1, zr2, rz, send, recv, part, zss, zrs, xss, xrs, fss, frs):
    s, z, c, x, y = place()
    z1, z2, z3 = (z + 1) % 4, (z + 2) % 4, (z + 3) % 4

    def quarter(b, n, q):
        return gk.at[pl.ds(b, n), pl.ds(pl.multiple_of(q * 16, 16), 16)]

    def first(u):
        b = 8 * u
        return [
            rcopy(quarter(b, 4, z2), zr1.at[u, 0], zss.at[u, 0, 0], zrs.at[u, 0, 0], s, z1),
            rcopy(quarter(b + 4, 4, z2), zr1.at[u, 1], zss.at[u, 0, 1], zrs.at[u, 0, 1], s, z3),
        ]

    def second(u):
        b = 8 * u
        return [
            rcopy(quarter(b, 8, z1), zr2.at[u, 0], zss.at[u, 1, 0], zrs.at[u, 1, 0], s, z1),
            rcopy(quarter(b, 8, z3), zr2.at[u, 1], zss.at[u, 1, 1], zrs.at[u, 1, 1], s, z3),
        ]

    def head_send(u):
        for q in first(u):
            q.start()

    def head_relay(u):
        b = 8 * u
        for q in first(u):
            q.wait()
        for r, b0, q in ((zr1.at[u, 0], b, z1), (zr1.at[u, 1], b + 4, z3)):
            t = quarter(b0, 4, q)
            t[...] = (t[...].astype(F32) + r[...].astype(F32)).astype(BF)
        for q in second(u):
            q.start()

    def head_sum(u):
        for q in second(u):
            q.wait()
        t = quarter(8 * u, 8, z)[...].astype(F32) + zr2[u, 0].astype(F32) + zr2[u, 1].astype(F32)
        rz[u // 2, 8 * (u % 2) : 8 * (u % 2) + 8] = t.astype(BF)
        if u % 2:
            rz[u // 2, 16] = jnp.zeros((16, KV), BF)

    def packed(t):
        v = rz[0, inv[0, t]].astype(F32) + rz[1, inv[1, t]].astype(F32)
        mark = jnp.zeros((16, KP - KV), F32) + flag[t].astype(F32)
        return jnp.concatenate([v, mark], 1).astype(BF)

    def message(d):
        return rcopy(send.at[d], recv.at[d], xss.at[d], xrs.at[d], (s + d) % 32, z)

    def spread():
        for d in range(32):
            send[d] = packed((s + d) % 32)

        def one(d, _):
            @pl.when(s + d >= 32)
            def _():
                message(d).start()

            return 0

        lax.fori_loop(1, 32, one, 0)

    def last(b):
        h = 2 * b + z // 2
        return h, rcopy(part.at[b], part.at[2 + z % 2], fss.at[b], frs.at[z % 2], s, h)

    def collect():
        def one(d, _):
            @pl.when(d > s)
            def _():
                message(d).wait_recv()

            @pl.when(s + d >= 32)
            def _():
                message(d).wait_send()

            return 0

        lax.fori_loop(1, 32, one, 0)
        first = rz[0, 0].astype(F32)
        other = rz[1, 0].astype(F32)
        for d in range(32):
            v = (recv[d] if d else send[0]).astype(F32)
            if d:
                v = jnp.where(d > s, v, 0.0)
            v, mark = v[:, :KV], v[:, KV : KV + 1]
            moved = v * mark
            other = other + moved
            first = first + (v - moved)
        part[0] = first
        part[1] = other
        for b in range(2):
            h, q = last(b)

            @pl.when(h != z)
            def _():
                q.start()

    def finish():
        for i in range(2):
            src = 2 * (z % 2) + i

            @pl.when(src == z)
            def _():
                gc[16 * i : 16 * i + 16] = part[z // 2]

            @pl.when(src != z)
            def _():
                rcopy(part.at[2 + i], part.at[2 + i], fss.at[0], frs.at[i], s, (z + 1) % 4).wait_recv()
                gc[16 * i : 16 * i + 16] = part[2 + i]

        for b in range(2):
            h, q = last(b)

            @pl.when(h != z)
            def _():
                q.wait_send()

    return head_send, head_relay, head_sum, spread, collect, finish


CACHE_SCRATCH = [
    pltpu.VMEM((4, 2, 4, 16, KV), BF),
    pltpu.VMEM((4, 2, 8, 16, KV), BF),
    pltpu.VMEM((2, 17, 16, KV), BF),
    pltpu.VMEM((32, 16, KP), BF),
    pltpu.VMEM((32, 16, KP), BF),
    pltpu.VMEM((4, 16, KV), F32),
    pltpu.SemaphoreType.DMA((4, 2, 2)),
    pltpu.SemaphoreType.DMA((4, 2, 2)),
    pltpu.SemaphoreType.DMA((32,)),
    pltpu.SemaphoreType.DMA((32,)),
    pltpu.SemaphoreType.DMA((2,)),
    pltpu.SemaphoreType.DMA((2,)),
]

PHASES = [("fwd", 8, 2.3), ("ds0", 2, 1.3), ("kv0", 4, 1.3), ("ds1", 2, 1.3), ("kv1", 4, 1.3), ("dq", 4, 1.5)]
UV_GAPS = [0.0, 4.8, 7.8, 4.8, 4.8, 7.8, 4.8]
HEAD_GAPS = [5.1, 6.8]
END_GAPS = [0.1, 13.6, 4.3]


def plan():
    ends, now = [], 0.0
    for name, n, us in PHASES:
        for i in range(n):
            now += us
            ends.append((now, name, i))
    when = {(name, i): t for t, name, i in ends}
    todo = []
    for k in range(NCH):
        t = when["fwd", 8 // NCH * (k + 1) - 1]
        for st in range(UV_STAGES):
            t += UV_GAPS[st]
            todo.append((t, "uv", (k, st)))
    for u in range(4):
        t = when["kv%d" % (u // 2), 2 * (u % 2) + 1]
        todo.append((t, "head_send", (u,)))
        todo.append((t + HEAD_GAPS[0], "head_relay", (u,)))
        t += sum(HEAD_GAPS)
        todo.append((t, "head_sum", (u,)))
    for op, gap in zip(("spread", "collect", "finish"), END_GAPS):
        t += gap
        todo.append((t, op, ()))
    todo.sort(key=lambda e: e[0])
    at, late = {}, []
    for t, op, arg in todo:
        for end, name, i in ends:
            if end >= t - 1e-6:
                at.setdefault((name, i), []).append((op, arg))
                break
        else:
            late.append((op, arg))
    return at, late


def fused_body(lists, cache, qt, w_hbm, gout_hbm, ho_hbm, dq_hbm, uv_hbm, gc, *scr):
    (qg, k, kt, mask, pt, do, cen, ot, sa, sb, u, w, gout, hb, qb, inv, flag,
     lsem, hsem, qsem, osem) = scr[:21]
    scr = scr[21:]
    gat = Gather(cache, *scr[: len(GATHER_SCRATCH)])
    full = gat.full
    scr = scr[len(GATHER_SCRATCH) :]
    stage = uv_stages(u, *scr[: len(UV_SCRATCH)])
    gk = full
    cs = cache_stages(inv, flag, gk, gc, *scr[len(UV_SCRATCH) :])
    head_send, head_relay, head_sum, spread, collect, finish = cs
    s, z, c, x, y = place()

    barrier = pltpu.get_barrier_semaphore()
    for d in range(1, 32):
        pl.semaphore_signal(barrier, inc=1, device_id=((s + d) % 32, z), device_id_type=MESH)
    for d in range(1, 4):
        pl.semaphore_signal(barrier, inc=1, device_id=(s, (z + d) % 4), device_id_type=MESH)

    def q_load(i, slot):
        return pltpu.make_async_copy(qt.at[pl.ds(8 * i, 8)], qb.at[slot], qsem.at[slot])

    g_load = pltpu.make_async_copy(gout_hbm, u.at[0], lsem.at[1])
    w_load = pltpu.make_async_copy(w_hbm, w, lsem.at[0])
    g_load.start()
    q_load(0, 0).start()
    q_load(1, 1).start()
    w_load.start()

    r = lax.broadcasted_iota(jnp.int32, (BLK, WIDE), 0)
    cc = lax.broadcasted_iota(jnp.int32, (BLK, WIDE), 1)
    mask[...] = jnp.where(r <= (cc % BLK), 0.0, NEG).astype(F32)
    row = lax.broadcasted_iota(jnp.int32, (64, ROWS), 0)
    one = jnp.where(row == 0, 1.0, 0.0).astype(BF)
    qg[0, KV:, :] = one
    qg[1, KV:, :] = one
    pl.semaphore_wait(barrier, 34)
    gat.step0()

    def find(t, _):
        which = jnp.int32(0)
        for g in range(2):
            slot = jnp.int32(16)
            for j in range(KEEP):
                d = lists[g, j] - 2 * t
                hit = (d >= 0) & (d < 2)
                slot = jnp.where(hit, j + 1, slot)
                which = jnp.where(hit, d, which)
            inv[g, t] = slot
        flag[t] = which
        return 0

    g_load.wait()

    def turn(i, _):
        t = pl.ds(pl.multiple_of(i * 16, 16), 16)
        x = u[0, pl.ds(pl.multiple_of(i * 512, 512), 512)].reshape(16, NH, VH)
        gout[:, t, :] = jnp.swapaxes(x, 0, 1)
        return 0

    lax.fori_loop(0, TD // 16, turn, 0)
    lax.fori_loop(0, 32, find, 0)
    gat.step1()

    def prep_q(lo, hi):
        def body(i, _):
            q_load(i, i % 2).wait()
            for p in range(4):
                a, b = halves(qb[i % 2, 2 * p], qb[i % 2, 2 * p + 1])
                col = pl.ds(pl.multiple_of(i * WIDE + p * 128, 128), 128)
                qg[0, :KV, col] = a
                qg[1, :KV, col] = b

            @pl.when(i + 2 < 4)
            def _():
                q_load(i + 2, i % 2).start()

            return 0

        lax.fori_loop(lo, hi, body, 0)

    def prep_do(lo, hi):
        def body(i, _):
            for p in range(4):
                h = 8 * i + 2 * p
                d0 = lax.dot_general(w[h], gout[h], NTD, preferred_element_type=F32).astype(BF)
                d1 = lax.dot_general(w[h + 1], gout[h + 1], NTD, preferred_element_type=F32).astype(BF)
                a, b = halves(d0, d1)
                col = pl.ds(pl.multiple_of(i * WIDE + p * 128, 128), 128)
                do[0, :, col] = a
                do[1, :, col] = b
            return 0

        lax.fori_loop(lo, hi, body, 0)

    prep_q(0, 2)
    gat.step2()
    prep_q(2, 3)
    gat.step3()
    prep_q(3, 4)
    gat.step4()
    w_load.wait()
    prep_do(0, 2)
    gat.step5()
    prep_do(2, 4)
    gat.step6()
    gat.step7()

    colid = lax.broadcasted_iota(jnp.int32, (BLK, KP - DL), 1)
    for g in range(2):
        for j in range(SLOTS):
            if j == 0:
                blk = full[2 * s + g]
                bias = jnp.float32(0.0)
            else:
                e = lists[g, j - 1]
                blk = full[jnp.maximum(e, 0)]
                bias = jnp.where(e >= 0, 0.0, NEG).astype(F32)
            k[g, j * BLK : (j + 1) * BLK, :DL] = blk[:, :DL]
            rot = jnp.concatenate([blk[:, DL:].astype(F32), jnp.zeros((BLK, 64), F32)], 1)
            k[g, j * BLK : (j + 1) * BLK, DL:] = jnp.where(colid == 64, bias, rot).astype(BF)
        for b in range(8):
            t = jnp.swapaxes(k[g, b * 128 : (b + 1) * 128, :], 0, 1)
            kt[g, :, b * 128 : (b + 1) * 128] = t[:KV]

    uv_out = [pltpu.make_async_copy(u.at[q], uv_hbm.at[q], osem.at[q]) for q in range(NCH)]

    def run(op, arg):
        if op == "uv":
            stage(*arg)
            if arg[1] == UV_STAGES - 1:
                uv_out[arg[0]].start()
        else:
            ops = {"head_send": head_send, "head_relay": head_relay, "head_sum": head_sum}
            ops.update({"spread": spread, "collect": collect, "finish": finish})
            ops[op](*arg)

    at, late = plan()
    steps = {p[0]: p[1] for p in PHASES}

    def hook(name, i, part=0, parts=1):
        for j in range(part, steps[name], parts):
            if (name, j) in at:

                @pl.when(i == j // parts)
                def _():
                    for op, arg in at[name, j]:
                        run(op, arg)

    def loop(name, body, parts=1):
        def step(i, _):
            body(i)
            hook(name, i, parts - 1, parts)
            return 0

        lax.fori_loop(0, steps[name] // parts, step, 0)

    def cols(i, n=WIDE):
        return pl.ds(pl.multiple_of(i * n, n), n)

    def ho_store(i, slot):
        return pltpu.make_async_copy(hb.at[slot], ho_hbm.at[pl.ds(8 * i, 8)], hsem.at[slot])

    def scores(to, g, i):
        to[...] = jnp.dot(k[g], qg[g, :, cols(i)], preferred_element_type=F32)

    def softmax(sc, g, col):
        sc[:BLK] = sc[:BLK] + mask[...]
        m = jnp.max(sc[...], axis=0, keepdims=True)
        total = jnp.zeros((8, WIDE), F32)
        for b in range(16):
            e = jnp.exp2((sc[b * 64 : (b + 1) * 64] - m) * (SC * L2E))
            total = total + jnp.sum(e.reshape(8, 8, WIDE), axis=0)
            pt[g, b * 64 : (b + 1) * 64, col] = e.astype(BF)
        return 1.0 / jnp.sum(total, axis=0, keepdims=True)

    def values(g, col, inv_l):
        o = jnp.dot(kt[g, :DL, :], pt[g, :, col], preferred_element_type=F32) * inv_l
        ot[g] = o.astype(BF)
        dn = (do[g, :, col].astype(F32) * inv_l).astype(BF)
        do[g, :, col] = dn
        centre = jnp.sum(o * dn.astype(F32), axis=0, keepdims=True)
        cen[g, :, col] = jnp.broadcast_to(centre, (8, WIDE))

    scores(sa, 0, 0)

    def fwd(i):
        col = cols(i)
        scores(sb, 1, i)
        values(0, col, softmax(sa, 0, col))
        hook("fwd", i, 0, 2)
        scores(sa, 0, jnp.minimum(i + 1, 3))
        values(1, col, softmax(sb, 1, col))

        @pl.when(i >= 2)
        def _():
            ho_store(i - 2, i % 2).wait()

        for p in range(4):
            hh = halves(ot[0, :, p * 128 : (p + 1) * 128], ot[1, :, p * 128 : (p + 1) * 128])
            for q in range(2):
                h = 2 * p + q
                part = jnp.dot(hh[q], gout[8 * i + h], preferred_element_type=F32).astype(BF)
                u[i, h * DL : (h + 1) * DL] = part
                hb[i % 2, h] = lax.dot_general(hh[q], w[8 * i + h], TND, preferred_element_type=F32).astype(BF)
        ho_store(i, i % 2).start()

    loop("fwd", fwd, 2)
    ho_store(2, 0).wait()
    ho_store(3, 1).wait()

    def back_ds(g, to):
        def body(i):
            for b, tmp in enumerate((sa, sb)):
                col = cols(2 * i + b)
                tmp[...] = jnp.dot(k[g, :, :DL], do[g, :, col], preferred_element_type=F32)
            for b, tmp in enumerate((sa, sb)):
                col = cols(2 * i + b)
                for q in range(8):
                    rows = slice(q * 128, (q + 1) * 128)
                    t = pt[g, rows, col].astype(F32) * (tmp[rows] - cen[g, 0:1, col])
                    pt[to, rows, col] = t.astype(BF)

        return body

    def back_kv(g, d):
        def body(i):
            rows = cols(i)
            sa[:KV] = lax.dot_general(qg[g, :KV, :], pt[d, rows, :], NTD, preferred_element_type=F32)
            hook("kv%d" % g, i, 0, 2)
            sb[:DL] = lax.dot_general(do[g], pt[g, rows, :], NTD, preferred_element_type=F32)
            zero = jnp.zeros((KP - KV, WIDE), F32)
            t = jnp.concatenate([sa[:DL] * SC + sb[:DL], sa[DL:KV] * SC, zero], 0).astype(BF)
            t = jnp.swapaxes(t, 0, 1)
            gk[pl.ds(16 * g + 8 * i, 8)] = t[:, :KV].reshape(8, BLK, KV)

        return body

    loop("ds0", back_ds(0, 2))
    loop("kv0", back_kv(0, 2), 2)
    loop("ds1", back_ds(1, 0))
    loop("kv1", back_kv(1, 0), 2)

    def dq_store(i, slot):
        return pltpu.make_async_copy(qb.at[slot], dq_hbm.at[pl.ds(8 * i, 8)], qsem.at[slot])

    def back_q(i):
        col = cols(i)

        @pl.when(i >= 2)
        def _():
            dq_store(i - 2, i % 2).wait()

        r = []
        for g, d in ((0, 2), (1, 0)):
            r.append((jnp.dot(kt[g], pt[d, :, col], preferred_element_type=F32) * SC).astype(BF))
        for p in range(4):
            a, b = halves(r[0][:, p * 128 : (p + 1) * 128], r[1][:, p * 128 : (p + 1) * 128])
            qb[i % 2, 2 * p] = a
            qb[i % 2, 2 * p + 1] = b
        dq_store(i, i % 2).start()

    loop("dq", back_q)
    for op, arg in late:
        run(op, arg)
    dq_store(2, 0).wait()
    dq_store(3, 1).wait()
    for q in uv_out:
        q.wait()


def attention(lists, cache, qt, w, gout):
    v = pl.BlockSpec(memory_space=pltpu.VMEM)
    m = pl.BlockSpec(memory_space=pltpu.SMEM)
    a = pl.BlockSpec(memory_space=pl.ANY)
    scratch = [
        pltpu.VMEM((2, KP, ROWS), BF),
        pltpu.VMEM((2, KEYS, KP), BF),
        pltpu.VMEM((2, KV, KEYS), BF),
        pltpu.VMEM((BLK, WIDE), F32),
        pltpu.VMEM((3, KEYS, ROWS), BF),
        pltpu.VMEM((2, DL, ROWS), BF),
        pltpu.VMEM((2, 8, ROWS), F32),
        pltpu.VMEM((2, DL, WIDE), BF),
        pltpu.VMEM((KEYS, WIDE), F32),
        pltpu.VMEM((KEYS, WIDE), F32),
        pltpu.VMEM((NCH, CROWS, 128), BF),
        pltpu.VMEM((NH, DL, VH), BF),
        pltpu.VMEM((NH, TD, VH), BF),
        pltpu.VMEM((2, 8, TD, VH), BF),
        pltpu.VMEM((2, 8, KV, TD), BF),
        pltpu.SMEM((2, 32), jnp.int32),
        pltpu.SMEM((32,), jnp.int32),
        pltpu.SemaphoreType.DMA((2,)),
        pltpu.SemaphoreType.DMA((2,)),
        pltpu.SemaphoreType.DMA((2,)),
        pltpu.SemaphoreType.DMA((NCH,)),
    ]
    return pl.pallas_call(
        fused_body,
        out_shape=(
            jax.ShapeDtypeStruct((NH, TD, VH), BF),
            jax.ShapeDtypeStruct((NH, KV, TD), BF),
            jax.ShapeDtypeStruct((NCH, CROWS, 128), BF),
            jax.ShapeDtypeStruct((32, KV), F32),
        ),
        in_specs=[m, v, a, a, a],
        out_specs=(a, a, a, v),
        scratch_shapes=scratch + GATHER_SCRATCH + UV_SCRATCH + CACHE_SCRATCH,
        compiler_params=pltpu.CompilerParams(
            collective_id=0, has_side_effects=True, vmem_limit_bytes=VMEM_LIMIT
        ),
        name="latent_attention",
    )(lists, cache, qt, w, gout)


def hand_on_body(ho, dq, uv, gc, ho_out, dq_out, uv_out, gc_out, vh, vt, vq, vu, vg, si, so):
    def part(ref, i):
        return ref.at[pl.ds(8 * i, 8)]

    gc_in = pltpu.make_async_copy(gc, vg, si.at[3, 0])
    gc_copy = pltpu.make_async_copy(vg, gc_out, so.at[3, 0])
    ins, outs = [], []
    for i in range(4):
        ins.append(pltpu.make_async_copy(part(ho, i), part(vh, i), si.at[0, i]))
    for i in range(4):
        ins.append(pltpu.make_async_copy(part(dq, i), part(vq, i), si.at[1, i]))
        outs.append(pltpu.make_async_copy(part(vq, i), part(dq_out, i), so.at[1, i]))
        ins.append(pltpu.make_async_copy(part(uv, i), part(vu, i), si.at[2, i]))
        outs.append(pltpu.make_async_copy(part(vu, i), part(uv_out, i), so.at[2, i]))
    gc_in.start()
    for q in ins:
        q.start()
    gc_in.wait()
    gc_copy.start()
    for q in ins[:4]:
        q.wait()
    turns = []
    for i in range(4):
        for q, out in zip(ins[4 + 2 * i : 6 + 2 * i], outs[2 * i : 2 * i + 2]):
            q.wait()
            out.start()
        t = pl.ds(32 * i, 32)
        vt[t] = jnp.swapaxes(vh[:, t, :], 0, 1)
        turns.append(pltpu.make_async_copy(vt.at[t], ho_out.at[t], so.at[0, i]))
        turns[-1].start()
    for q in outs + turns:
        q.wait()
    gc_copy.wait()


def hand_on(ho, dq, uv, gc):
    a = pl.BlockSpec(memory_space=pl.ANY)
    return pl.pallas_call(
        hand_on_body,
        out_shape=(
            jax.ShapeDtypeStruct((TD, NH, VH), BF),
            jax.ShapeDtypeStruct((NH, KV, TD), BF),
            jax.ShapeDtypeStruct((NH, DL, VH), BF),
            jax.ShapeDtypeStruct((32, KV), F32),
        ),
        in_specs=[a] * 4,
        out_specs=(a,) * 4,
        scratch_shapes=[
            pltpu.VMEM((NH, TD, VH), BF),
            pltpu.VMEM((TD, NH, VH), BF),
            pltpu.VMEM((NH, KV, TD), BF),
            pltpu.VMEM((NH, DL, VH), BF),
            pltpu.VMEM((32, KV), F32),
            pltpu.SemaphoreType.DMA((4, 4)),
            pltpu.SemaphoreType.DMA((4, 4)),
        ],
        compiler_params=pltpu.CompilerParams(vmem_limit_bytes=VMEM_LIMIT),
        name="hand_on",
    )(ho, dq, uv, gc)


def on_device(queries, cache, lists, w_uv, grad_out):
    ho, dq, uv, gc = attention(
        lists, cache, queries.transpose(1, 2, 0), w_uv, grad_out.reshape(TD * NH, VH)
    )
    ho, dq, uv, gc = hand_on(ho, dq, uv.reshape(NH, DL, VH), gc)
    return ho, dq.transpose(2, 0, 1), gc, uv


def solution(mesh):
    return jax.shard_map(
        on_device,
        mesh=mesh,
        in_specs=(
            P("seq", "head", None),
            P(("seq", "head"), None),
            P("seq", None),
            P("head", None, None),
            P("seq", "head", None),
        ),
        out_specs=(
            P("seq", "head", None),
            P("seq", "head", None),
            P(("seq", "head"), None),
            P("head", None, None),
        ),
        check_vma=False,
    )
```
